32 devices in a mesh: seq: 8 (over z, y), batch: 4 (over x, core).
Axes of the slice: x: 2, y: 2, z: 4, core: 2. Of those that a mesh axis runs over, the one named last changes fastest.
Arguments:
- tokens: bfloat16 [4, 1024, 2048], P('batch', 'seq'), may hold values from -6 to 6
- out_grad: bfloat16 [4, 1024, 2048], P('batch', 'seq'), may hold values from -6 to 6
- doc_lengths: int32 [4, 8], P('batch'), may hold values from 1 to 960, 1024 in all within a row
- qkv_weight: float32 [2048, 6144], P(('seq', 'batch')), may hold values from -0.125 to 0.125
- qkv_first: float32 [2048, 6144], P(('seq', 'batch')), may hold values from -40 to 40
- qkv_second: float32 [2048, 6144], P(('seq', 'batch')), may hold values from 106.496 to 1720.32
- out_weight: float32 [2048, 2048], P(('seq', 'batch')), may hold values from -1.75 to 1.75
- out_first: float32 [2048, 2048], P(('seq', 'batch')), may hold values from -6 to 6
- out_second: float32 [2048, 2048], P(('seq', 'batch')), may hold values from 0.6 to 9.6
- gate_up_weight: float32 [2048, 16384], P(('seq', 'batch')), may hold values from -0.125 to 0.125
- gate_up_first: float32 [2048, 16384], P(('seq', 'batch')), may hold values from -6 to 6
- gate_up_second: float32 [2048, 16384], P(('seq', 'batch')), may hold values from 9.4208 to 155.648
- down_weight: float32 [2048, 8192], P(('seq', 'batch')), may hold values from -0.0625 to 0.0625
- down_first: float32 [2048, 8192], P(('seq', 'batch')), may hold values from -24 to 24
- down_second: float32 [2048, 8192], P(('seq', 'batch')), may hold values from 38.5024 to 614.4
- gains: float32 [2, 2048], replicated, may hold values from 0.5 to 1.5
- gain_first: float32 [2, 2048], replicated, may hold values from -48 to 48
- gain_second: float32 [2, 2048], replicated, may hold values from 151.552 to 2457.6
Outputs:
- block_out: bfloat16 [4, 1024, 2048], P('batch', 'seq')
- input_grad: float32 [4, 1024, 2048], P('batch', 'seq')
- qkv_first_new: float32 [2048, 6144], P(('seq', 'batch'))
- qkv_second_new: float32 [2048, 6144], P(('seq', 'batch'))
- qkv_new: float32 [2048, 6144], P(('seq', 'batch'))
- out_first_new: float32 [2048, 2048], P(('seq', 'batch'))
- out_second_new: float32 [2048, 2048], P(('seq', 'batch'))
- out_new: float32 [2048, 2048], P(('seq', 'batch'))
- gate_up_first_new: float32 [2048, 16384], P(('seq', 'batch'))
- gate_up_second_new: float32 [2048, 16384], P(('seq', 'batch'))
- gate_up_new: float32 [2048, 16384], P(('seq', 'batch'))
- down_first_new: float32 [2048, 8192], P(('seq', 'batch'))
- down_second_new: float32 [2048, 8192], P(('seq', 'batch'))
- down_new: float32 [2048, 8192], P(('seq', 'batch'))
- gain_first_new: float32 [2, 2048], replicated
- gain_second_new: float32 [2, 2048], replicated
- gain_new: float32 [2, 2048], replicated
The draws below stay inside these ranges and needn't reach their ends.
Inputs may be any that keep to these rules, and one draw needn't show every extreme that they name: `doc_lengths`: each row gives the lengths of the 8 documents of one sequence in order, summing to 1024; one of them has exactly 960 positions.
All inputs are finite; a program needn't handle non-finite values.
Results may differ from the reference program's by a relative error of at most 0.015.
Values may be sent and summed in bfloat16 or wider, within the bound.
No kernel may reach another device: no remote copies, remote signals or barrier semaphores. Data moves between devices by JAX's collectives and lax.ppermute only.
A program may use at most 704 MiB of HBM per device.

```python
import math
import jax
import jax.numpy as jnp
import numpy as np
from jax import lax

D = 2048
HD = 64
FF = 8192
TOK_DEV = 128
NDOC = 8
STEP = 10
SEQS = 4
LENGTH = 1024


def shard_levels(key, dims, pieces, smallest, top_value):
    def one(position, shards_of):
        draws = jax.random.uniform(jax.random.fold_in(jax.random.fold_in(key, 6), position), (shards_of,), jnp.float32, smallest / len(pieces), top_value / len(pieces))
        return jnp.repeat(jnp.exp(draws), dims[position] // shards_of).reshape((-1,) + (1,) * (len(dims) - position - 1))

    gain = one(*pieces[0])
    for cut in pieces[1:]:
        gain = gain * one(*cut)
    return gain


def length_profile(count, total, reach, lean):
    weights = [(1 << 20) // math.isqrt(standing ** lean) + 1 for standing in range(2, count + 1)]
    surplus, counts = total - reach - (count - 1), [1] * (count - 1)
    while surplus > 0:
        free = [i for i in range(count - 1) if counts[i] < reach]
        pool, budget = sum([weights[i] for i in free]), surplus
        for i in free:
            more = min(reach - counts[i], max(1, budget * weights[i] // pool), surplus)
            counts[i] = counts[i] + more
            surplus = surplus - more
    return np.array([reach] + counts)


def ragged_sizes(stream_key, amount, total, most, skew):
    if amount == 2:
        one = jax.random.randint(stream_key, (), max(1, total - most), min(most, total - 1) + 1)
        return jnp.stack([one, total - one])
    sizes = jnp.asarray(length_profile(amount, total, most, skew), jnp.int32)
    couples = (amount - 1) // 2
    donor, sink = sizes[1:1 + 2 * couples:2], sizes[2:2 + 2 * couples:2]
    slack = jnp.minimum(donor - 1, most - sink)
    shifted = jax.random.randint(jax.random.fold_in(stream_key, 1), (couples,), 0, 1 << 20) % (slack + 1)
    sizes = sizes.at[1:1 + 2 * couples:2].set(donor - shifted).at[2:2 + 2 * couples:2].set(sink + shifted)
    return sizes[jax.random.permutation(jax.random.fold_in(stream_key, 2), amount)]


def bell_draw(key, shape, width, most, cuts=(), kind=jnp.bfloat16):
    entries = jax.random.normal(key, shape, jnp.float32) * width
    if len(cuts) > 0:
        entries = shard_levels(key, shape, cuts, -0.22, 0.18) * entries
    return jnp.clip(entries, min=-most, max=most).astype(kind)


def setup_inputs(seed: int = 0) -> dict:
    splits = jax.random.split(jax.random.key(seed), 19)
    tokens = bell_draw(splits[0], (SEQS, LENGTH, D), 1.0, 6.0, ((0, 4), (1, 8)))
    out_grad = bell_draw(splits[1], (SEQS, LENGTH, D), 1.0, 6.0, ((0, 4), (1, 8)))
    doc_lengths = jax.vmap(lambda own: ragged_sizes(own, NDOC, LENGTH, LENGTH - TOK_DEV // 2, 2))(jax.random.split(splits[2], SEQS)).reshape((SEQS, NDOC)).astype(jnp.int32)
    qkv_weight = bell_draw(splits[3], (D, 3 * D), D ** -0.5, 0.125, ((0, 32),), jnp.float32)
    qkv_first = bell_draw(splits[4], (D, 3 * D), (0.11 * (SEQS * LENGTH) ** 0.5), 40.0, ((0, 32),), jnp.float32)
    qkv_second = jnp.clip(jnp.exp(math.log(1720.32) - 2.7821581 * jax.random.uniform(splits[5], (D, 3 * D), jnp.float32) ** shard_levels(splits[5], (D, 3 * D), ((0, 32),), -0.2, 0.2)), 106.496, 1720.32)
    out_weight = bell_draw(splits[6], (D, D), (max(1, D * 6 // LENGTH)) ** -0.5, 1.75, ((0, 32),), jnp.float32)
    out_first = bell_draw(splits[7], (D, D), (0.26 * SEQS ** 0.5), 6.0, ((0, 32),), jnp.float32)
    out_second = jnp.clip(jnp.exp(math.log(9.6) - 2.7725887 * jax.random.uniform(splits[8], (D, D), jnp.float32) ** shard_levels(splits[8], (D, D), ((0, 32),), -0.2, 0.2)), 0.6, 9.6)
    gate_up_weight = bell_draw(splits[9], (D, 2 * FF), D ** -0.5, 0.125, ((0, 32),), jnp.float32)
    gate_up_first = bell_draw(splits[10], (D, 2 * FF), (0.033 * (SEQS * LENGTH) ** 0.5), 6.0, ((0, 32),), jnp.float32)
    gate_up_second = jnp.clip(jnp.exp(math.log(155.648) - 2.804677 * jax.random.uniform(splits[11], (D, 2 * FF), jnp.float32) ** shard_levels(splits[11], (D, 2 * FF), ((0, 32),), -0.2, 0.2)), 9.4208, 155.648)
    down_weight = bell_draw(splits[12], (D, FF), FF ** -0.5, 0.0625, ((0, 32),), jnp.float32)
    down_first = bell_draw(splits[13], (D, FF), (0.067 * (SEQS * LENGTH) ** 0.5), 24.0, ((0, 32),), jnp.float32)
    down_second = jnp.clip(jnp.exp(math.log(614.4) - 2.7699257 * jax.random.uniform(splits[14], (D, FF), jnp.float32) ** shard_levels(splits[14], (D, FF), ((0, 32),), -0.2, 0.2)), 38.5024, 614.4)
    gains = jnp.clip(1.0 + 0.1 * jax.random.normal(splits[15], (2, D), jnp.float32), 0.5, 1.5)
    gain_first = bell_draw(splits[16], (2, D), (0.13 * (SEQS * LENGTH) ** 0.5), 48.0, (), jnp.float32)
    gain_second = jnp.clip(jnp.exp(jax.random.uniform(splits[17], (2, D), jnp.float32, math.log(151.552), math.log(2457.6))), 151.552, 2457.6)
    return {"tokens": tokens, "out_grad": out_grad, "doc_lengths": doc_lengths, "qkv_weight": qkv_weight, "qkv_first": qkv_first, "qkv_second": qkv_second, "out_weight": out_weight, "out_first": out_first, "out_second": out_second, "gate_up_weight": gate_up_weight, "gate_up_first": gate_up_first, "gate_up_second": gate_up_second, "down_weight": down_weight, "down_first": down_first, "down_second": down_second, "gains": gains, "gain_first": gain_first, "gain_second": gain_second}


@jax.custom_vjp
def low(v):
    return lax.optimization_barrier(v.astype(jnp.bfloat16)).astype(jnp.float32)

@jax.custom_vjp
def low_back(v):
    return v

def low_keep(v):
    return (low(v), None)

def low_pass(kept, grad):
    return (grad,)

def back_keep(v):
    return (v, None)

def back_low(kept, grad):
    return (low(grad),)
low.defvjp(low_keep, low_pass)
low_back.defvjp(back_keep, back_low)
norm_eps = 1e-05
rope_base = 130000.0
beta_one = 0.9
beta_two = 0.95
adam_eps = 1e-08
weight_decay = 0.1
masked_score = -1e+30
rate_qkv = 0.05
rate_out = 0.5
rate_gate = 0.05
rate_down = 0.03
rate_gain = 0.3

def dot_high(left_side, right_side):
    return jnp.dot(left_side, right_side, precision=lax.Precision.HIGHEST, preferred_element_type=jnp.float32)

def rms_norm(values, gain_row):
    scale_rows = lax.rsqrt(lax.optimization_barrier(jnp.mean(values * values, axis=-1, keepdims=True)) + norm_eps)
    return values * scale_rows * gain_row

def rotate_half(values):
    middle = values.shape[-1] // 2
    return jnp.concatenate([-values[..., middle:], values[..., :middle]], axis=-1)

def rope_tables(positions):
    inverse = rope_base ** (-jnp.arange(0, HD, 2, dtype=jnp.float32) / HD)
    angles = positions.astype(jnp.float32)[:, None] * inverse[None, :]
    angles = jnp.concatenate([angles, angles], axis=1)
    return (jnp.cos(angles)[:, None, :], jnp.sin(angles)[:, None, :])

def apply_rope(values, cos_table, sin_table):
    return values * cos_table + rotate_half(values) * sin_table

def doc_numbers(lengths, positions):
    ends_running = jnp.cumsum(lengths)
    return lax.optimization_barrier(jnp.sum((positions[:, None] >= ends_running[None, :]).astype(jnp.int32), axis=1))

def forward(inputs, gain_rows, weight_qkv, weight_out, weight_gate, weight_down, documents, positions, cos_table, sin_table):
    length = inputs.shape[0]
    model_width = inputs.shape[1]
    head_count = model_width // HD
    hidden_width = weight_gate.shape[1] // 2
    score_scale = HD ** (-0.5)
    act_one = low(rms_norm(inputs, gain_rows[0]))
    qkv = low_back(dot_high(act_one, low(weight_qkv)))
    query = low(apply_rope(qkv[:, :model_width].reshape(length, head_count, HD), cos_table, sin_table))
    keys_all = low(apply_rope(qkv[:, model_width:2 * model_width].reshape(length, head_count, HD), cos_table, sin_table))
    values_all = low(qkv[:, 2 * model_width:].reshape(length, head_count, HD))
    block_rows = math.gcd(length, 512)
    block_count = length // block_rows

    def attend(query_block, position_block, doc_block):
        scores = jnp.einsum('qhd,khd->hqk', query_block, keys_all, precision=lax.Precision.HIGHEST) * score_scale
        scores = low_back(scores)
        allowed = (positions[None, :] <= position_block[:, None]) & (documents[None, :] == doc_block[:, None])
        scores = jnp.where(allowed[None], scores, masked_score)
        probs = jax.nn.softmax(scores, axis=-1)
        return jnp.einsum('hqk,khd->qhd', low(probs), values_all, precision=lax.Precision.HIGHEST)
    checked = jax.checkpoint(attend)
    attended = lax.map(lambda block_item: checked(block_item[0], block_item[1], block_item[2]), (query.reshape(block_count, block_rows, head_count, HD), positions.reshape(block_count, block_rows), documents.reshape(block_count, block_rows)))
    attn_rows = low(low_back(attended.reshape(length, model_width)))
    middle = inputs + low_back(dot_high(attn_rows, low(weight_out)))
    act_two = low(rms_norm(middle, gain_rows[1]))
    gate_up = low_back(dot_high(act_two, low(weight_gate)))
    hidden_rows = low(jax.nn.silu(gate_up[:, :hidden_width]) * gate_up[:, hidden_width:])
    return middle + low_back(dot_high(hidden_rows, low(weight_down).T))

def adam_update(weight, first_moment, second, gradient, step_rate):
    first_new = beta_one * first_moment + (1.0 - beta_one) * gradient
    second_new = beta_two * second + (1.0 - beta_two) * gradient * gradient
    first_hat = first_new / (1.0 - beta_one ** STEP)
    second_hat = second_new / (1.0 - beta_two ** STEP)
    weight_new = weight - step_rate * (first_hat / (jnp.sqrt(second_hat) + adam_eps) + weight_decay * weight)
    return (first_new, second_new, weight_new)

def reference(tokens, out_grad, doc_lengths, qkv_weight, qkv_first, qkv_second, out_weight, out_first, out_second, gate_up_weight, gate_up_first, gate_up_second, down_weight, down_first, down_second, gains, gain_first, gain_second):
    positions = jnp.arange(LENGTH, dtype=jnp.int32)
    cos_table, sin_table = rope_tables(positions)

    def one_sequence(totals, sequence_item):
        inputs, cotangent, lengths = sequence_item
        documents = doc_numbers(lengths, positions)

        def block_layer(values, gain_rows, weight_qkv, weight_out, weight_gate, weight_down):
            return forward(values, gain_rows, weight_qkv, weight_out, weight_gate, weight_down, documents, positions, cos_table, sin_table)
        result, pullback = jax.vjp(block_layer, inputs.astype(jnp.float32), gains, qkv_weight, out_weight, gate_up_weight, down_weight)
        gradients = pullback(cotangent.astype(jnp.float32))
        totals = tuple((running + increment for running, increment in zip(totals, gradients[1:])))
        return (totals, (result.astype(jnp.bfloat16), gradients[0]))
    initial = (jnp.zeros_like(gains), jnp.zeros_like(qkv_weight), jnp.zeros_like(out_weight), jnp.zeros_like(gate_up_weight), jnp.zeros_like(down_weight))
    totals, outputs = lax.scan(one_sequence, initial, (tokens, out_grad, doc_lengths))
    block_out, input_grad = outputs
    gain_grad, qkv_grad, out_grad_weight, gate_grad, down_grad = totals
    qkv_m, qkv_s, qkv_w = adam_update(qkv_weight, qkv_first, qkv_second, qkv_grad, rate_qkv)
    out_m, out_s, out_w = adam_update(out_weight, out_first, out_second, out_grad_weight, rate_out)
    gate_m, gate_s, gate_w = adam_update(gate_up_weight, gate_up_first, gate_up_second, gate_grad, rate_gate)
    down_m, down_s, down_w = adam_update(down_weight, down_first, down_second, down_grad, rate_down)
    gain_m, gain_s, gain_w = adam_update(gains, gain_first, gain_second, gain_grad, rate_gain)
    return (block_out, input_grad, qkv_m, qkv_s, qkv_w, out_m, out_s, out_w, gate_m, gate_s, gate_w, down_m, down_s, down_w, gain_m, gain_s, gain_w)
```

```python
import jax
import jax.numpy as jnp
from jax import lax
from jax.experimental import pallas as pl
from jax.experimental.pallas import tpu as pltpu
from jax.sharding import PartitionSpec as P

HD = 64
STEP = 10
LANES = 128
QUERY_ROWS = 256


norm_eps = 1e-05
rope_base = 130000.0
beta_one = 0.9
beta_two = 0.95
adam_eps = 1e-08
weight_decay = 0.1
masked_score = -1e30
rate_qkv = 0.05
rate_out = 0.5
rate_gate = 0.05
rate_down = 0.03
rate_gain = 0.3


def rotate_half(values):
    middle = values.shape[-1] // 2
    return jnp.concatenate([-values[..., middle:], values[..., :middle]], axis=-1)


def rope_tables(positions):
    inverse = rope_base ** (-jnp.arange(0, HD, 2, dtype=jnp.float32) / HD)
    angles = positions.astype(jnp.float32)[:, None] * inverse[None, :]
    angles = jnp.concatenate([angles, angles], axis=1)
    return (jnp.cos(angles), jnp.sin(angles))


def apply_rope(values, cos_table, sin_table):
    return values * cos_table + rotate_half(values) * sin_table


def undo_rope(values, cos_table, sin_table):
    return values * cos_table - rotate_half(values) * sin_table


def unit_rows(values):
    scale_rows = lax.rsqrt(jnp.mean(values * values, axis=-1, keepdims=True) + norm_eps)
    return (values * scale_rows, scale_rows)


def norm_back(grad_normed, unit_values, scale_rows, gain_row):
    grad_unit = grad_normed * gain_row
    gain_part = jnp.sum(grad_normed * unit_values, axis=0)
    grad_values = scale_rows * (
        grad_unit - unit_values * jnp.mean(grad_unit * unit_values, axis=-1, keepdims=True)
    )
    return (grad_values, gain_part)


def contract_rows(left_side, right_side):
    return lax.dot_general(
        left_side, right_side, (((0,), (0,)), ((), ())), preferred_element_type=jnp.float32
    )


def contract_cols(left_side, right_side):
    return lax.dot_general(
        left_side, right_side, (((1,), (1,)), ((), ())), preferred_element_type=jnp.float32
    )


def matmul(left_side, right_side):
    return jnp.dot(left_side, right_side, preferred_element_type=jnp.float32)


def adam_update(weight, first_moment, second, gradient, step_rate):
    first_new = beta_one * first_moment + (1.0 - beta_one) * gradient
    second_new = beta_two * second + (1.0 - beta_two) * gradient * gradient
    first_hat = first_new / (1.0 - beta_one**STEP)
    second_hat = second_new / (1.0 - beta_two**STEP)
    weight_new = weight - step_rate * (
        first_hat / (jnp.sqrt(second_hat) + adam_eps) + weight_decay * weight
    )
    return (first_new, second_new, weight_new)


def swapped(value, axis, bit):
    count = lax.axis_size(axis)
    return lax.ppermute(value, axis, [(source, source ^ bit) for source in range(count)])


def ring_order(count):
    return list(range(0, count, 2)) + list(range(count - 1, 0, -2))


def ring_shift(value, steps):
    count = lax.axis_size("seq")
    order = ring_order(count)
    pairs = [(order[i], order[(i + steps) % count]) for i in range(count)]
    return lax.ppermute(value, "seq", pairs)


def ring_place(offset):
    count = lax.axis_size("seq")
    order = ring_order(count)
    table = jnp.array([order[(order.index(own) + offset) % count] for own in range(count)], jnp.int32)
    return table[lax.axis_index("seq")]


def ring_gather(parts, fillers=()):
    count = lax.axis_size("seq")
    far = count // 2
    packed = jnp.concatenate(parts, axis=1) if len(parts) > 1 else parts[0]
    middle = packed.shape[1] // 2
    blocks = {0: packed}
    ahead = behind = packed
    for step in range(1, far):
        if 0 <= step - 2 < len(fillers):
            ahead, behind = after_all((ahead, behind), fillers[step - 2])
        ahead, behind = ring_shift(ahead, 1), ring_shift(behind, -1)
        blocks[-step], blocks[step] = ahead, behind
    if far - 2 < len(fillers):
        ahead, behind = after_all((ahead, behind), fillers[far - 2])
    left, right = ring_shift(ahead[:, :middle], 1), ring_shift(behind[:, middle:], -1)
    blocks[far] = jnp.concatenate([left, right], axis=1)
    gathered = []
    first = 0
    for part in parts:
        last = first + part.shape[1]
        gathered.append({offset: block[:, first:last] for offset, block in blocks.items()})
        first = last
    return gathered


def with_rows(block, rows):
    if block.shape[0] >= rows:
        return jnp.concatenate(jnp.split(block, block.shape[0] // rows, axis=0), axis=1)
    return jnp.concatenate(jnp.split(block, rows // block.shape[0], axis=1), axis=0)


def stacked_rows(blocks):
    rows, width = blocks[0].shape
    whole = jnp.zeros((len(blocks) * rows, width), blocks[0].dtype)
    for offset, block in blocks.items():
        whole = lax.dynamic_update_slice(whole, block, (ring_place(offset) * rows, 0))
    return whole


def stacked_columns(blocks):
    rows, width = blocks[0].shape
    whole = jnp.zeros((rows, len(blocks) * width), blocks[0].dtype)
    for offset, block in blocks.items():
        whole = lax.dynamic_update_slice(whole, block, (0, ring_place(offset) * width))
    return whole


def ring_rows(whole, offsets):
    rows = whole.shape[0] // lax.axis_size("seq")
    return jnp.concatenate(
        [lax.dynamic_slice_in_dim(whole, ring_place(o) * rows, rows, 0) for o in offsets], axis=0
    )


def added(block, got):
    return (block.astype(jnp.float32) + got.astype(jnp.float32)).astype(block.dtype)


def ring_scatter_sum(parts, fillers=()):
    far = lax.axis_size("seq") // 2
    first, second = parts
    ahead, behind = (ring_shift(first[far], 1),), (ring_shift(second[far], -1),)
    for turn, step in enumerate(range(far - 1, 0, -1)):
        onward = [first[step], second[step]]
        backward = [first[-step], second[-step]]
        if turn == 0:
            onward[0] = added(onward[0], ahead[0])
            backward[1] = added(backward[1], behind[0])
        else:
            onward = [added(block, got) for block, got in zip(onward, ahead)]
            backward = [added(block, got) for block, got in zip(backward, behind)]
        if turn < len(fillers):
            moved = after_all(onward + backward, fillers[turn])
            onward, backward = moved[:2], moved[2:]
        ahead = [ring_shift(block, 1) for block in onward]
        behind = [ring_shift(block, -1) for block in backward]
    return [
        own.astype(jnp.float32) + left.astype(jnp.float32) + right.astype(jnp.float32)
        for own, left, right in zip((first[0], second[0]), ahead, behind)
    ]


def ring_scatter_one(whole, fillers=()):
    far = lax.axis_size("seq") // 2
    middle = whole.shape[1] // 2
    offsets = [0] + [sign * step for step in range(1, far) for sign in (1, -1)] + [far]
    blocks = {offset: ring_rows(whole, [offset]) for offset in offsets}
    halves = ring_scatter_sum(
        (
            {offset: block[:, :middle] for offset, block in blocks.items()},
            {offset: block[:, middle:] for offset, block in blocks.items()},
        ),
        fillers,
    )
    return jnp.concatenate(halves, axis=1)


def sum_everywhere(values):
    total = lax.axis_size("seq") * lax.axis_size("batch")
    copies = jnp.broadcast_to(values[None], (total,) + values.shape)
    return jnp.sum(lax.all_to_all(copies, ("seq", "batch"), 0, 0, tiled=True), axis=0)


def after(value, *others):
    return lax.optimization_barrier((value,) + others)[0]


def after_all(values, others):
    return lax.optimization_barrier(tuple(values) + tuple(others))[: len(values)]


def batch_bits():
    count = lax.axis_size("batch")
    bits = []
    while (1 << len(bits)) < count:
        bits.append(1 << len(bits))
    return bits


def of_offset(choices, offset):
    index = lax.axis_index("batch")
    picked = choices[offset]
    for own in range(1, len(choices)):
        picked = jnp.where(index == own, choices[own ^ offset], picked)
    return picked


def offset_order():
    order = [0]
    for bit in reversed(batch_bits()):
        order = order + [offset ^ bit for offset in order]
    return order


def batch_columns(rows, rows_own):
    count, width = rows.shape
    batch_total = lax.axis_size("batch")
    blocks = rows.reshape(count, -1, batch_total, rows_own)
    return [blocks[:, :, b].reshape(count, width // batch_total) for b in range(batch_total)]


def to_relative(rows, rows_own):
    columns = batch_columns(rows, rows_own)
    return jnp.concatenate([of_offset(columns, m) for m in offset_order()], axis=1)


def from_relative(rows, rows_own):
    count, width = rows.shape
    batch_total = lax.axis_size("batch")
    order = offset_order()
    part = width // batch_total
    columns = [
        rows[:, order.index(m) * part : (order.index(m) + 1) * part] for m in range(batch_total)
    ]
    blocks = [
        of_offset(columns, b).reshape(count, width // (batch_total * rows_own), rows_own)
        for b in range(batch_total)
    ]
    return jnp.stack(blocks, axis=2).reshape(count, width)


def gather_pieces(block):
    pieces = [block]
    for bit in reversed(batch_bits()):
        pieces = pieces + [swapped(piece, "batch", bit) for piece in pieces]
    return pieces


def gather_batch(block):
    return jnp.concatenate(gather_pieces(block), axis=0)


def partial_sum_batch(left, right):
    width = left.shape[1]
    held = None
    sends = []

    def product(first, last):
        part = contract_rows(left[:, first:last], right)
        return part if held is None else part + held[first:last]

    for bit in batch_bits():
        half = width // 2
        sends.append(product(half, width).astype(jnp.bfloat16))
        got = swapped(sends[-1], "batch", bit).astype(jnp.float32)
        held = got if held is None else held[:half] + got
        width = half
    return (product(0, width).astype(jnp.bfloat16), sends)


def scatter_sum_batch(blocks):
    held = blocks
    for bit in batch_bits():
        pairs = held.reshape((held.shape[0] // 2, 2) + held.shape[1:])
        got = swapped(pairs[:, 1], "batch", bit)
        held = (pairs[:, 0].astype(jnp.float32) + got.astype(jnp.float32)).astype(jnp.bfloat16)
    return held[0]


def seqs_in_block(columns, seq_total):
    return max(1, min(seq_total, 1024 // columns))


def rounded_by_owner(weight, groups):
    rows_own, width = weight.shape
    seq_total = lax.axis_size("seq")
    columns = width // (groups * seq_total)
    if columns % LANES:
        blocks = weight.astype(jnp.bfloat16).reshape(rows_own, groups, seq_total, columns)
        return jnp.transpose(blocks, (2, 0, 1, 3)).reshape(seq_total, rows_own, groups * columns)
    taken = seqs_in_block(columns, seq_total)
    steps = seq_total // taken

    def kernel(weight_ref, out_ref):
        for place in range(taken):
            out_ref[place] = weight_ref[:, place * columns : (place + 1) * columns].astype(
                jnp.bfloat16
            )

    return pl.pallas_call(
        kernel,
        grid=(groups, steps),
        in_specs=[pl.BlockSpec((rows_own, taken * columns), lambda g, j: (0, g * steps + j))],
        out_specs=pl.BlockSpec((taken, rows_own, columns), lambda g, j: (j, 0, g)),
        out_shape=jax.ShapeDtypeStruct(
            (seq_total, rows_own, groups * columns), jnp.bfloat16
        ),
        cost_estimate=pl.CostEstimate(flops=0, bytes_accessed=weight.size * 6, transcendentals=0),
    )(weight)


def to_column_owners(blocks):
    got = lax.all_to_all(blocks, "seq", 0, 0, tiled=True)
    return got.reshape(-1, blocks.shape[2])


def to_row_owners(grad):
    seq_total = lax.axis_size("seq")
    blocks = grad.reshape(seq_total, grad.shape[0] // seq_total, grad.shape[1])
    return lax.all_to_all(blocks, "seq", 0, 0, tiled=True)


def adam_by_owner(weight, first_moment, second, gradient, groups, step_rate, skipped=0):
    rows_own, width = weight.shape
    seq_total = lax.axis_size("seq")
    columns = width // (groups * seq_total)
    if columns % LANES:
        own = gradient[:, :, skipped * columns : (skipped + groups) * columns]
        natural = jnp.transpose(
            own.reshape(seq_total, rows_own, groups, columns), (1, 2, 0, 3)
        ).reshape(rows_own, width)
        return adam_update(weight, first_moment, second, natural.astype(jnp.float32), step_rate)
    taken = seqs_in_block(columns, seq_total)
    steps = seq_total // taken

    def kernel(weight_ref, first_ref, second_ref, gradient_ref, *out_refs):
        for place in range(taken):
            here = slice(place * columns, (place + 1) * columns)
            results = adam_update(
                weight_ref[:, here],
                first_ref[:, here],
                second_ref[:, here],
                gradient_ref[place].astype(jnp.float32),
                step_rate,
            )
            for out_ref, result in zip(out_refs, results):
                out_ref[:, here] = result

    whole = pl.BlockSpec((rows_own, taken * columns), lambda g, j: (0, g * steps + j))
    return pl.pallas_call(
        kernel,
        grid=(groups, steps),
        in_specs=[whole] * 3 + [
            pl.BlockSpec((taken, rows_own, columns), lambda g, j: (j, 0, g + skipped))
        ],
        out_specs=[whole] * 3,
        out_shape=[jax.ShapeDtypeStruct(weight.shape, jnp.float32)] * 3,
        cost_estimate=pl.CostEstimate(
            flops=weight.size * 15, bytes_accessed=weight.size * 26, transcendentals=weight.size
        ),
    )(weight, first_moment, second, gradient)


def swap_halves(values):
    lane = lax.broadcasted_iota(jnp.int32, values.shape, 1)
    return jnp.where(
        lane % HD < HD // 2,
        pltpu.roll(values, LANES - HD // 2, 1),
        pltpu.roll(values, HD // 2, 1),
    )


def of_head(values, head, axis=1):
    lane = lax.broadcasted_iota(jnp.int32, values.shape, axis)
    return jnp.where(lane // HD == head, values, jnp.zeros_like(values))


def allowed_here(starts_ref, first, rows):
    shape = (rows, QUERY_ROWS)
    key = lax.broadcasted_iota(jnp.int32, shape, 0)
    query = lax.broadcasted_iota(jnp.int32, shape, 1) + first
    return (key <= query) & (key >= starts_ref[:, first : first + QUERY_ROWS])


def mm_last(left, right):
    return lax.dot_general(
        left, right, (((1,), (1,)), ((), ())), preferred_element_type=jnp.float32
    )


def attend_kernel(
    query_in, key_in, value_in, cos_ref, sin_ref, starts_ref,
    out_ref, low_ref, query_ref, key_ref, value_ref, total_ref, key_own, value_turned,
):
    length = query_in.shape[0]
    cos, sin = cos_ref[...], sin_ref[...]
    raw_query, raw_key = query_in[...], key_in[...]
    query_ref[...] = (raw_query * cos + swap_halves(raw_query) * sin).astype(jnp.bfloat16) * HD**-0.5
    key_ref[...] = (raw_key * cos + swap_halves(raw_key) * sin).astype(jnp.bfloat16)
    value_ref[...] = value_in[...].astype(jnp.bfloat16)
    turned = value_in[...].T
    for head in range(2):
        key_own[head] = of_head(key_ref[...], head)
        value_turned[head] = of_head(turned, head, 0).astype(jnp.bfloat16)
    for first in range(0, length, QUERY_ROWS):
        last = first + QUERY_ROWS
        allowed = allowed_here(starts_ref, first, last)
        weighted = jnp.zeros((LANES, QUERY_ROWS), jnp.float32)
        for head in range(2):
            scores = mm_last(key_own[head, :last], query_ref[first:last])
            scores = jnp.where(allowed, scores, masked_score)
            top = jnp.max(scores, axis=0, keepdims=True)
            powers = jnp.exp(scores - top)
            total = jnp.sum(powers, axis=0, keepdims=True)
            probs = (powers * (1.0 / total)).astype(jnp.bfloat16)
            weighted += matmul(value_turned[head, :, :last], probs)
            total_ref[0, head : head + 1, first:last] = top + jnp.log(total)
        attended = weighted.T
        out_ref[first:last] = attended
        low_ref[first:last] = attended.astype(jnp.bfloat16)


def attend_back_kernel(
    query_ref, key_ref, value_ref, grad_ref, attended_ref, total_ref, cos_ref, sin_ref, starts_ref,
    out_ref, key_own, value_own, key_turned, key_grad, value_grad,
):
    length = query_ref.shape[0]
    pair = pl.program_id(0)
    width = out_ref.shape[1] // 3
    turned = key_ref[...].astype(jnp.float32).T
    for head in range(2):
        key_own[head] = of_head(key_ref[...], head)
        value_own[head] = of_head(value_ref[...], head)
        key_turned[head] = of_head(turned, head, 0).astype(jnp.bfloat16)
    key_grad[...] = jnp.zeros_like(key_grad)
    value_grad[...] = jnp.zeros_like(value_grad)

    def undone(values, rows):
        back = values * cos_ref[rows] - swap_halves(values) * sin_ref[rows]
        return back.astype(jnp.bfloat16)

    def lanes(group):
        return pl.ds(pl.multiple_of(group * width + pair * LANES, LANES), LANES)

    for first in range(0, length, QUERY_ROWS):
        last = first + QUERY_ROWS
        rows = slice(first, last)
        allowed = allowed_here(starts_ref, first, last)
        grad, query = grad_ref[rows], query_ref[rows]
        products = (grad.astype(jnp.float32) * attended_ref[rows]).T
        query_grad = jnp.zeros((LANES, QUERY_ROWS), jnp.float32)
        for head in range(2):
            scores = mm_last(key_own[head, :last], query)
            probs = jnp.where(allowed, jnp.exp(scores - total_ref[0, head : head + 1, rows]), 0.0)
            delta = jnp.sum(products[head * HD : (head + 1) * HD], axis=0, keepdims=True)
            grad_probs = mm_last(value_own[head, :last], grad)
            grad_scores = (probs * (grad_probs - delta)).astype(jnp.bfloat16)
            value_grad[:last] += matmul(probs.astype(jnp.bfloat16), of_head(grad, head))
            key_grad[:last] += matmul(grad_scores, of_head(query, head))
            query_grad += matmul(key_turned[head, :, :last], grad_scores)
        out_ref[rows, lanes(0)] = undone(query_grad.T * HD**-0.5, rows)
    everything = slice(0, length)
    out_ref[:, lanes(1)] = undone(key_grad[...], everything)
    out_ref[:, lanes(2)] = value_grad[...].astype(jnp.bfloat16)


def attend_forward(qkv, cos_table, sin_table, starts):
    length, width = qkv.shape[0], qkv.shape[1] // 3
    pairs = width // LANES
    whole = pl.BlockSpec((length, LANES), lambda p: (0, 0))
    own = pl.BlockSpec((length, LANES), lambda p: (0, p))
    low = jax.ShapeDtypeStruct((length, width), jnp.bfloat16)
    work = pairs * length * length
    return pl.pallas_call(
        attend_kernel,
        grid=(pairs,),
        in_specs=[
            own,
            pl.BlockSpec((length, LANES), lambda p: (0, pairs + p)),
            pl.BlockSpec((length, LANES), lambda p: (0, 2 * pairs + p)),
            whole,
            whole,
            pl.BlockSpec((1, length), lambda p: (0, 0)),
        ],
        out_specs=[own] * 5 + [pl.BlockSpec((1, 2, length), lambda p: (p, 0, 0))],
        out_shape=[
            jax.ShapeDtypeStruct((length, width), jnp.float32),
            low,
            low,
            low,
            low,
            jax.ShapeDtypeStruct((pairs, 2, length), jnp.float32),
        ],
        scratch_shapes=[
            pltpu.VMEM((2, length, LANES), jnp.bfloat16),
            pltpu.VMEM((2, LANES, length), jnp.bfloat16),
        ],
        compiler_params=pltpu.CompilerParams(vmem_limit_bytes=48 << 20),
        cost_estimate=pl.CostEstimate(
            flops=8 * work * LANES, bytes_accessed=qkv.size * 8, transcendentals=2 * work
        ),
    )(qkv, qkv, qkv, cos_table, sin_table, starts)


def attend_backward(query, key, value, grad, attended, total, cos_table, sin_table, starts):
    length, width = query.shape
    pairs = width // LANES
    whole = pl.BlockSpec((length, LANES), lambda p: (0, 0))
    own = pl.BlockSpec((length, LANES), lambda p: (0, p))
    work = pairs * length * length
    return pl.pallas_call(
        attend_back_kernel,
        grid=(pairs,),
        in_specs=[own] * 5
        + [
            pl.BlockSpec((1, 2, length), lambda p: (p, 0, 0)),
            whole,
            whole,
            pl.BlockSpec((1, length), lambda p: (0, 0)),
        ],
        out_specs=pl.BlockSpec((length, 3 * width), lambda p: (0, 0)),
        out_shape=jax.ShapeDtypeStruct((length, 3 * width), jnp.bfloat16),
        scratch_shapes=[
            pltpu.VMEM((2, length, LANES), jnp.bfloat16),
            pltpu.VMEM((2, length, LANES), jnp.bfloat16),
            pltpu.VMEM((2, LANES, length), jnp.bfloat16),
            pltpu.VMEM((length, LANES), jnp.float32),
            pltpu.VMEM((length, LANES), jnp.float32),
        ],
        compiler_params=pltpu.CompilerParams(vmem_limit_bytes=48 << 20),
        cost_estimate=pl.CostEstimate(
            flops=20 * work * LANES, bytes_accessed=query.size * 16, transcendentals=2 * work
        ),
    )(query, key, value, grad, attended, total, cos_table, sin_table, starts)


def on_device(
    tokens,
    out_grad,
    doc_lengths,
    qkv_weight,
    qkv_first,
    qkv_second,
    out_weight,
    out_first,
    out_second,
    gate_up_weight,
    gate_up_first,
    gate_up_second,
    down_weight,
    down_first,
    down_second,
    gains,
    gain_first,
    gain_second,
):
    local_rows = tokens.shape[1]
    model_width = tokens.shape[2]
    rows_own = qkv_weight.shape[0]
    seq_total = lax.axis_size("seq")
    batch_total = lax.axis_size("batch")
    head_width = model_width // seq_total
    heads = head_width // HD
    length = local_rows * seq_total
    hidden = down_weight.shape[1] // seq_total
    score_scale = HD ** (-0.5)
    positions = jnp.arange(length, dtype=jnp.int32)
    ends = jnp.cumsum(doc_lengths[0])
    starts = jnp.max(jnp.where(positions[:, None] >= ends[None, :], ends[None, :], 0), axis=1)
    cos_table, sin_table = rope_tables(positions)
    in_pairs = head_width % LANES == 0 and length % QUERY_ROWS == 0
    if in_pairs:
        sign = jnp.where(jnp.arange(HD) < HD // 2, -1.0, 1.0)
        cos_pair = jnp.tile(cos_table, (1, 2))
        sin_pair = jnp.tile(sin_table * sign, (1, 2))

    def split_heads(columns):
        return jnp.transpose(columns.reshape(length, heads, HD), (1, 0, 2))

    def join_heads(values):
        return jnp.transpose(values, (1, 0, 2)).reshape(length, head_width)

    def allowed_pairs():
        return (
            (positions[None, :] <= positions[:, None]) & (positions[None, :] >= starts[:, None])
        )[None]

    def attention(qkv):
        if in_pairs:
            attended, low, *kept = attend_forward(qkv, cos_pair, sin_pair, starts[None])
            return (low, (attended, kept))
        query = split_heads(qkv[:, :head_width])
        query = apply_rope(query, cos_table, sin_table).astype(jnp.bfloat16)
        key = split_heads(qkv[:, head_width : 2 * head_width])
        key = apply_rope(key, cos_table, sin_table).astype(jnp.bfloat16)
        value = split_heads(qkv[:, 2 * head_width :]).astype(jnp.bfloat16)
        scores = jnp.einsum("hqd,hkd->hqk", query, key, preferred_element_type=jnp.float32)
        scores = jnp.where(allowed_pairs(), scores * score_scale, masked_score)
        probs = jax.nn.softmax(scores, axis=-1)
        attended = jnp.einsum(
            "hqk,hkd->hqd", probs.astype(jnp.bfloat16), value, preferred_element_type=jnp.float32
        )
        return (join_heads(attended.astype(jnp.bfloat16)), (attended, (query, key, value, probs)))

    def attention_back(grad, kept):
        if in_pairs:
            attended, (query, key, value, total) = kept
            return attend_backward(
                query, key, value, grad, attended, total, cos_pair, sin_pair, starts[None]
            )
        attended, (query, key, value, probs) = kept
        grad = split_heads(grad)
        delta = jnp.sum(grad.astype(jnp.float32) * attended, axis=-1, keepdims=True)
        grad_probs = jnp.einsum("hqd,hkd->hqk", grad, value, preferred_element_type=jnp.float32)
        grad_scores = (probs * (grad_probs - delta)).astype(jnp.bfloat16)

        def over_queries(left, right):
            return jnp.einsum("hqk,hqd->hkd", left, right, preferred_element_type=jnp.float32)

        grad_value = over_queries(probs.astype(jnp.bfloat16), grad)
        grad_key = over_queries(grad_scores, query) * score_scale
        grad_query = (
            jnp.einsum("hqk,hkd->hqd", grad_scores, key, preferred_element_type=jnp.float32)
            * score_scale
        )
        return jnp.concatenate(
            [
                join_heads(undo_rope(grad_query, cos_table, sin_table)),
                join_heads(undo_rope(grad_key, cos_table, sin_table)),
                join_heads(grad_value),
            ],
            axis=1,
        ).astype(jnp.bfloat16)

    far = seq_total // 2
    first_row = lax.axis_index("seq") * local_rows
    gains_here = to_relative(gains, rows_own)
    tokens_here = to_relative(tokens[0], rows_own)
    grads_here = to_relative(out_grad[0], rows_own)
    out_here = jnp.stack(batch_columns(out_weight.astype(jnp.bfloat16), rows_own))
    out_here = lax.all_to_all(out_here, "batch", 0, 0, tiled=True).reshape(head_width, -1)
    out_here = with_rows(out_here, local_rows)
    qkv_low = rounded_by_owner(qkv_weight, 3)
    gate_low = rounded_by_owner(gate_up_weight, 2)
    down_low = rounded_by_owner(down_weight, 1)
    qkv_block = to_column_owners(qkv_low)
    tokens_all, grads_all, out_all = ring_gather(
        after_all([tokens_here, grads_here, out_here], (qkv_low, gate_low, down_low)),
        ((qkv_block,),),
    )
    tokens_all, grads_all = stacked_rows(tokens_all), stacked_rows(grads_all)
    out_all = stacked_rows(
        {offset: with_rows(block, head_width) for offset, block in out_all.items()}
    )
    qkv_full = gather_batch(qkv_block)
    gate_block = to_column_owners(after(gate_low, tokens_all))
    down_block = to_column_owners(after(down_low, gate_block))

    inputs = tokens_all.astype(jnp.float32)
    act_one = (unit_rows(inputs)[0] * gains_here[0]).astype(jnp.bfloat16)
    qkv = matmul(act_one, qkv_full)
    attn_own, attn_kept = attention(qkv)

    out_full = jnp.concatenate(gather_pieces(out_all), axis=1)

    attn_own_late = after(attn_own, gate_block)
    attn_all = stacked_columns(ring_gather([attn_own_late], ((down_block,),))[0])
    gate_full = gather_batch(gate_block)
    down_full = gather_batch(down_block)
    middle_all = inputs + matmul(attn_all, out_full)
    act_two = (unit_rows(middle_all)[0] * gains_here[1]).astype(jnp.bfloat16)

    def feed_forward(rows, grads):
        gate_up = matmul(rows, gate_full)
        gate_part = gate_up[:, :hidden]
        up_part = gate_up[:, hidden:]
        sigmoid_gate = jax.nn.sigmoid(gate_part)
        silu_gate = gate_part * sigmoid_gate
        hidden_low = (silu_gate * up_part).astype(jnp.bfloat16)
        grad_hidden = matmul(grads, down_full)
        grad_gate = (
            grad_hidden * up_part * (sigmoid_gate * (1.0 + gate_part * (1.0 - sigmoid_gate)))
        )
        grad_up = grad_hidden * silu_gate
        grad_gate_up = jnp.concatenate([grad_gate, grad_up], axis=1).astype(jnp.bfloat16)
        grad_two = contract_cols(grad_gate_up, gate_full).astype(jnp.bfloat16)
        block_part = contract_cols(hidden_low, down_full).astype(jnp.bfloat16)
        return (grad_gate_up, hidden_low, grad_two, block_part)

    offsets = [far] + [sign * step for step in range(far - 1, 0, -1) for sign in (1, -1)] + [0]
    grad_gate_up, hidden_low, grad_two, block_part = feed_forward(act_two, grads_all)
    hidden_late, gate_up_late = after_all((hidden_low, grad_gate_up), (grad_two, block_part))
    down_own, down_sends = partial_sum_batch(grads_all, hidden_late)
    gate_own, gate_sends = partial_sum_batch(act_two, gate_up_late)
    grad_two, block_rest = ring_scatter_sum(
        [
            {offset: ring_rows(whole, [offset]) for offset in offsets}
            for whole in (grad_two, block_part)
        ],
        ((down_sends[0], gate_sends[0]), (down_sends[-1], gate_sends[-1]), (down_own,)),
    )

    def own_rows(whole):
        return lax.dynamic_slice_in_dim(whole, first_row, local_rows, 0)

    middle = own_rows(middle_all)
    unit_two, scale_two = unit_rows(middle)
    block_out = from_relative((middle + block_rest).astype(jnp.bfloat16), rows_own)
    grad_mid_norm, gain_two_grad = norm_back(grad_two, unit_two, scale_two, gains_here[1])
    grad_middle = grads_here.astype(jnp.float32) + grad_mid_norm
    grad_attn_low = grad_middle.astype(jnp.bfloat16)
    grad_heads = contract_cols(grad_attn_low, out_full).astype(jnp.bfloat16)
    by_owner = jnp.concatenate(
        [
            grad_heads.reshape(local_rows, seq_total, head_width),
            from_relative(grad_attn_low, rows_own).reshape(local_rows, seq_total, head_width),
        ],
        axis=2,
    )
    got = lax.all_to_all(jnp.transpose(by_owner, (1, 0, 2)), "seq", 0, 0, tiled=True)
    got = got.reshape(length, 2 * head_width)
    grad_heads = got[:, :head_width]
    grad_attn_own = got[:, head_width:]
    down_grad = to_row_owners(after(down_own, got))
    gate_grad = to_row_owners(after(gate_own, down_grad))

    grad_qkv = attention_back(grad_heads, attn_kept)
    qkv_own, qkv_sends = partial_sum_batch(act_one, grad_qkv)
    out_part = contract_rows(attn_all, grad_attn_own).astype(jnp.bfloat16)
    out_part = out_part.reshape(seq_total, batch_total, rows_own, head_width)
    out_part = [
        out_part[:, b].reshape(seq_total * rows_own, head_width) for b in range(batch_total)
    ]
    out_own = scatter_sum_batch(jnp.stack([of_offset(out_part, m) for m in range(batch_total)]))
    grad_qkv = after(grad_qkv, qkv_sends[0], out_own)
    grad_one_part = contract_cols(grad_qkv, qkv_full)
    gain_one_part = jnp.sum(grad_one_part * act_one.astype(jnp.float32), axis=0)
    gain_grad = jnp.stack([gain_one_part / gains_here[0], gain_two_grad])
    gain_grad = sum_everywhere(from_relative(gain_grad, rows_own))
    down_m, down_s, down_w = adam_by_owner(
        down_weight, down_first, down_second, down_grad, 1, rate_down
    )
    grad_one = ring_scatter_one(
        grad_one_part.astype(jnp.bfloat16), ((qkv_sends[-1], down_m), (gate_grad,), (qkv_own,))
    )
    unit_one, scale_one = unit_rows(tokens_here.astype(jnp.float32))
    grad_in_norm = norm_back(grad_one, unit_one, scale_one, gains_here[0])[0]
    input_grad = from_relative(grad_middle + grad_in_norm, rows_own)
    qkv_grad = to_row_owners(
        jnp.concatenate([after(qkv_own, gate_grad), out_own], axis=1)
    )

    qkv_m, qkv_s, qkv_w = adam_by_owner(
        qkv_weight, qkv_first, qkv_second, qkv_grad, 3, rate_qkv
    )
    out_m, out_s, out_w = adam_by_owner(
        out_weight, out_first, out_second, qkv_grad, 1, rate_out, skipped=3
    )
    gate_m, gate_s, gate_w = adam_by_owner(
        gate_up_weight, gate_up_first, gate_up_second, gate_grad, 2, rate_gate
    )
    gain_m, gain_s, gain_w = adam_update(gains, gain_first, gain_second, gain_grad, rate_gain)
    return (
        block_out[None],
        input_grad[None],
        qkv_m,
        qkv_s,
        qkv_w,
        out_m,
        out_s,
        out_w,
        gate_m,
        gate_s,
        gate_w,
        down_m,
        down_s,
        down_w,
        gain_m,
        gain_s,
        gain_w,
    )


def solution(mesh):
    rows = P(("seq", "batch"), None)
    blocks = P("batch", "seq", None)
    return jax.shard_map(
        on_device,
        mesh=mesh,
        in_specs=(blocks, blocks, P("batch", None)) + (rows,) * 12 + (P(),) * 3,
        out_specs=(blocks, blocks) + (rows,) * 12 + (P(),) * 3,
        check_vma=False,
    )
```

```python
import jax
import jax.numpy as jnp
from jax import lax
from jax.experimental import pallas as pl
from jax.experimental.pallas import tpu as pltpu
from jax.sharding import PartitionSpec as P

HD = 64
STEP = 10
LANES = 128
QUERY_ROWS = 256


norm_eps = 1e-05
rope_base = 130000.0
beta_one = 0.9
beta_two = 0.95
adam_eps = 1e-08
weight_decay = 0.1
masked_score = -1e30
rate_qkv = 0.05
rate_out = 0.5
rate_gate = 0.05
rate_down = 0.03
rate_gain = 0.3


def rotate_half(values):
    middle = values.shape[-1] // 2
    return jnp.concatenate([-values[..., middle:], values[..., :middle]], axis=-1)


def rope_tables(positions):
    inverse = rope_base ** (-jnp.arange(0, HD, 2, dtype=jnp.float32) / HD)
    angles = positions.astype(jnp.float32)[:, None] * inverse[None, :]
    angles = jnp.concatenate([angles, angles], axis=1)
    return (jnp.cos(angles), jnp.sin(angles))


def apply_rope(values, cos_table, sin_table):
    return values * cos_table + rotate_half(values) * sin_table


def undo_rope(values, cos_table, sin_table):
    return values * cos_table - rotate_half(values) * sin_table


def unit_rows(values):
    scale_rows = lax.rsqrt(jnp.mean(values * values, axis=-1, keepdims=True) + norm_eps)
    return (values * scale_rows, scale_rows)


def norm_back(grad_normed, unit_values, scale_rows, gain_row):
    grad_unit = grad_normed * gain_row
    gain_part = jnp.sum(grad_normed * unit_values, axis=0)
    grad_values = scale_rows * (
        grad_unit - unit_values * jnp.mean(grad_unit * unit_values, axis=-1, keepdims=True)
    )
    return (grad_values, gain_part)


def contract_rows(left_side, right_side):
    return lax.dot_general(
        left_side, right_side, (((0,), (0,)), ((), ())), preferred_element_type=jnp.float32
    )


def contract_cols(left_side, right_side):
    return lax.dot_general(
        left_side, right_side, (((1,), (1,)), ((), ())), preferred_element_type=jnp.float32
    )


def matmul(left_side, right_side):
    return jnp.dot(left_side, right_side, preferred_element_type=jnp.float32)


def adam_update(weight, first_moment, second, gradient, step_rate):
    first_new = beta_one * first_moment + (1.0 - beta_one) * gradient
    second_new = beta_two * second + (1.0 - beta_two) * gradient * gradient
    first_hat = first_new / (1.0 - beta_one**STEP)
    second_hat = second_new / (1.0 - beta_two**STEP)
    weight_new = weight - step_rate * (
        first_hat / (jnp.sqrt(second_hat) + adam_eps) + weight_decay * weight
    )
    return (first_new, second_new, weight_new)


def swapped(value, axis, bit):
    count = lax.axis_size(axis)
    return lax.ppermute(value, axis, [(source, source ^ bit) for source in range(count)])


def ring_order(count):
    return list(range(0, count, 2)) + list(range(count - 1, 0, -2))


def ring_shift(value, steps):
    count = lax.axis_size("seq")
    order = ring_order(count)
    pairs = [(order[i], order[(i + steps) % count]) for i in range(count)]
    return lax.ppermute(value, "seq", pairs)


def ring_place(offset):
    count = lax.axis_size("seq")
    order = ring_order(count)
    table = jnp.array([order[(order.index(own) + offset) % count] for own in range(count)], jnp.int32)
    return table[lax.axis_index("seq")]


def filled(arrays, filler):
    return filler(arrays) if callable(filler) else after_all(arrays, filler)


def ring_gather(parts, fillers=()):
    count = lax.axis_size("seq")
    far = count // 2
    packed = jnp.concatenate(parts, axis=1) if len(parts) > 1 else parts[0]
    middle = packed.shape[1] // 2
    blocks = {0: packed}
    ahead = behind = packed
    for step in range(1, far):
        if 0 <= step - 2 < len(fillers):
            ahead, behind = filled((ahead, behind), fillers[step - 2])
        ahead, behind = ring_shift(ahead, 1), ring_shift(behind, -1)
        blocks[-step], blocks[step] = ahead, behind
    if far - 2 < len(fillers):
        ahead, behind = filled((ahead, behind), fillers[far - 2])
    left, right = ring_shift(ahead[:, :middle], 1), ring_shift(behind[:, middle:], -1)
    blocks[far] = jnp.concatenate([left, right], axis=1)
    gathered = []
    first = 0
    for part in parts:
        last = first + part.shape[1]
        gathered.append({offset: block[:, first:last] for offset, block in blocks.items()})
        first = last
    return gathered


def with_rows(block, rows):
    if block.shape[0] >= rows:
        return jnp.concatenate(jnp.split(block, block.shape[0] // rows, axis=0), axis=1)
    return jnp.concatenate(jnp.split(block, rows // block.shape[0], axis=1), axis=0)


def stacked_rows(blocks):
    rows, width = blocks[0].shape
    whole = jnp.zeros((len(blocks) * rows, width), blocks[0].dtype)
    for offset, block in blocks.items():
        whole = lax.dynamic_update_slice(whole, block, (ring_place(offset) * rows, 0))
    return whole


def stacked_columns(blocks):
    rows, width = blocks[0].shape
    whole = jnp.zeros((rows, len(blocks) * width), blocks[0].dtype)
    for offset, block in blocks.items():
        whole = lax.dynamic_update_slice(whole, block, (0, ring_place(offset) * width))
    return whole


def ring_rows(whole, offsets):
    rows = whole.shape[0] // lax.axis_size("seq")
    return jnp.concatenate(
        [lax.dynamic_slice_in_dim(whole, ring_place(o) * rows, rows, 0) for o in offsets], axis=0
    )


def added(block, got):
    return (block.astype(jnp.float32) + got.astype(jnp.float32)).astype(block.dtype)


def ring_scatter_sum(parts, fillers=()):
    far = lax.axis_size("seq") // 2
    first, second = parts
    ahead, behind = [ring_shift(first[far], 1)], [ring_shift(second[far], -1)]
    for turn, step in enumerate(range(far - 1, 0, -1)):
        onward = [first[step], second[step]]
        backward = [first[-step], second[-step]]
        if turn == 0:
            onward[0] = added(onward[0], ahead[0])
            backward[1] = added(backward[1], behind[0])
        else:
            onward = [added(block, got) for block, got in zip(onward, ahead)]
            backward = [added(block, got) for block, got in zip(backward, behind)]
        if turn < len(fillers):
            needed = fillers[turn]
            if callable(needed):
                needed = needed(ahead + behind)
            moved = after_all(onward + backward, needed)
            onward, backward = moved[:2], moved[2:]
        ahead = [ring_shift(block, 1) for block in onward]
        behind = [ring_shift(block, -1) for block in backward]
    if far - 1 < len(fillers):
        needed = fillers[far - 1]
        if callable(needed):
            needed = needed(ahead + behind)
        moved = after_all(ahead + behind, needed)
        ahead, behind = moved[:2], moved[2:]
    return [
        own.astype(jnp.float32) + left.astype(jnp.float32) + right.astype(jnp.float32)
        for own, left, right in zip((first[0], second[0]), ahead, behind)
    ]


def ring_scatter_one(whole, fillers=()):
    far = lax.axis_size("seq") // 2
    middle = whole.shape[1] // 2
    offsets = [0] + [sign * step for step in range(1, far) for sign in (1, -1)] + [far]
    blocks = {offset: ring_rows(whole, [offset]) for offset in offsets}
    halves = ring_scatter_sum(
        (
            {offset: block[:, :middle] for offset, block in blocks.items()},
            {offset: block[:, middle:] for offset, block in blocks.items()},
        ),
        fillers,
    )
    return jnp.concatenate(halves, axis=1)


def sum_everywhere(values):
    total = lax.axis_size("seq") * lax.axis_size("batch")
    copies = jnp.broadcast_to(values[None], (total,) + values.shape)
    return jnp.sum(lax.all_to_all(copies, ("seq", "batch"), 0, 0, tiled=True), axis=0)


def after(value, *others):
    return lax.optimization_barrier((value,) + others)[0]


def after_all(values, others):
    return lax.optimization_barrier(tuple(values) + tuple(others))[: len(values)]


def batch_bits():
    count = lax.axis_size("batch")
    bits = []
    while (1 << len(bits)) < count:
        bits.append(1 << len(bits))
    return bits


def of_offset(choices, offset):
    index = lax.axis_index("batch")
    picked = choices[offset]
    for own in range(1, len(choices)):
        picked = jnp.where(index == own, choices[own ^ offset], picked)
    return picked


def offset_order():
    order = [0]
    for bit in reversed(batch_bits()):
        order = order + [offset ^ bit for offset in order]
    return order


def batch_columns(rows, rows_own):
    count, width = rows.shape
    batch_total = lax.axis_size("batch")
    blocks = rows.reshape(count, -1, batch_total, rows_own)
    return [blocks[:, :, b].reshape(count, width // batch_total) for b in range(batch_total)]


def to_relative(rows, rows_own):
    columns = batch_columns(rows, rows_own)
    return jnp.concatenate([of_offset(columns, m) for m in offset_order()], axis=1)


def from_relative(rows, rows_own):
    count, width = rows.shape
    batch_total = lax.axis_size("batch")
    order = offset_order()
    part = width // batch_total
    columns = [
        rows[:, order.index(m) * part : (order.index(m) + 1) * part] for m in range(batch_total)
    ]
    blocks = [
        of_offset(columns, b).reshape(count, width // (batch_total * rows_own), rows_own)
        for b in range(batch_total)
    ]
    return jnp.stack(blocks, axis=2).reshape(count, width)


def gather_pieces(block):
    pieces = [block]
    for bit in reversed(batch_bits()):
        pieces = pieces + [swapped(piece, "batch", bit) for piece in pieces]
    return pieces


def gather_batch(block):
    return jnp.concatenate(gather_pieces(block), axis=0)


def partial_sum_batch(left, right):
    width = left.shape[1]
    held = None
    sends = []

    def product(first, last):
        part = contract_rows(left[:, first:last], right)
        return part if held is None else part + held[first:last]

    for bit in batch_bits():
        half = width // 2
        sends.append(product(half, width).astype(jnp.bfloat16))
        got = swapped(sends[-1], "batch", bit).astype(jnp.float32)
        held = got if held is None else held[:half] + got
        width = half
    return (product(0, width).astype(jnp.bfloat16), sends)


def scatter_sum_batch(blocks):
    held = blocks
    for bit in batch_bits():
        pairs = held.reshape((held.shape[0] // 2, 2) + held.shape[1:])
        got = swapped(pairs[:, 1], "batch", bit)
        held = (pairs[:, 0].astype(jnp.float32) + got.astype(jnp.float32)).astype(jnp.bfloat16)
    return held[0]


def seqs_in_block(columns, seq_total):
    return max(1, min(seq_total, 1024 // columns))


def rounded_by_owner(weight, groups):
    rows_own, width = weight.shape
    seq_total = lax.axis_size("seq")
    columns = width // (groups * seq_total)
    if columns % LANES:
        blocks = weight.astype(jnp.bfloat16).reshape(rows_own, groups, seq_total, columns)
        return jnp.transpose(blocks, (2, 0, 1, 3)).reshape(seq_total, rows_own, groups * columns)
    taken = seqs_in_block(columns, seq_total)
    steps = seq_total // taken

    def kernel(weight_ref, out_ref):
        for place in range(taken):
            out_ref[place] = weight_ref[:, place * columns : (place + 1) * columns].astype(
                jnp.bfloat16
            )

    return pl.pallas_call(
        kernel,
        grid=(groups, steps),
        in_specs=[pl.BlockSpec((rows_own, taken * columns), lambda g, j: (0, g * steps + j))],
        out_specs=pl.BlockSpec((taken, rows_own, columns), lambda g, j: (j, 0, g)),
        out_shape=jax.ShapeDtypeStruct(
            (seq_total, rows_own, groups * columns), jnp.bfloat16
        ),
        cost_estimate=pl.CostEstimate(flops=0, bytes_accessed=weight.size * 6, transcendentals=0),
    )(weight)


def to_column_owners(blocks):
    got = lax.all_to_all(blocks, "seq", 0, 0, tiled=True)
    return got.reshape(-1, blocks.shape[2])


def to_row_owners(grad):
    seq_total = lax.axis_size("seq")
    blocks = grad.reshape(seq_total, grad.shape[0] // seq_total, grad.shape[1])
    return lax.all_to_all(blocks, "seq", 0, 0, tiled=True)


def adam_by_owner(weight, first_moment, second, gradient, groups, step_rate, skipped=0):
    rows_own, width = weight.shape
    seq_total = lax.axis_size("seq")
    columns = width // (groups * seq_total)
    if columns % LANES:
        own = gradient[:, :, skipped * columns : (skipped + groups) * columns]
        natural = jnp.transpose(
            own.reshape(seq_total, rows_own, groups, columns), (1, 2, 0, 3)
        ).reshape(rows_own, width)
        return adam_update(weight, first_moment, second, natural.astype(jnp.float32), step_rate)
    taken = seqs_in_block(columns, seq_total)
    steps = seq_total // taken

    def kernel(weight_ref, first_ref, second_ref, gradient_ref, *out_refs):
        for place in range(taken):
            here = slice(place * columns, (place + 1) * columns)
            results = adam_update(
                weight_ref[:, here],
                first_ref[:, here],
                second_ref[:, here],
                gradient_ref[place].astype(jnp.float32),
                step_rate,
            )
            for out_ref, result in zip(out_refs, results):
                out_ref[:, here] = result

    whole = pl.BlockSpec((rows_own, taken * columns), lambda g, j: (0, g * steps + j))
    return pl.pallas_call(
        kernel,
        grid=(groups, steps),
        in_specs=[whole] * 3 + [
            pl.BlockSpec((taken, rows_own, columns), lambda g, j: (j, 0, g + skipped))
        ],
        out_specs=[whole] * 3,
        out_shape=[jax.ShapeDtypeStruct(weight.shape, jnp.float32)] * 3,
        cost_estimate=pl.CostEstimate(
            flops=weight.size * 15, bytes_accessed=weight.size * 26, transcendentals=weight.size
        ),
    )(weight, first_moment, second, gradient)


def swap_halves(values):
    lane = lax.broadcasted_iota(jnp.int32, values.shape, 1)
    return jnp.where(
        lane % HD < HD // 2,
        pltpu.roll(values, LANES - HD // 2, 1),
        pltpu.roll(values, HD // 2, 1),
    )


def of_head(values, head, axis=1):
    lane = lax.broadcasted_iota(jnp.int32, values.shape, axis)
    return jnp.where(lane // HD == head, values, jnp.zeros_like(values))


def allowed_here(starts_ref, first, rows):
    shape = (rows, QUERY_ROWS)
    key = lax.broadcasted_iota(jnp.int32, shape, 0)
    query = lax.broadcasted_iota(jnp.int32, shape, 1) + first
    return (key <= query) & (key >= starts_ref[:, first : first + QUERY_ROWS])


def mm_last(left, right):
    return lax.dot_general(
        left, right, (((1,), (1,)), ((), ())), preferred_element_type=jnp.float32
    )


def attend_kernel(
    query_in, key_in, value_in, cos_ref, sin_ref, starts_ref,
    out_ref, low_ref, query_ref, key_ref, value_ref, total_ref, key_own, value_turned,
):
    length = query_in.shape[0]
    cos, sin = cos_ref[...], sin_ref[...]
    raw_query, raw_key = query_in[...], key_in[...]
    query_ref[...] = (raw_query * cos + swap_halves(raw_query) * sin).astype(jnp.bfloat16) * HD**-0.5
    key_ref[...] = (raw_key * cos + swap_halves(raw_key) * sin).astype(jnp.bfloat16)
    value_ref[...] = value_in[...].astype(jnp.bfloat16)
    turned = value_in[...].T
    for head in range(2):
        key_own[head] = of_head(key_ref[...], head)
        value_turned[head] = of_head(turned, head, 0).astype(jnp.bfloat16)
    for first in range(0, length, QUERY_ROWS):
        last = first + QUERY_ROWS
        allowed = allowed_here(starts_ref, first, last)
        weighted = jnp.zeros((LANES, QUERY_ROWS), jnp.float32)
        for head in range(2):
            scores = mm_last(key_own[head, :last], query_ref[first:last])
            scores = jnp.where(allowed, scores, masked_score)
            top = jnp.max(scores, axis=0, keepdims=True)
            powers = jnp.exp(scores - top)
            total = jnp.sum(powers, axis=0, keepdims=True)
            probs = (powers * (1.0 / total)).astype(jnp.bfloat16)
            weighted += matmul(value_turned[head, :, :last], probs)
            total_ref[0, head : head + 1, first:last] = top + jnp.log(total)
        attended = weighted.T
        out_ref[first:last] = attended
        low_ref[first:last] = attended.astype(jnp.bfloat16)


def attend_back_kernel(
    query_ref, key_ref, value_ref, grad_ref, attended_ref, total_ref, cos_ref, sin_ref, starts_ref,
    out_ref, key_own, value_own, key_turned, key_grad, value_grad,
):
    length = query_ref.shape[0]
    pair = pl.program_id(0)
    width = out_ref.shape[1] // 3
    turned = key_ref[...].astype(jnp.float32).T
    for head in range(2):
        key_own[head] = of_head(key_ref[...], head)
        value_own[head] = of_head(value_ref[...], head)
        key_turned[head] = of_head(turned, head, 0).astype(jnp.bfloat16)
    key_grad[...] = jnp.zeros_like(key_grad)
    value_grad[...] = jnp.zeros_like(value_grad)

    def undone(values, rows):
        back = values * cos_ref[rows] - swap_halves(values) * sin_ref[rows]
        return back.astype(jnp.bfloat16)

    def lanes(group):
        return pl.ds(pl.multiple_of(group * width + pair * LANES, LANES), LANES)

    for first in range(0, length, QUERY_ROWS):
        last = first + QUERY_ROWS
        rows = slice(first, last)
        allowed = allowed_here(starts_ref, first, last)
        grad, query = grad_ref[rows], query_ref[rows]
        products = (grad.astype(jnp.float32) * attended_ref[rows]).T
        query_grad = jnp.zeros((LANES, QUERY_ROWS), jnp.float32)
        for head in range(2):
            scores = mm_last(key_own[head, :last], query)
            probs = jnp.where(allowed, jnp.exp(scores - total_ref[0, head : head + 1, rows]), 0.0)
            delta = jnp.sum(products[head * HD : (head + 1) * HD], axis=0, keepdims=True)
            grad_probs = mm_last(value_own[head, :last], grad)
            grad_scores = (probs * (grad_probs - delta)).astype(jnp.bfloat16)
            value_grad[:last] += matmul(probs.astype(jnp.bfloat16), of_head(grad, head))
            key_grad[:last] += matmul(grad_scores, of_head(query, head))
            query_grad += matmul(key_turned[head, :, :last], grad_scores)
        out_ref[rows, lanes(0)] = undone(query_grad.T * HD**-0.5, rows)
    everything = slice(0, length)
    out_ref[:, lanes(1)] = undone(key_grad[...], everything)
    out_ref[:, lanes(2)] = value_grad[...].astype(jnp.bfloat16)


def project_kernel(total, attended_ref, inputs_ref, gain_ref, *refs):
    weight_refs, (middle_ref, unit_ref) = refs[:total], refs[total:]
    width = inputs_ref.shape[1]
    part = width // total
    attended = attended_ref[...]
    squares = 0.0
    for place, weight_ref in enumerate(weight_refs):
        columns = slice(place * part, (place + 1) * part)
        block = inputs_ref[:, columns].astype(jnp.float32) + matmul(attended, weight_ref[...])
        middle_ref[:, columns] = block
        squares += jnp.sum(block * block, axis=1, keepdims=True)
    scale = lax.rsqrt(squares / width + norm_eps)
    unit_ref[...] = (middle_ref[...] * scale * gain_ref[...]).astype(jnp.bfloat16)


def project_rows(attended, inputs, gain, pieces):
    length, width = inputs.shape
    total = len(pieces)
    rows = pl.BlockSpec((QUERY_ROWS, width), lambda i: (i, 0))
    return pl.pallas_call(
        lambda *refs: project_kernel(total, *refs),
        grid=(length // QUERY_ROWS,),
        in_specs=[rows, rows, pl.BlockSpec((1, width), lambda i: (0, 0))]
        + [pl.BlockSpec((width, width // total), lambda i: (0, 0))] * total,
        out_specs=[rows, rows],
        out_shape=[
            jax.ShapeDtypeStruct((length, width), jnp.float32),
            jax.ShapeDtypeStruct((length, width), jnp.bfloat16),
        ],
        compiler_params=pltpu.CompilerParams(vmem_limit_bytes=48 << 20),
        cost_estimate=pl.CostEstimate(
            flops=2 * length * width * width,
            bytes_accessed=10 * length * width + 2 * width * width,
            transcendentals=length,
        ),
    )(attended, inputs, gain, *pieces)


def summed_product(left_ref, weight_refs):
    part = left_ref.shape[1] // len(weight_refs)
    return sum(
        matmul(left_ref[:, place * part : (place + 1) * part], weight_ref[...])
        for place, weight_ref in enumerate(weight_refs)
    )


def hidden_kernel(total, rows_ref, *refs):
    gate_ref, up_ref, low_ref = refs[2 * total :]
    gate = summed_product(rows_ref, refs[:total])
    up = summed_product(rows_ref, refs[total : 2 * total])
    gate_ref[...] = gate
    up_ref[...] = up
    low_ref[...] = (gate * jax.nn.sigmoid(gate) * up).astype(jnp.bfloat16)


def hidden_units(rows, gate_pieces):
    length, width = rows.shape
    total = len(gate_pieces)
    hidden = gate_pieces[0].shape[1] // 2
    tile = min(hidden, 2 * LANES)
    steps = hidden // tile
    own = pl.BlockSpec((length, tile), lambda j: (0, j))
    wide = jax.ShapeDtypeStruct((length, hidden), jnp.float32)
    return pl.pallas_call(
        lambda *refs: hidden_kernel(total, *refs),
        grid=(steps,),
        in_specs=[pl.BlockSpec((length, width), lambda j: (0, 0))]
        + [pl.BlockSpec((width // total, tile), lambda j: (0, j))] * total
        + [pl.BlockSpec((width // total, tile), lambda j: (0, steps + j))] * total,
        out_specs=[own] * 3,
        out_shape=[wide, wide, jax.ShapeDtypeStruct((length, hidden), jnp.bfloat16)],
        compiler_params=pltpu.CompilerParams(vmem_limit_bytes=48 << 20),
        cost_estimate=pl.CostEstimate(
            flops=4 * length * width * hidden,
            bytes_accessed=2 * length * width + 4 * width * hidden + 10 * length * hidden,
            transcendentals=length * hidden,
        ),
    )(rows, *gate_pieces, *gate_pieces)


def hidden_back_kernel(total, grads_ref, gate_ref, up_ref, *refs):
    grad_ref = refs[total]
    tile = gate_ref.shape[1]
    hidden = grad_ref.shape[1] // 2
    grad = summed_product(grads_ref, refs[:total])
    gate, up = gate_ref[...], up_ref[...]
    sigmoid = jax.nn.sigmoid(gate)
    first = pl.multiple_of(pl.program_id(0) * tile, tile)
    grad_gate = grad * up * (sigmoid * (1.0 + gate * (1.0 - sigmoid)))
    grad_ref[:, pl.ds(first, tile)] = grad_gate.astype(jnp.bfloat16)
    second = pl.multiple_of(hidden + pl.program_id(0) * tile, tile)
    grad_ref[:, pl.ds(second, tile)] = (grad * (gate * sigmoid)).astype(jnp.bfloat16)


def hidden_back(grads, gate, up, down_pieces):
    length, width = grads.shape
    total = len(down_pieces)
    hidden = gate.shape[1]
    tile = min(hidden, 2 * LANES)
    own = pl.BlockSpec((length, tile), lambda j: (0, j))
    return pl.pallas_call(
        lambda *refs: hidden_back_kernel(total, *refs),
        grid=(hidden // tile,),
        in_specs=[pl.BlockSpec((length, width), lambda j: (0, 0)), own, own]
        + [pl.BlockSpec((width // total, tile), lambda j: (0, j))] * total,
        out_specs=pl.BlockSpec((length, 2 * hidden), lambda j: (0, 0)),
        out_shape=jax.ShapeDtypeStruct((length, 2 * hidden), jnp.bfloat16),
        compiler_params=pltpu.CompilerParams(vmem_limit_bytes=48 << 20),
        cost_estimate=pl.CostEstimate(
            flops=2 * length * width * hidden,
            bytes_accessed=2 * length * width + 2 * width * hidden + 12 * length * hidden,
            transcendentals=length * hidden,
        ),
    )(grads, gate, up, *down_pieces)


def back_kernel(total, left_ref, *refs):
    each = pl.num_programs(0) // total
    for place in range(total):

        @pl.when(pl.program_id(0) // each == place)
        def _():
            refs[total][...] = mm_last(left_ref[...], refs[place][...]).astype(jnp.bfloat16)


def back_to_model(left, pieces):
    length, inner = left.shape
    total = len(pieces)
    part = pieces[0].shape[0]
    tile = min(part, 2 * LANES)
    each = part // tile

    def rows_of(place):
        return pl.BlockSpec((tile, inner), lambda i: (jnp.clip(i - place * each, 0, each - 1), 0))

    return pl.pallas_call(
        lambda *refs: back_kernel(total, *refs),
        grid=(total * each,),
        in_specs=[pl.BlockSpec((length, inner), lambda i: (0, 0))]
        + [rows_of(place) for place in range(total)],
        out_specs=pl.BlockSpec((length, tile), lambda i: (0, i)),
        out_shape=jax.ShapeDtypeStruct((length, part * total), jnp.bfloat16),
        compiler_params=pltpu.CompilerParams(vmem_limit_bytes=48 << 20),
        cost_estimate=pl.CostEstimate(
            flops=2 * length * part * total * inner,
            bytes_accessed=2 * inner * (length + part * total) + 2 * length * part * total,
            transcendentals=0,
        ),
    )(left, *pieces)


def attend_forward(qkv, cos_table, sin_table, starts):
    length, width = qkv.shape[0], qkv.shape[1] // 3
    pairs = width // LANES
    whole = pl.BlockSpec((length, LANES), lambda p: (0, 0))
    own = pl.BlockSpec((length, LANES), lambda p: (0, p))
    low = jax.ShapeDtypeStruct((length, width), jnp.bfloat16)
    work = pairs * length * length
    return pl.pallas_call(
        attend_kernel,
        grid=(pairs,),
        in_specs=[
            own,
            pl.BlockSpec((length, LANES), lambda p: (0, pairs + p)),
            pl.BlockSpec((length, LANES), lambda p: (0, 2 * pairs + p)),
            whole,
            whole,
            pl.BlockSpec((1, length), lambda p: (0, 0)),
        ],
        out_specs=[own] * 5 + [pl.BlockSpec((1, 2, length), lambda p: (p, 0, 0))],
        out_shape=[
            jax.ShapeDtypeStruct((length, width), jnp.float32),
            low,
            low,
            low,
            low,
            jax.ShapeDtypeStruct((pairs, 2, length), jnp.float32),
        ],
        scratch_shapes=[
            pltpu.VMEM((2, length, LANES), jnp.bfloat16),
            pltpu.VMEM((2, LANES, length), jnp.bfloat16),
        ],
        compiler_params=pltpu.CompilerParams(vmem_limit_bytes=48 << 20),
        cost_estimate=pl.CostEstimate(
            flops=8 * work * LANES, bytes_accessed=qkv.size * 8, transcendentals=2 * work
        ),
    )(qkv, qkv, qkv, cos_table, sin_table, starts)


def attend_backward(query, key, value, grad, attended, total, cos_table, sin_table, starts):
    length, width = query.shape
    pairs = width // LANES
    whole = pl.BlockSpec((length, LANES), lambda p: (0, 0))
    own = pl.BlockSpec((length, LANES), lambda p: (0, p))
    work = pairs * length * length
    return pl.pallas_call(
        attend_back_kernel,
        grid=(pairs,),
        in_specs=[own] * 5
        + [
            pl.BlockSpec((1, 2, length), lambda p: (p, 0, 0)),
            whole,
            whole,
            pl.BlockSpec((1, length), lambda p: (0, 0)),
        ],
        out_specs=pl.BlockSpec((length, 3 * width), lambda p: (0, 0)),
        out_shape=jax.ShapeDtypeStruct((length, 3 * width), jnp.bfloat16),
        scratch_shapes=[
            pltpu.VMEM((2, length, LANES), jnp.bfloat16),
            pltpu.VMEM((2, length, LANES), jnp.bfloat16),
            pltpu.VMEM((2, LANES, length), jnp.bfloat16),
            pltpu.VMEM((length, LANES), jnp.float32),
            pltpu.VMEM((length, LANES), jnp.float32),
        ],
        compiler_params=pltpu.CompilerParams(vmem_limit_bytes=48 << 20),
        cost_estimate=pl.CostEstimate(
            flops=20 * work * LANES, bytes_accessed=query.size * 16, transcendentals=2 * work
        ),
    )(query, key, value, grad, attended, total, cos_table, sin_table, starts)


def on_device(
    tokens,
    out_grad,
    doc_lengths,
    qkv_weight,
    qkv_first,
    qkv_second,
    out_weight,
    out_first,
    out_second,
    gate_up_weight,
    gate_up_first,
    gate_up_second,
    down_weight,
    down_first,
    down_second,
    gains,
    gain_first,
    gain_second,
):
    local_rows = tokens.shape[1]
    model_width = tokens.shape[2]
    rows_own = qkv_weight.shape[0]
    seq_total = lax.axis_size("seq")
    batch_total = lax.axis_size("batch")
    head_width = model_width // seq_total
    heads = head_width // HD
    length = local_rows * seq_total
    hidden = down_weight.shape[1] // seq_total
    score_scale = HD ** (-0.5)
    positions = jnp.arange(length, dtype=jnp.int32)
    ends = jnp.cumsum(doc_lengths[0])
    starts = jnp.max(jnp.where(positions[:, None] >= ends[None, :], ends[None, :], 0), axis=1)
    cos_table, sin_table = rope_tables(positions)
    in_pairs = head_width % LANES == 0 and length % QUERY_ROWS == 0
    if in_pairs:
        sign = jnp.where(jnp.arange(HD) < HD // 2, -1.0, 1.0)
        cos_pair = jnp.tile(cos_table, (1, 2))
        sin_pair = jnp.tile(sin_table * sign, (1, 2))

    def split_heads(columns):
        return jnp.transpose(columns.reshape(length, heads, HD), (1, 0, 2))

    def join_heads(values):
        return jnp.transpose(values, (1, 0, 2)).reshape(length, head_width)

    def allowed_pairs():
        return (
            (positions[None, :] <= positions[:, None]) & (positions[None, :] >= starts[:, None])
        )[None]

    def attention(qkv):
        if in_pairs:
            attended, low, *kept = attend_forward(qkv, cos_pair, sin_pair, starts[None])
            return (low, (attended, kept))
        query = split_heads(qkv[:, :head_width])
        query = apply_rope(query, cos_table, sin_table).astype(jnp.bfloat16)
        key = split_heads(qkv[:, head_width : 2 * head_width])
        key = apply_rope(key, cos_table, sin_table).astype(jnp.bfloat16)
        value = split_heads(qkv[:, 2 * head_width :]).astype(jnp.bfloat16)
        scores = jnp.einsum("hqd,hkd->hqk", query, key, preferred_element_type=jnp.float32)
        scores = jnp.where(allowed_pairs(), scores * score_scale, masked_score)
        probs = jax.nn.softmax(scores, axis=-1)
        attended = jnp.einsum(
            "hqk,hkd->hqd", probs.astype(jnp.bfloat16), value, preferred_element_type=jnp.float32
        )
        return (join_heads(attended.astype(jnp.bfloat16)), (attended, (query, key, value, probs)))

    def attention_back(grad, kept):
        if in_pairs:
            attended, (query, key, value, total) = kept
            return attend_backward(
                query, key, value, grad, attended, total, cos_pair, sin_pair, starts[None]
            )
        attended, (query, key, value, probs) = kept
        grad = split_heads(grad)
        delta = jnp.sum(grad.astype(jnp.float32) * attended, axis=-1, keepdims=True)
        grad_probs = jnp.einsum("hqd,hkd->hqk", grad, value, preferred_element_type=jnp.float32)
        grad_scores = (probs * (grad_probs - delta)).astype(jnp.bfloat16)

        def over_queries(left, right):
            return jnp.einsum("hqk,hqd->hkd", left, right, preferred_element_type=jnp.float32)

        grad_value = over_queries(probs.astype(jnp.bfloat16), grad)
        grad_key = over_queries(grad_scores, query) * score_scale
        grad_query = (
            jnp.einsum("hqk,hkd->hqd", grad_scores, key, preferred_element_type=jnp.float32)
            * score_scale
        )
        return jnp.concatenate(
            [
                join_heads(undo_rope(grad_query, cos_table, sin_table)),
                join_heads(undo_rope(grad_key, cos_table, sin_table)),
                join_heads(grad_value),
            ],
            axis=1,
        ).astype(jnp.bfloat16)

    far = seq_total // 2
    first_row = lax.axis_index("seq") * local_rows
    gains_here = to_relative(gains, rows_own)
    tokens_here = to_relative(tokens[0], rows_own)
    grads_here = to_relative(out_grad[0], rows_own)
    qkv_low = rounded_by_owner(qkv_weight, 3)
    out_columns = batch_columns(after(out_weight, qkv_low).astype(jnp.bfloat16), rows_own)
    out_here = [
        swapped(of_offset(out_columns, m), "batch", m) if m else of_offset(out_columns, m)
        for m in range(batch_total)
    ]
    out_here = [of_offset(out_here, b) for b in range(batch_total)]
    out_here = with_rows(jnp.concatenate(out_here, axis=0), local_rows)
    gate_low = rounded_by_owner(gate_up_weight, 2)
    down_low = rounded_by_owner(down_weight, 1)
    qkv_block = to_column_owners(qkv_low)
    tokens_all, out_all = ring_gather(
        [after(tokens_here, qkv_low), out_here], ((qkv_block,), (gate_low, down_low))
    )
    tokens_all = stacked_rows(tokens_all)
    out_all = stacked_rows(
        {offset: with_rows(block, head_width) for offset, block in out_all.items()}
    )
    qkv_full = gather_batch(qkv_block)
    gate_block = to_column_owners(after(gate_low, tokens_all))
    inputs = tokens_all.astype(jnp.float32)
    act_one = (unit_rows(inputs)[0] * gains_here[0]).astype(jnp.bfloat16)
    qkv = matmul(act_one, qkv_full)
    attn_own, attn_kept = attention(qkv)

    out_pieces = gather_pieces(out_all)
    out_full = jnp.concatenate(out_pieces, axis=1)

    gate_block = after(gate_block, attn_own)
    down_block = to_column_owners(after(down_low, gate_block))
    attn_own_late = after(attn_own, gate_block)
    attn_all = stacked_columns(ring_gather([attn_own_late], ((down_block,),))[0])
    gate_pieces, down_pieces = gather_pieces(gate_block), gather_pieces(down_block)
    grads_here_late = after(grads_here, attn_all)
    if in_pairs and length * model_width <= 1 << 21:
        middle_all, act_two = project_rows(attn_all, tokens_all, gains_here[1:], out_pieces)
        gate_part, up_part, hidden_low = hidden_units(act_two, gate_pieces)
        late = {}

        def block_meanwhile(moved):
            *moved, low = lax.optimization_barrier((*moved, hidden_low))
            late["block"] = back_to_model(low, down_pieces)
            return moved

        grads_all = ring_gather(
            [grads_here_late],
            ((act_two,), block_meanwhile, lambda moved: after_all(moved, (late["block"],))),
        )
        grads_all, block_part = stacked_rows(grads_all[0]), late["block"]
        grad_gate_up = hidden_back(grads_all, gate_part, up_part, down_pieces)
        grad_two = back_to_model(grad_gate_up, gate_pieces)
    else:
        grads_all = stacked_rows(ring_gather([grads_here_late])[0])
        middle_all = inputs + matmul(attn_all, out_full)
        act_two = (unit_rows(middle_all)[0] * gains_here[1]).astype(jnp.bfloat16)
        gate_full, down_full = jnp.concatenate(gate_pieces), jnp.concatenate(down_pieces)
        gate_up = matmul(act_two, gate_full)
        gate_part, up_part = gate_up[:, :hidden], gate_up[:, hidden:]
        sigmoid_gate = jax.nn.sigmoid(gate_part)
        silu_gate = gate_part * sigmoid_gate
        hidden_low = (silu_gate * up_part).astype(jnp.bfloat16)
        grad_hidden = matmul(grads_all, down_full)
        grad_gate = (
            grad_hidden * up_part * (sigmoid_gate * (1.0 + gate_part * (1.0 - sigmoid_gate)))
        )
        grad_gate_up = jnp.concatenate([grad_gate, grad_hidden * silu_gate], axis=1)
        grad_gate_up = grad_gate_up.astype(jnp.bfloat16)
        grad_two = contract_cols(grad_gate_up, gate_full).astype(jnp.bfloat16)
        block_part = contract_cols(hidden_low, down_full).astype(jnp.bfloat16)

    offsets = [far] + [sign * step for step in range(far - 1, 0, -1) for sign in (1, -1)] + [0]
    sums = {}

    def weight_sums(arrived):
        late = after_all((hidden_low, grad_gate_up), arrived)
        sums["down"] = partial_sum_batch(grads_all, late[0])
        sums["gate"] = partial_sum_batch(act_two, late[1])
        return ()

    def sent(stage):
        return lambda arrived: (sums["down"][1][stage], sums["gate"][1][stage])

    grad_two, block_rest = ring_scatter_sum(
        [
            {offset: ring_rows(whole, [offset]) for offset in offsets}
            for whole in (grad_two, block_part)
        ],
        (weight_sums, lambda arrived: (*sent(0)(arrived), *sent(-1)(arrived))),
    )
    down_own, gate_own = sums["down"][0], sums["gate"][0]

    def own_rows(whole):
        return lax.dynamic_slice_in_dim(whole, first_row, local_rows, 0)

    middle = own_rows(middle_all)
    unit_two, scale_two = unit_rows(middle)
    block_out = from_relative((middle + block_rest).astype(jnp.bfloat16), rows_own)
    grad_mid_norm, gain_two_grad = norm_back(grad_two, unit_two, scale_two, gains_here[1])
    grad_middle = grads_here.astype(jnp.float32) + grad_mid_norm
    grad_attn_low = grad_middle.astype(jnp.bfloat16)
    grad_heads = contract_cols(grad_attn_low, out_full).astype(jnp.bfloat16)
    by_owner = jnp.concatenate(
        [
            grad_heads.reshape(local_rows, seq_total, head_width),
            from_relative(grad_attn_low, rows_own).reshape(local_rows, seq_total, head_width),
        ],
        axis=2,
    )
    down_grad = to_row_owners(down_own)
    by_owner = after(jnp.transpose(by_owner, (1, 0, 2)), down_grad)
    got = lax.all_to_all(by_owner, "seq", 0, 0, tiled=True)
    got = got.reshape(length, 2 * head_width)
    grad_heads = got[:, :head_width]
    grad_attn_own = got[:, head_width:]
    gate_grad = to_row_owners(after(gate_own, got))

    grad_qkv = attention_back(grad_heads, attn_kept)
    qkv_own, qkv_sends = partial_sum_batch(act_one, grad_qkv)
    out_part = contract_rows(attn_all, grad_attn_own).astype(jnp.bfloat16)
    out_part = out_part.reshape(seq_total, batch_total, rows_own, head_width)
    out_part = [
        out_part[:, b].reshape(seq_total * rows_own, head_width) for b in range(batch_total)
    ]
    out_own = scatter_sum_batch(jnp.stack([of_offset(out_part, m) for m in range(batch_total)]))
    grad_qkv = after(grad_qkv, qkv_sends[0], out_own, gate_grad)
    grad_one_part = contract_cols(grad_qkv, qkv_full)
    gain_one_part = jnp.sum(grad_one_part * act_one.astype(jnp.float32), axis=0)
    gain_grad = jnp.stack([gain_one_part / gains_here[0], gain_two_grad])
    gain_grad = from_relative(gain_grad, rows_own)
    down_m, down_s, down_w = adam_by_owner(
        down_weight, down_first, down_second, down_grad, 1, rate_down
    )
    gate_m, gate_s, gate_w = adam_by_owner(
        gate_up_weight, gate_up_first, gate_up_second, gate_grad, 2, rate_gate
    )

    def last_transfer(arrived):
        both = jnp.concatenate([after(qkv_own, gate_grad, *arrived), out_own], axis=1)
        sums["rest"] = to_row_owners(both)
        return (gate_m,)

    grad_one = ring_scatter_one(
        after(grad_one_part.astype(jnp.bfloat16), gate_grad),
        ((qkv_sends[-1], down_m), last_transfer, (), lambda arrived: (sums["rest"],)),
    )
    qkv_grad = sums["rest"]
    gain_grad = sum_everywhere(after(gain_grad, qkv_grad))
    unit_one, scale_one = unit_rows(tokens_here.astype(jnp.float32))
    grad_in_norm = norm_back(grad_one, unit_one, scale_one, gains_here[0])[0]
    input_grad = from_relative(grad_middle + grad_in_norm, rows_own)
    qkv_m, qkv_s, qkv_w = adam_by_owner(
        qkv_weight, qkv_first, qkv_second, qkv_grad, 3, rate_qkv
    )
    out_m, out_s, out_w = adam_by_owner(
        out_weight, out_first, out_second, qkv_grad, 1, rate_out, skipped=3
    )
    gain_m, gain_s, gain_w = adam_update(gains, gain_first, gain_second, gain_grad, rate_gain)
    return (
        block_out[None],
        input_grad[None],
        qkv_m,
        qkv_s,
        qkv_w,
        out_m,
        out_s,
        out_w,
        gate_m,
        gate_s,
        gate_w,
        down_m,
        down_s,
        down_w,
        gain_m,
        gain_s,
        gain_w,
    )


def solution(mesh):
    rows = P(("seq", "batch"), None)
    blocks = P("batch", "seq", None)
    return jax.shard_map(
        on_device,
        mesh=mesh,
        in_specs=(blocks, blocks, P("batch", None)) + (rows,) * 12 + (P(),) * 3,
        out_specs=(blocks, blocks) + (rows,) * 12 + (P(),) * 3,
        check_vma=False,
    )
```

```python
import jax
import jax.numpy as jnp
from jax import lax
from jax.experimental import pallas as pl
from jax.experimental.pallas import tpu as pltpu
from jax.sharding import PartitionSpec as P

HD = 64
STEP = 10
LANES = 128
QUERY_ROWS = 256


norm_eps = 1e-05
rope_base = 130000.0
beta_one = 0.9
beta_two = 0.95
adam_eps = 1e-08
weight_decay = 0.1
masked_score = -1e30
rate_qkv = 0.05
rate_out = 0.5
rate_gate = 0.05
rate_down = 0.03
rate_gain = 0.3


def rotate_half(values):
    middle = values.shape[-1] // 2
    return jnp.concatenate([-values[..., middle:], values[..., :middle]], axis=-1)


def rope_tables(positions):
    inverse = rope_base ** (-jnp.arange(0, HD, 2, dtype=jnp.float32) / HD)
    angles = positions.astype(jnp.float32)[:, None] * inverse[None, :]
    angles = jnp.concatenate([angles, angles], axis=1)
    return (jnp.cos(angles), jnp.sin(angles))


def apply_rope(values, cos_table, sin_table):
    return values * cos_table + rotate_half(values) * sin_table


def undo_rope(values, cos_table, sin_table):
    return values * cos_table - rotate_half(values) * sin_table


def unit_rows(values):
    scale_rows = lax.rsqrt(jnp.mean(values * values, axis=-1, keepdims=True) + norm_eps)
    return (values * scale_rows, scale_rows)


def norm_back(grad_normed, unit_values, scale_rows, gain_row):
    grad_unit = grad_normed * gain_row
    gain_part = jnp.sum(grad_normed * unit_values, axis=0)
    grad_values = scale_rows * (
        grad_unit - unit_values * jnp.mean(grad_unit * unit_values, axis=-1, keepdims=True)
    )
    return (grad_values, gain_part)


def contract_rows(left_side, right_side):
    return lax.dot_general(
        left_side, right_side, (((0,), (0,)), ((), ())), preferred_element_type=jnp.float32
    )


def contract_cols(left_side, right_side):
    return lax.dot_general(
        left_side, right_side, (((1,), (1,)), ((), ())), preferred_element_type=jnp.float32
    )


def matmul(left_side, right_side):
    return jnp.dot(left_side, right_side, preferred_element_type=jnp.float32)


def adam_update(weight, first_moment, second, gradient, step_rate):
    first_new = beta_one * first_moment + (1.0 - beta_one) * gradient
    second_new = beta_two * second + (1.0 - beta_two) * gradient * gradient
    first_hat = first_new / (1.0 - beta_one**STEP)
    second_hat = second_new / (1.0 - beta_two**STEP)
    weight_new = weight - step_rate * (
        first_hat / (jnp.sqrt(second_hat) + adam_eps) + weight_decay * weight
    )
    return (first_new, second_new, weight_new)


def swapped(value, axis, bit):
    count = lax.axis_size(axis)
    return lax.ppermute(value, axis, [(source, source ^ bit) for source in range(count)])


def ring_order(count):
    return list(range(0, count, 2)) + list(range(count - 1, 0, -2))


def ring_shift(value, steps):
    count = lax.axis_size("seq")
    order = ring_order(count)
    pairs = [(order[i], order[(i + steps) % count]) for i in range(count)]
    return lax.ppermute(value, "seq", pairs)


def ring_place(offset):
    count = lax.axis_size("seq")
    own = lax.axis_index("seq")
    standing = jnp.where(own % 2 == 0, own // 2, count - 1 - own // 2)
    there = (standing + offset + count) % count
    return jnp.where(there < count // 2, 2 * there, 2 * (count - 1 - there) + 1)


def filled(arrays, filler):
    return filler(arrays) if callable(filler) else after_all(arrays, filler)


def ring_gather(parts, fillers=()):
    count = lax.axis_size("seq")
    far = count // 2
    packed = jnp.concatenate(parts, axis=1) if len(parts) > 1 else parts[0]
    middle = packed.shape[1] // 2
    blocks = {0: packed}
    ahead = behind = packed
    for step in range(1, far):
        if 0 <= step - 2 < len(fillers):
            ahead, behind = filled((ahead, behind), fillers[step - 2])
        ahead, behind = ring_shift(ahead, 1), ring_shift(behind, -1)
        blocks[-step], blocks[step] = ahead, behind
    if far - 2 < len(fillers):
        ahead, behind = filled((ahead, behind), fillers[far - 2])
    left, right = ring_shift(ahead[:, :middle], 1), ring_shift(behind[:, middle:], -1)
    blocks[far] = jnp.concatenate([left, right], axis=1)
    gathered = []
    first = 0
    for part in parts:
        last = first + part.shape[1]
        gathered.append({offset: block[:, first:last] for offset, block in blocks.items()})
        first = last
    return gathered


def with_rows(block, rows):
    if block.shape[0] >= rows:
        return jnp.concatenate(jnp.split(block, block.shape[0] // rows, axis=0), axis=1)
    return jnp.concatenate(jnp.split(block, rows // block.shape[0], axis=1), axis=0)


def stacked_rows(blocks):
    rows, width = blocks[0].shape
    whole = jnp.zeros((len(blocks) * rows, width), blocks[0].dtype)
    for offset, block in blocks.items():
        whole = lax.dynamic_update_slice(whole, block, (ring_place(offset) * rows, 0))
    return whole


def stacked_columns(blocks):
    rows, width = blocks[0].shape
    whole = jnp.zeros((rows, len(blocks) * width), blocks[0].dtype)
    for offset, block in blocks.items():
        whole = lax.dynamic_update_slice(whole, block, (0, ring_place(offset) * width))
    return whole


def ring_rows(whole, offsets):
    rows = whole.shape[0] // lax.axis_size("seq")
    return jnp.concatenate(
        [lax.dynamic_slice_in_dim(whole, ring_place(o) * rows, rows, 0) for o in offsets], axis=0
    )


def added(block, got):
    return (block.astype(jnp.float32) + got.astype(jnp.float32)).astype(block.dtype)


def ring_scatter_sum(blocks, fillers=()):
    far = lax.axis_size("seq") // 2
    middle = blocks[0].shape[1] // 2
    ahead = ring_shift(blocks[far][:, :middle], 1)
    behind = ring_shift(blocks[far][:, middle:], -1)
    for turn, step in enumerate(range(far - 1, 0, -1)):
        onward, backward = blocks[step], blocks[-step]
        if turn == 0:
            onward = jnp.concatenate([added(onward[:, :middle], ahead), onward[:, middle:]], axis=1)
            backward = jnp.concatenate(
                [backward[:, :middle], added(backward[:, middle:], behind)], axis=1
            )
        else:
            onward, backward = added(onward, ahead), added(backward, behind)
        if turn < len(fillers):
            onward, backward = filled([onward, backward], fillers[turn])
        ahead, behind = ring_shift(onward, 1), ring_shift(backward, -1)
    if far - 1 < len(fillers):
        ahead, behind = filled([ahead, behind], fillers[far - 1])
    return blocks[0].astype(jnp.float32) + ahead.astype(jnp.float32) + behind.astype(jnp.float32)


def ring_blocks(wholes):
    far = lax.axis_size("seq") // 2
    offsets = [far] + [sign * step for step in range(far - 1, 0, -1) for sign in (1, -1)] + [0]
    return {
        offset: jnp.concatenate([ring_rows(whole, [offset]) for whole in wholes], axis=1)
        for offset in offsets
    }


def butterfly_steps():
    steps = []
    for axis in ("batch", "seq"):
        bit = 1
        while bit < lax.axis_size(axis):
            steps.append((axis, bit))
            bit *= 2
    return steps


def after(value, *others):
    return lax.optimization_barrier((value,) + others)[0]


def after_all(values, others):
    return lax.optimization_barrier(tuple(values) + tuple(others))[: len(values)]


def batch_bits():
    count = lax.axis_size("batch")
    bits = []
    while (1 << len(bits)) < count:
        bits.append(1 << len(bits))
    return bits


def of_offset(choices, offset):
    index = lax.axis_index("batch")
    picked = choices[offset]
    for own in range(1, len(choices)):
        picked = jnp.where(index == own, choices[own ^ offset], picked)
    return picked


def offset_order():
    order = [0]
    for bit in reversed(batch_bits()):
        order = order + [offset ^ bit for offset in order]
    return order


def batch_columns(rows, rows_own):
    count, width = rows.shape
    batch_total = lax.axis_size("batch")
    blocks = rows.reshape(count, -1, batch_total, rows_own)
    return [blocks[:, :, b].reshape(count, width // batch_total) for b in range(batch_total)]


def to_relative(rows, rows_own):
    columns = batch_columns(rows, rows_own)
    return jnp.concatenate([of_offset(columns, m) for m in offset_order()], axis=1)


def from_relative(rows, rows_own):
    count, width = rows.shape
    batch_total = lax.axis_size("batch")
    order = offset_order()
    part = width // batch_total
    columns = [
        rows[:, order.index(m) * part : (order.index(m) + 1) * part] for m in range(batch_total)
    ]
    blocks = [
        of_offset(columns, b).reshape(count, width // (batch_total * rows_own), rows_own)
        for b in range(batch_total)
    ]
    return jnp.stack(blocks, axis=2).reshape(count, width)


def gather_pieces(block):
    pieces = [block]
    for bit in reversed(batch_bits()):
        pieces = pieces + [swapped(piece, "batch", bit) for piece in pieces]
    return pieces


def gather_batch(block):
    return jnp.concatenate(gather_pieces(block), axis=0)


def partial_sum_batch(left, right):
    width = left.shape[1]
    held = None
    sends = []

    def product(first, last):
        part = contract_rows(left[:, first:last], right)
        return part if held is None else part + held[first:last]

    for bit in batch_bits():
        half = width // 2
        sends.append(product(half, width).astype(jnp.bfloat16))
        got = swapped(sends[-1], "batch", bit).astype(jnp.float32)
        held = got if held is None else held[:half] + got
        width = half
    return (product(0, width).astype(jnp.bfloat16), sends)


def scatter_sum_batch(blocks):
    held = blocks
    for bit in batch_bits():
        pairs = held.reshape((held.shape[0] // 2, 2) + held.shape[1:])
        got = swapped(pairs[:, 1], "batch", bit)
        held = (pairs[:, 0].astype(jnp.float32) + got.astype(jnp.float32)).astype(jnp.bfloat16)
    return held[0]


def seqs_in_block(columns, seq_total):
    return max(1, min(seq_total, 1024 // columns))


def rounded_by_owner(weight, groups):
    rows_own, width = weight.shape
    seq_total = lax.axis_size("seq")
    columns = width // (groups * seq_total)
    if columns % LANES:
        blocks = weight.astype(jnp.bfloat16).reshape(rows_own, groups, seq_total, columns)
        return jnp.transpose(blocks, (2, 0, 1, 3)).reshape(seq_total, rows_own, groups * columns)
    taken = seqs_in_block(columns, seq_total)
    steps = seq_total // taken

    def kernel(weight_ref, out_ref):
        for place in range(taken):
            out_ref[place] = weight_ref[:, place * columns : (place + 1) * columns].astype(
                jnp.bfloat16
            )

    return pl.pallas_call(
        kernel,
        grid=(groups, steps),
        in_specs=[pl.BlockSpec((rows_own, taken * columns), lambda g, j: (0, g * steps + j))],
        out_specs=pl.BlockSpec((taken, rows_own, columns), lambda g, j: (j, 0, g)),
        out_shape=jax.ShapeDtypeStruct(
            (seq_total, rows_own, groups * columns), jnp.bfloat16
        ),
        cost_estimate=pl.CostEstimate(flops=0, bytes_accessed=weight.size * 6, transcendentals=0),
    )(weight)


def to_column_owners(blocks):
    got = lax.all_to_all(blocks, "seq", 0, 0, tiled=True)
    return got.reshape(-1, blocks.shape[2])


def to_row_owners(grad):
    seq_total = lax.axis_size("seq")
    blocks = grad.reshape(seq_total, grad.shape[0] // seq_total, grad.shape[1])
    return lax.all_to_all(blocks, "seq", 0, 0, tiled=True)


def adam_by_owner(weight, first_moment, second, gradient, groups, step_rate, skipped=0):
    rows_own, width = weight.shape
    seq_total = lax.axis_size("seq")
    columns = width // (groups * seq_total)
    if columns % LANES:
        own = gradient[:, :, skipped * columns : (skipped + groups) * columns]
        natural = jnp.transpose(
            own.reshape(seq_total, rows_own, groups, columns), (1, 2, 0, 3)
        ).reshape(rows_own, width)
        return adam_update(weight, first_moment, second, natural.astype(jnp.float32), step_rate)
    taken = seqs_in_block(columns, seq_total)
    steps = seq_total // taken

    def kernel(weight_ref, first_ref, second_ref, gradient_ref, *out_refs):
        for place in range(taken):
            here = slice(place * columns, (place + 1) * columns)
            results = adam_update(
                weight_ref[:, here],
                first_ref[:, here],
                second_ref[:, here],
                gradient_ref[place].astype(jnp.float32),
                step_rate,
            )
            for out_ref, result in zip(out_refs, results):
                out_ref[:, here] = result

    whole = pl.BlockSpec((rows_own, taken * columns), lambda g, j: (0, g * steps + j))
    return pl.pallas_call(
        kernel,
        grid=(groups, steps),
        in_specs=[whole] * 3 + [
            pl.BlockSpec((taken, rows_own, columns), lambda g, j: (j, 0, g + skipped))
        ],
        out_specs=[whole] * 3,
        out_shape=[jax.ShapeDtypeStruct(weight.shape, jnp.float32)] * 3,
        cost_estimate=pl.CostEstimate(
            flops=weight.size * 15, bytes_accessed=weight.size * 26, transcendentals=weight.size
        ),
    )(weight, first_moment, second, gradient)


def swap_halves(values):
    lane = lax.broadcasted_iota(jnp.int32, values.shape, 1)
    return jnp.where(
        lane % HD < HD // 2,
        pltpu.roll(values, LANES - HD // 2, 1),
        pltpu.roll(values, HD // 2, 1),
    )


def of_head(values, head, axis=1):
    lane = lax.broadcasted_iota(jnp.int32, values.shape, axis)
    return jnp.where(lane // HD == head, values, jnp.zeros_like(values))


def allowed_here(starts_ref, first, rows):
    shape = (rows, QUERY_ROWS)
    key = lax.broadcasted_iota(jnp.int32, shape, 0)
    query = lax.broadcasted_iota(jnp.int32, shape, 1) + first
    return (key <= query) & (key >= starts_ref[:, first : first + QUERY_ROWS])


def mm_last(left, right):
    return lax.dot_general(
        left, right, (((1,), (1,)), ((), ())), preferred_element_type=jnp.float32
    )


def attend_kernel(
    query_in, key_in, value_in, cos_ref, sin_ref, starts_ref,
    out_ref, low_ref, query_ref, key_ref, value_ref, total_ref, key_own, value_turned,
):
    length = query_in.shape[0]
    cos, sin = cos_ref[...], sin_ref[...]
    raw_query, raw_key = query_in[...], key_in[...]
    query_ref[...] = (raw_query * cos + swap_halves(raw_query) * sin).astype(jnp.bfloat16) * HD**-0.5
    key_ref[...] = (raw_key * cos + swap_halves(raw_key) * sin).astype(jnp.bfloat16)
    value_ref[...] = value_in[...].astype(jnp.bfloat16)
    turned = value_in[...].T
    for head in range(2):
        key_own[head] = of_head(key_ref[...], head)
        value_turned[head] = of_head(turned, head, 0).astype(jnp.bfloat16)
    for first in range(0, length, QUERY_ROWS):
        last = first + QUERY_ROWS
        allowed = allowed_here(starts_ref, first, last)
        weighted = jnp.zeros((LANES, QUERY_ROWS), jnp.float32)
        for head in range(2):
            scores = mm_last(key_own[head, :last], query_ref[first:last])
            scores = jnp.where(allowed, scores, masked_score)
            top = jnp.max(scores, axis=0, keepdims=True)
            powers = jnp.exp(scores - top)
            total = jnp.sum(powers, axis=0, keepdims=True)
            probs = (powers * (1.0 / total)).astype(jnp.bfloat16)
            weighted += matmul(value_turned[head, :, :last], probs)
            total_ref[0, head : head + 1, first:last] = top + jnp.log(total)
        attended = weighted.T
        out_ref[first:last] = attended
        low_ref[first:last] = attended.astype(jnp.bfloat16)


def attend_back_kernel(
    query_ref, key_ref, value_ref, grad_ref, attended_ref, total_ref, cos_ref, sin_ref, starts_ref,
    out_ref, key_own, value_own, key_turned, key_grad, value_grad,
):
    length = query_ref.shape[0]
    pair = pl.program_id(0)
    width = out_ref.shape[1] // 3
    turned = key_ref[...].astype(jnp.float32).T
    for head in range(2):
        key_own[head] = of_head(key_ref[...], head)
        value_own[head] = of_head(value_ref[...], head)
        key_turned[head] = of_head(turned, head, 0).astype(jnp.bfloat16)
    key_grad[...] = jnp.zeros_like(key_grad)
    value_grad[...] = jnp.zeros_like(value_grad)

    def undone(values, rows):
        back = values * cos_ref[rows] - swap_halves(values) * sin_ref[rows]
        return back.astype(jnp.bfloat16)

    def lanes(group):
        return pl.ds(pl.multiple_of(group * width + pair * LANES, LANES), LANES)

    for first in range(0, length, QUERY_ROWS):
        last = first + QUERY_ROWS
        rows = slice(first, last)
        allowed = allowed_here(starts_ref, first, last)
        grad, query = grad_ref[rows], query_ref[rows]
        products = (grad.astype(jnp.float32) * attended_ref[rows]).T
        query_grad = jnp.zeros((LANES, QUERY_ROWS), jnp.float32)
        for head in range(2):
            scores = mm_last(key_own[head, :last], query)
            probs = jnp.where(allowed, jnp.exp(scores - total_ref[0, head : head + 1, rows]), 0.0)
            delta = jnp.sum(products[head * HD : (head + 1) * HD], axis=0, keepdims=True)
            grad_probs = mm_last(value_own[head, :last], grad)
            grad_scores = (probs * (grad_probs - delta)).astype(jnp.bfloat16)
            value_grad[:last] += matmul(probs.astype(jnp.bfloat16), of_head(grad, head))
            key_grad[:last] += matmul(grad_scores, of_head(query, head))
            query_grad += matmul(key_turned[head, :, :last], grad_scores)
        out_ref[rows, lanes(0)] = undone(query_grad.T * HD**-0.5, rows)
    everything = slice(0, length)
    out_ref[:, lanes(1)] = undone(key_grad[...], everything)
    out_ref[:, lanes(2)] = value_grad[...].astype(jnp.bfloat16)


def project_kernel(total, attended_ref, inputs_ref, gain_ref, *refs):
    weight_refs, (middle_ref, unit_ref) = refs[:total], refs[total:]
    width = inputs_ref.shape[1]
    part = width // total
    attended = attended_ref[...]
    squares = 0.0
    for place, weight_ref in enumerate(weight_refs):
        columns = slice(place * part, (place + 1) * part)
        block = inputs_ref[:, columns].astype(jnp.float32) + matmul(attended, weight_ref[...])
        middle_ref[:, columns] = block
        squares += jnp.sum(block * block, axis=1, keepdims=True)
    scale = lax.rsqrt(squares / width + norm_eps)
    unit_ref[...] = (middle_ref[...] * scale * gain_ref[...]).astype(jnp.bfloat16)


def project_rows(attended, inputs, gain, pieces):
    length, width = inputs.shape
    total = len(pieces)
    rows = pl.BlockSpec((QUERY_ROWS, width), lambda i: (i, 0))
    return pl.pallas_call(
        lambda *refs: project_kernel(total, *refs),
        grid=(length // QUERY_ROWS,),
        in_specs=[rows, rows, pl.BlockSpec((1, width), lambda i: (0, 0))]
        + [pl.BlockSpec((width, width // total), lambda i: (0, 0))] * total,
        out_specs=[rows, rows],
        out_shape=[
            jax.ShapeDtypeStruct((length, width), jnp.float32),
            jax.ShapeDtypeStruct((length, width), jnp.bfloat16),
        ],
        compiler_params=pltpu.CompilerParams(vmem_limit_bytes=48 << 20),
        cost_estimate=pl.CostEstimate(
            flops=2 * length * width * width,
            bytes_accessed=10 * length * width + 2 * width * width,
            transcendentals=length,
        ),
    )(attended, inputs, gain, *pieces)


def summed_product(left_ref, weight_refs):
    part = left_ref.shape[1] // len(weight_refs)
    return sum(
        matmul(left_ref[:, place * part : (place + 1) * part], weight_ref[...])
        for place, weight_ref in enumerate(weight_refs)
    )


def hidden_kernel(total, rows_ref, *refs):
    gate_ref, up_ref, low_ref = refs[2 * total :]
    gate = summed_product(rows_ref, refs[:total])
    up = summed_product(rows_ref, refs[total : 2 * total])
    gate_ref[...] = gate
    up_ref[...] = up
    low_ref[...] = (gate * jax.nn.sigmoid(gate) * up).astype(jnp.bfloat16)


def hidden_units(rows, gate_pieces):
    length, width = rows.shape
    total = len(gate_pieces)
    hidden = gate_pieces[0].shape[1] // 2
    tile = min(hidden, 2 * LANES)
    steps = hidden // tile
    own = pl.BlockSpec((length, tile), lambda j: (0, j))
    wide = jax.ShapeDtypeStruct((length, hidden), jnp.float32)
    return pl.pallas_call(
        lambda *refs: hidden_kernel(total, *refs),
        grid=(steps,),
        in_specs=[pl.BlockSpec((length, width), lambda j: (0, 0))]
        + [pl.BlockSpec((width // total, tile), lambda j: (0, j))] * total
        + [pl.BlockSpec((width // total, tile), lambda j: (0, steps + j))] * total,
        out_specs=[own] * 3,
        out_shape=[wide, wide, jax.ShapeDtypeStruct((length, hidden), jnp.bfloat16)],
        compiler_params=pltpu.CompilerParams(vmem_limit_bytes=48 << 20),
        cost_estimate=pl.CostEstimate(
            flops=4 * length * width * hidden,
            bytes_accessed=2 * length * width + 4 * width * hidden + 10 * length * hidden,
            transcendentals=length * hidden,
        ),
    )(rows, *gate_pieces, *gate_pieces)


def hidden_back_kernel(total, grads_ref, gate_ref, up_ref, *refs):
    grad_ref = refs[total]
    tile = gate_ref.shape[1]
    hidden = grad_ref.shape[1] // 2
    grad = summed_product(grads_ref, refs[:total])
    gate, up = gate_ref[...], up_ref[...]
    sigmoid = jax.nn.sigmoid(gate)
    first = pl.multiple_of(pl.program_id(0) * tile, tile)
    grad_gate = grad * up * (sigmoid * (1.0 + gate * (1.0 - sigmoid)))
    grad_ref[:, pl.ds(first, tile)] = grad_gate.astype(jnp.bfloat16)
    second = pl.multiple_of(hidden + pl.program_id(0) * tile, tile)
    grad_ref[:, pl.ds(second, tile)] = (grad * (gate * sigmoid)).astype(jnp.bfloat16)


def hidden_back(grads, gate, up, down_pieces):
    length, width = grads.shape
    total = len(down_pieces)
    hidden = gate.shape[1]
    tile = min(hidden, 2 * LANES)
    own = pl.BlockSpec((length, tile), lambda j: (0, j))
    return pl.pallas_call(
        lambda *refs: hidden_back_kernel(total, *refs),
        grid=(hidden // tile,),
        in_specs=[pl.BlockSpec((length, width), lambda j: (0, 0)), own, own]
        + [pl.BlockSpec((width // total, tile), lambda j: (0, j))] * total,
        out_specs=pl.BlockSpec((length, 2 * hidden), lambda j: (0, 0)),
        out_shape=jax.ShapeDtypeStruct((length, 2 * hidden), jnp.bfloat16),
        compiler_params=pltpu.CompilerParams(vmem_limit_bytes=48 << 20),
        cost_estimate=pl.CostEstimate(
            flops=2 * length * width * hidden,
            bytes_accessed=2 * length * width + 2 * width * hidden + 12 * length * hidden,
            transcendentals=length * hidden,
        ),
    )(grads, gate, up, *down_pieces)


def back_kernel(total, left_ref, *refs):
    each = pl.num_programs(0) // total
    for place in range(total):

        @pl.when(pl.program_id(0) // each == place)
        def _():
            refs[total][...] = mm_last(left_ref[...], refs[place][...]).astype(jnp.bfloat16)


def back_to_model(left, pieces):
    length, inner = left.shape
    total = len(pieces)
    part = pieces[0].shape[0]
    tile = min(part, 2 * LANES)
    each = part // tile

    def rows_of(place):
        return pl.BlockSpec((tile, inner), lambda i: (jnp.clip(i - place * each, 0, each - 1), 0))

    return pl.pallas_call(
        lambda *refs: back_kernel(total, *refs),
        grid=(total * each,),
        in_specs=[pl.BlockSpec((length, inner), lambda i: (0, 0))]
        + [rows_of(place) for place in range(total)],
        out_specs=pl.BlockSpec((length, tile), lambda i: (0, i)),
        out_shape=jax.ShapeDtypeStruct((length, part * total), jnp.bfloat16),
        compiler_params=pltpu.CompilerParams(vmem_limit_bytes=48 << 20),
        cost_estimate=pl.CostEstimate(
            flops=2 * length * part * total * inner,
            bytes_accessed=2 * inner * (length + part * total) + 2 * length * part * total,
            transcendentals=0,
        ),
    )(left, *pieces)


def attend_forward(qkv, cos_table, sin_table, starts):
    length, width = qkv.shape[0], qkv.shape[1] // 3
    pairs = width // LANES
    whole = pl.BlockSpec((length, LANES), lambda p: (0, 0))
    own = pl.BlockSpec((length, LANES), lambda p: (0, p))
    low = jax.ShapeDtypeStruct((length, width), jnp.bfloat16)
    work = pairs * length * length
    return pl.pallas_call(
        attend_kernel,
        grid=(pairs,),
        in_specs=[
            own,
            pl.BlockSpec((length, LANES), lambda p: (0, pairs + p)),
            pl.BlockSpec((length, LANES), lambda p: (0, 2 * pairs + p)),
            whole,
            whole,
            pl.BlockSpec((1, length), lambda p: (0, 0)),
        ],
        out_specs=[own] * 5 + [pl.BlockSpec((1, 2, length), lambda p: (p, 0, 0))],
        out_shape=[
            jax.ShapeDtypeStruct((length, width), jnp.float32),
            low,
            low,
            low,
            low,
            jax.ShapeDtypeStruct((pairs, 2, length), jnp.float32),
        ],
        scratch_shapes=[
            pltpu.VMEM((2, length, LANES), jnp.bfloat16),
            pltpu.VMEM((2, LANES, length), jnp.bfloat16),
        ],
        compiler_params=pltpu.CompilerParams(vmem_limit_bytes=48 << 20),
        cost_estimate=pl.CostEstimate(
            flops=8 * work * LANES, bytes_accessed=qkv.size * 8, transcendentals=2 * work
        ),
    )(qkv, qkv, qkv, cos_table, sin_table, starts)


def attend_backward(query, key, value, grad, attended, total, cos_table, sin_table, starts):
    length, width = query.shape
    pairs = width // LANES
    whole = pl.BlockSpec((length, LANES), lambda p: (0, 0))
    own = pl.BlockSpec((length, LANES), lambda p: (0, p))
    work = pairs * length * length
    return pl.pallas_call(
        attend_back_kernel,
        grid=(pairs,),
        in_specs=[own] * 5
        + [
            pl.BlockSpec((1, 2, length), lambda p: (p, 0, 0)),
            whole,
            whole,
            pl.BlockSpec((1, length), lambda p: (0, 0)),
        ],
        out_specs=pl.BlockSpec((length, 3 * width), lambda p: (0, 0)),
        out_shape=jax.ShapeDtypeStruct((length, 3 * width), jnp.bfloat16),
        scratch_shapes=[
            pltpu.VMEM((2, length, LANES), jnp.bfloat16),
            pltpu.VMEM((2, length, LANES), jnp.bfloat16),
            pltpu.VMEM((2, LANES, length), jnp.bfloat16),
            pltpu.VMEM((length, LANES), jnp.float32),
            pltpu.VMEM((length, LANES), jnp.float32),
        ],
        compiler_params=pltpu.CompilerParams(vmem_limit_bytes=48 << 20),
        cost_estimate=pl.CostEstimate(
            flops=work * LANES, bytes_accessed=query.size * 4, transcendentals=work // 16
        ),
    )(query, key, value, grad, attended, total, cos_table, sin_table, starts)


def on_device(
    tokens,
    out_grad,
    doc_lengths,
    qkv_weight,
    qkv_first,
    qkv_second,
    out_weight,
    out_first,
    out_second,
    gate_up_weight,
    gate_up_first,
    gate_up_second,
    down_weight,
    down_first,
    down_second,
    gains,
    gain_first,
    gain_second,
):
    local_rows = tokens.shape[1]
    model_width = tokens.shape[2]
    rows_own = qkv_weight.shape[0]
    seq_total = lax.axis_size("seq")
    batch_total = lax.axis_size("batch")
    head_width = model_width // seq_total
    heads = head_width // HD
    length = local_rows * seq_total
    hidden = down_weight.shape[1] // seq_total
    score_scale = HD ** (-0.5)
    positions = jnp.arange(length, dtype=jnp.int32)
    ends = jnp.cumsum(doc_lengths[0])
    starts = jnp.max(jnp.where(positions[:, None] >= ends[None, :], ends[None, :], 0), axis=1)
    cos_table, sin_table = rope_tables(positions)
    in_pairs = head_width % LANES == 0 and length % QUERY_ROWS == 0
    if in_pairs:
        sign = jnp.where(jnp.arange(HD) < HD // 2, -1.0, 1.0)
        cos_pair = jnp.tile(cos_table, (1, 2))
        sin_pair = jnp.tile(sin_table * sign, (1, 2))

    def split_heads(columns):
        return jnp.transpose(columns.reshape(length, heads, HD), (1, 0, 2))

    def join_heads(values):
        return jnp.transpose(values, (1, 0, 2)).reshape(length, head_width)

    def allowed_pairs():
        return (
            (positions[None, :] <= positions[:, None]) & (positions[None, :] >= starts[:, None])
        )[None]

    def attention(qkv):
        if in_pairs:
            attended, low, *kept = attend_forward(qkv, cos_pair, sin_pair, starts[None])
            return (low, (attended, kept))
        query = split_heads(qkv[:, :head_width])
        query = apply_rope(query, cos_table, sin_table).astype(jnp.bfloat16)
        key = split_heads(qkv[:, head_width : 2 * head_width])
        key = apply_rope(key, cos_table, sin_table).astype(jnp.bfloat16)
        value = split_heads(qkv[:, 2 * head_width :]).astype(jnp.bfloat16)
        scores = jnp.einsum("hqd,hkd->hqk", query, key, preferred_element_type=jnp.float32)
        scores = jnp.where(allowed_pairs(), scores * score_scale, masked_score)
        probs = jax.nn.softmax(scores, axis=-1)
        attended = jnp.einsum(
            "hqk,hkd->hqd", probs.astype(jnp.bfloat16), value, preferred_element_type=jnp.float32
        )
        return (join_heads(attended.astype(jnp.bfloat16)), (attended, (query, key, value, probs)))

    def attention_back(grad, kept):
        if in_pairs:
            attended, (query, key, value, total) = kept
            return attend_backward(
                query, key, value, grad, attended, total, cos_pair, sin_pair, starts[None]
            )
        attended, (query, key, value, probs) = kept
        grad = split_heads(grad)
        delta = jnp.sum(grad.astype(jnp.float32) * attended, axis=-1, keepdims=True)
        grad_probs = jnp.einsum("hqd,hkd->hqk", grad, value, preferred_element_type=jnp.float32)
        grad_scores = (probs * (grad_probs - delta)).astype(jnp.bfloat16)

        def over_queries(left, right):
            return jnp.einsum("hqk,hqd->hkd", left, right, preferred_element_type=jnp.float32)

        grad_value = over_queries(probs.astype(jnp.bfloat16), grad)
        grad_key = over_queries(grad_scores, query) * score_scale
        grad_query = (
            jnp.einsum("hqk,hkd->hqd", grad_scores, key, preferred_element_type=jnp.float32)
            * score_scale
        )
        return jnp.concatenate(
            [
                join_heads(undo_rope(grad_query, cos_table, sin_table)),
                join_heads(undo_rope(grad_key, cos_table, sin_table)),
                join_heads(grad_value),
            ],
            axis=1,
        ).astype(jnp.bfloat16)

    first_row = lax.axis_index("seq") * local_rows
    gains_here = to_relative(gains, rows_own)
    tokens_here = to_relative(tokens[0], rows_own)
    grads_here = to_relative(out_grad[0], rows_own)
    qkv_low = rounded_by_owner(qkv_weight, 3)
    out_columns = batch_columns(after(out_weight, qkv_low).astype(jnp.bfloat16), rows_own)
    out_here = [
        swapped(of_offset(out_columns, m), "batch", m) if m else of_offset(out_columns, m)
        for m in range(batch_total)
    ]
    out_here = [of_offset(out_here, b) for b in range(batch_total)]
    out_here = with_rows(jnp.concatenate(out_here, axis=0), local_rows)
    gate_low = rounded_by_owner(gate_up_weight, 2)
    down_low = rounded_by_owner(down_weight, 1)
    qkv_block = to_column_owners(qkv_low)
    tokens_all, out_all = ring_gather(
        [after(tokens_here, qkv_low), out_here], ((qkv_block,), (gate_low, down_low))
    )
    tokens_all = stacked_rows(tokens_all)
    out_all = stacked_rows(
        {offset: with_rows(block, head_width) for offset, block in out_all.items()}
    )
    qkv_full = gather_batch(qkv_block)
    gate_block = to_column_owners(after(gate_low, tokens_all))
    inputs = tokens_all.astype(jnp.float32)
    act_one = (unit_rows(inputs)[0] * gains_here[0]).astype(jnp.bfloat16)
    qkv = matmul(act_one, qkv_full)
    attn_own, attn_kept = attention(qkv)

    out_pieces = gather_pieces(out_all)
    out_full = jnp.concatenate(out_pieces, axis=1)

    gate_block = after(gate_block, attn_own)
    attn_own_late = after(attn_own, gate_block)
    attn_all = stacked_columns(ring_gather([attn_own_late])[0])
    down_block = to_column_owners(after(down_low, attn_all))
    gate_pieces, down_pieces = gather_pieces(gate_block), gather_pieces(down_block)
    grads_here_late = after(grads_here, down_block)
    if in_pairs and length * model_width <= 1 << 21:
        middle_all, act_two = project_rows(attn_all, tokens_all, gains_here[1:], out_pieces)
        gate_part, up_part, hidden_low = hidden_units(act_two, gate_pieces)
        late = {}

        def block_meanwhile(moved):
            *moved, low = lax.optimization_barrier((*moved, hidden_low))
            late["block"] = back_to_model(low, down_pieces)
            return moved

        grads_all = ring_gather(
            [grads_here_late],
            ((hidden_low,), block_meanwhile, lambda moved: after_all(moved, (late["block"],))),
        )
        grads_all, block_part = stacked_rows(grads_all[0]), late["block"]
        grad_gate_up = hidden_back(grads_all, gate_part, up_part, down_pieces)
        grad_two = back_to_model(grad_gate_up, gate_pieces)
    else:
        grads_all = stacked_rows(ring_gather([grads_here_late])[0])
        middle_all = inputs + matmul(attn_all, out_full)
        act_two = (unit_rows(middle_all)[0] * gains_here[1]).astype(jnp.bfloat16)
        gate_full, down_full = jnp.concatenate(gate_pieces), jnp.concatenate(down_pieces)
        gate_up = matmul(act_two, gate_full)
        gate_part, up_part = gate_up[:, :hidden], gate_up[:, hidden:]
        sigmoid_gate = jax.nn.sigmoid(gate_part)
        silu_gate = gate_part * sigmoid_gate
        hidden_low = (silu_gate * up_part).astype(jnp.bfloat16)
        grad_hidden = matmul(grads_all, down_full)
        grad_gate = (
            grad_hidden * up_part * (sigmoid_gate * (1.0 + gate_part * (1.0 - sigmoid_gate)))
        )
        grad_gate_up = jnp.concatenate([grad_gate, grad_hidden * silu_gate], axis=1)
        grad_gate_up = grad_gate_up.astype(jnp.bfloat16)
        grad_two = contract_cols(grad_gate_up, gate_full).astype(jnp.bfloat16)
        block_part = contract_cols(hidden_low, down_full).astype(jnp.bfloat16)

    sums = {}

    def weight_sums(moved):
        *moved, low, grad = lax.optimization_barrier((*moved, hidden_low, grad_gate_up))
        sums["down"] = partial_sum_batch(grads_all, low)
        sums["gate"] = partial_sum_batch(act_two, grad)
        return moved

    def sent(stage):
        return lambda moved: after_all(moved, (sums["down"][1][stage], sums["gate"][1][stage]))

    summed = ring_scatter_sum(
        ring_blocks([grad_two, block_part]), (weight_sums, sent(0), sent(-1))
    )
    grad_two, block_rest = summed[:, :model_width], summed[:, model_width:]
    down_own, gate_own = sums["down"][0], sums["gate"][0]

    def own_rows(whole):
        return lax.dynamic_slice_in_dim(whole, first_row, local_rows, 0)

    middle = own_rows(middle_all)
    unit_two, scale_two = unit_rows(middle)
    block_out = from_relative((middle + block_rest).astype(jnp.bfloat16), rows_own)
    grad_mid_norm, gain_two_grad = norm_back(grad_two, unit_two, scale_two, gains_here[1])
    grad_middle = grads_here.astype(jnp.float32) + grad_mid_norm
    grad_attn_low = grad_middle.astype(jnp.bfloat16)
    grad_heads = contract_cols(grad_attn_low, out_full).astype(jnp.bfloat16)
    by_owner = jnp.concatenate(
        [
            grad_heads.reshape(local_rows, seq_total, head_width),
            from_relative(grad_attn_low, rows_own).reshape(local_rows, seq_total, head_width),
        ],
        axis=2,
    )
    down_grad = to_row_owners(down_own)
    by_owner = after(jnp.transpose(by_owner, (1, 0, 2)), down_grad)
    got = lax.all_to_all(by_owner, "seq", 0, 0, tiled=True)
    got = got.reshape(length, 2 * head_width)
    grad_heads = got[:, :head_width]
    grad_attn_own = got[:, head_width:]
    gate_grad = to_row_owners(after(gate_own, got))

    grad_qkv = attention_back(grad_heads, attn_kept)
    qkv_own, qkv_sends = partial_sum_batch(act_one, grad_qkv)
    out_part = contract_rows(attn_all, grad_attn_own).astype(jnp.bfloat16)
    out_part = out_part.reshape(seq_total, batch_total, rows_own, head_width)
    out_part = [
        out_part[:, b].reshape(seq_total * rows_own, head_width) for b in range(batch_total)
    ]
    out_own = scatter_sum_batch(jnp.stack([of_offset(out_part, m) for m in range(batch_total)]))
    grad_qkv = after(grad_qkv, qkv_sends[0], out_own, gate_grad)
    grad_one_part = contract_cols(grad_qkv, qkv_full)
    gain_one_part = jnp.sum(grad_one_part * act_one.astype(jnp.float32), axis=0)
    gain_grad = jnp.stack([gain_one_part / gains_here[0], gain_two_grad])
    gain_grad = from_relative(gain_grad, rows_own)
    down_m, down_s, down_w = adam_by_owner(
        down_weight, down_first, down_second, down_grad, 1, rate_down
    )
    steps = butterfly_steps()

    def next_gain_sum():
        if steps:
            axis, bit = steps.pop(0)
            sums["gain"] = sums["gain"] + swapped(sums["gain"], axis, bit)

    def tied(moved, *names):
        moved = lax.optimization_barrier((*moved, *(sums[name] for name in names)))
        for name, value in zip(names, moved[len(moved) - len(names) :]):
            sums[name] = value
        next_gain_sum()
        return moved[: len(moved) - len(names)]

    def gate_update(moved):
        moved = tied(moved, "gain", "gate_grad")
        sums["gate_new"] = adam_by_owner(
            gate_up_weight, gate_up_first, gate_up_second, sums["gate_grad"], 2, rate_gate
        )
        return moved

    def last_transfer(moved):
        moved = tied(after_all(moved, (sums["gate_new"][0],)), "gain")
        return moved

    def last_updates(moved):
        sums["qkv"] = adam_by_owner(
            qkv_weight, qkv_first, qkv_second, sums["rest"], 3, rate_qkv
        )
        sums["out"] = adam_by_owner(
            out_weight, out_first, out_second, sums["rest"], 1, rate_out, skipped=3
        )
        return tied(after_all(moved, (sums["qkv"][0], sums["out"][0])), "gain")

    sums["gain"], sums["gate_grad"] = gain_grad, gate_grad
    next_gain_sum()
    sums["rest"] = to_row_owners(jnp.concatenate([after(qkv_own, gate_grad), out_own], axis=1))
    grad_one = ring_scatter_sum(
        ring_blocks([after(grad_one_part.astype(jnp.bfloat16), qkv_sends[-1], down_m)]),
        (gate_update, last_transfer, lambda moved: tied(moved, "gain"), last_updates),
    )
    while steps:
        next_gain_sum()
    gain_grad = sums["gain"]
    (qkv_m, qkv_s, qkv_w), (out_m, out_s, out_w) = sums["qkv"], sums["out"]
    gate_m, gate_s, gate_w = sums["gate_new"]
    unit_one, scale_one = unit_rows(tokens_here.astype(jnp.float32))
    grad_in_norm = norm_back(grad_one, unit_one, scale_one, gains_here[0])[0]
    input_grad = from_relative(grad_middle + grad_in_norm, rows_own)
    gain_m, gain_s, gain_w = adam_update(gains, gain_first, gain_second, gain_grad, rate_gain)
    return (
        block_out[None],
        input_grad[None],
        qkv_m,
        qkv_s,
        qkv_w,
        out_m,
        out_s,
        out_w,
        gate_m,
        gate_s,
        gate_w,
        down_m,
        down_s,
        down_w,
        gain_m,
        gain_s,
        gain_w,
    )


def solution(mesh):
    rows = P(("seq", "batch"), None)
    blocks = P("batch", "seq", None)
    return jax.shard_map(
        on_device,
        mesh=mesh,
        in_specs=(blocks, blocks, P("batch", None)) + (rows,) * 12 + (P(),) * 3,
        out_specs=(blocks, blocks) + (rows,) * 12 + (P(),) * 3,
        check_vma=False,
    )
```

```python
import jax
import jax.numpy as jnp
from jax import lax
from jax.experimental import pallas as pl
from jax.experimental.pallas import tpu as pltpu
from jax.sharding import PartitionSpec as P

HD = 64
STEP = 10
LANES = 128
QUERY_ROWS = 256


norm_eps = 1e-05
rope_base = 130000.0
beta_one = 0.9
beta_two = 0.95
adam_eps = 1e-08
weight_decay = 0.1
masked_score = -1e30
rate_qkv = 0.05
rate_out = 0.5
rate_gate = 0.05
rate_down = 0.03
rate_gain = 0.3


def rotate_half(values):
    middle = values.shape[-1] // 2
    return jnp.concatenate([-values[..., middle:], values[..., :middle]], axis=-1)


def rope_tables(positions):
    inverse = rope_base ** (-jnp.arange(0, HD, 2, dtype=jnp.float32) / HD)
    angles = positions.astype(jnp.float32)[:, None] * inverse[None, :]
    angles = jnp.concatenate([angles, angles], axis=1)
    return (jnp.cos(angles), jnp.sin(angles))


def apply_rope(values, cos_table, sin_table):
    return values * cos_table + rotate_half(values) * sin_table


def undo_rope(values, cos_table, sin_table):
    return values * cos_table - rotate_half(values) * sin_table


def unit_rows(values):
    scale_rows = lax.rsqrt(jnp.mean(values * values, axis=-1, keepdims=True) + norm_eps)
    return (values * scale_rows, scale_rows)


def norm_back(grad_normed, unit_values, scale_rows, gain_row):
    grad_unit = grad_normed * gain_row
    gain_part = jnp.sum(grad_normed * unit_values, axis=0)
    grad_values = scale_rows * (
        grad_unit - unit_values * jnp.mean(grad_unit * unit_values, axis=-1, keepdims=True)
    )
    return (grad_values, gain_part)


def contract_rows(left_side, right_side):
    return lax.dot_general(
        left_side, right_side, (((0,), (0,)), ((), ())), preferred_element_type=jnp.float32
    )


def contract_cols(left_side, right_side):
    return lax.dot_general(
        left_side, right_side, (((1,), (1,)), ((), ())), preferred_element_type=jnp.float32
    )


def matmul(left_side, right_side):
    return jnp.dot(left_side, right_side, preferred_element_type=jnp.float32)


def adam_update(weight, first_moment, second, gradient, step_rate):
    first_new = beta_one * first_moment + (1.0 - beta_one) * gradient
    second_new = beta_two * second + (1.0 - beta_two) * gradient * gradient
    first_hat = first_new / (1.0 - beta_one**STEP)
    second_hat = second_new / (1.0 - beta_two**STEP)
    weight_new = weight - step_rate * (
        first_hat / (jnp.sqrt(second_hat) + adam_eps) + weight_decay * weight
    )
    return (first_new, second_new, weight_new)


def swapped(value, axis, bit):
    count = lax.axis_size(axis)
    return lax.ppermute(value, axis, [(source, source ^ bit) for source in range(count)])


def ring_order(count):
    return list(range(0, count, 2)) + list(range(count - 1, 0, -2))


def ring_shift(value, steps):
    count = lax.axis_size("seq")
    order = ring_order(count)
    pairs = [(order[i], order[(i + steps) % count]) for i in range(count)]
    return lax.ppermute(value, "seq", pairs)


def ring_place(offset):
    count = lax.axis_size("seq")
    own = lax.axis_index("seq")
    standing = jnp.where(own % 2 == 0, own // 2, count - 1 - own // 2)
    there = (standing + offset + count) % count
    return jnp.where(there < count // 2, 2 * there, 2 * (count - 1 - there) + 1)


def filled(arrays, filler):
    return filler(arrays) if callable(filler) else after_all(arrays, filler)


def ring_gather(parts, fillers=()):
    count = lax.axis_size("seq")
    far = count // 2
    packed = jnp.concatenate(parts, axis=1) if len(parts) > 1 else parts[0]
    middle = packed.shape[1] // 2
    blocks = {0: packed}
    ahead = behind = packed
    for step in range(1, far):
        if 0 <= step - 2 < len(fillers):
            ahead, behind = filled((ahead, behind), fillers[step - 2])
        ahead, behind = ring_shift(ahead, 1), ring_shift(behind, -1)
        blocks[-step], blocks[step] = ahead, behind
    if far - 2 < len(fillers):
        ahead, behind = filled((ahead, behind), fillers[far - 2])
    left, right = ring_shift(ahead[:, :middle], 1), ring_shift(behind[:, middle:], -1)
    blocks[far] = jnp.concatenate([left, right], axis=1)
    gathered = []
    first = 0
    for part in parts:
        last = first + part.shape[1]
        gathered.append({offset: block[:, first:last] for offset, block in blocks.items()})
        first = last
    return gathered


def with_rows(block, rows):
    if block.shape[0] >= rows:
        return jnp.concatenate(jnp.split(block, block.shape[0] // rows, axis=0), axis=1)
    return jnp.concatenate(jnp.split(block, rows // block.shape[0], axis=1), axis=0)


def stacked_rows(blocks):
    rows, width = blocks[0].shape
    whole = jnp.zeros((len(blocks) * rows, width), blocks[0].dtype)
    for offset, block in blocks.items():
        whole = lax.dynamic_update_slice(whole, block, (ring_place(offset) * rows, 0))
    return whole


def stacked_columns(blocks):
    rows, width = blocks[0].shape
    whole = jnp.zeros((rows, len(blocks) * width), blocks[0].dtype)
    for offset, block in blocks.items():
        whole = lax.dynamic_update_slice(whole, block, (0, ring_place(offset) * width))
    return whole


def ring_rows(whole, offsets):
    rows = whole.shape[0] // lax.axis_size("seq")
    return jnp.concatenate(
        [lax.dynamic_slice_in_dim(whole, ring_place(o) * rows, rows, 0) for o in offsets], axis=0
    )


def added(block, got):
    return (block.astype(jnp.float32) + got.astype(jnp.float32)).astype(block.dtype)


def ring_scatter_sum(blocks, fillers=()):
    far = lax.axis_size("seq") // 2
    middle = blocks[0].shape[1] // 2
    ahead = ring_shift(blocks[far][:, :middle], 1)
    behind = ring_shift(blocks[far][:, middle:], -1)
    for turn, step in enumerate(range(far - 1, 0, -1)):
        onward, backward = blocks[step], blocks[-step]
        if turn == 0:
            onward = jnp.concatenate([added(onward[:, :middle], ahead), onward[:, middle:]], axis=1)
            backward = jnp.concatenate(
                [backward[:, :middle], added(backward[:, middle:], behind)], axis=1
            )
        else:
            onward, backward = added(onward, ahead), added(backward, behind)
        if turn < len(fillers):
            onward, backward = filled([onward, backward], fillers[turn])
        ahead, behind = ring_shift(onward, 1), ring_shift(backward, -1)
    if far - 1 < len(fillers):
        ahead, behind = filled([ahead, behind], fillers[far - 1])
    return blocks[0].astype(jnp.float32) + ahead.astype(jnp.float32) + behind.astype(jnp.float32)


def ring_blocks(wholes):
    far = lax.axis_size("seq") // 2
    offsets = [far] + [sign * step for step in range(far - 1, 0, -1) for sign in (1, -1)] + [0]
    blocks = {far: jnp.concatenate([ring_rows(whole, [far]) for whole in wholes], axis=1)}
    wholes = after_all(wholes, (blocks[far],))
    for offset in offsets[1:]:
        blocks[offset] = jnp.concatenate([ring_rows(whole, [offset]) for whole in wholes], axis=1)
    return blocks


def butterfly_steps():
    steps = []
    for axis in ("batch", "seq"):
        bit = 1
        while bit < lax.axis_size(axis):
            steps.append((axis, bit))
            bit *= 2
    return steps


def after(value, *others):
    return lax.optimization_barrier((value,) + others)[0]


def after_all(values, others):
    return lax.optimization_barrier(tuple(values) + tuple(others))[: len(values)]


def batch_bits():
    count = lax.axis_size("batch")
    bits = []
    while (1 << len(bits)) < count:
        bits.append(1 << len(bits))
    return bits


def of_offset(choices, offset):
    index = lax.axis_index("batch")
    picked = choices[offset]
    for own in range(1, len(choices)):
        picked = jnp.where(index == own, choices[own ^ offset], picked)
    return picked


def offset_order():
    order = [0]
    for bit in reversed(batch_bits()):
        order = order + [offset ^ bit for offset in order]
    return order


def batch_columns(rows, rows_own):
    count, width = rows.shape
    batch_total = lax.axis_size("batch")
    blocks = rows.reshape(count, -1, batch_total, rows_own)
    return [blocks[:, :, b].reshape(count, width // batch_total) for b in range(batch_total)]


def to_relative(rows, rows_own):
    columns = batch_columns(rows, rows_own)
    return jnp.concatenate([of_offset(columns, m) for m in offset_order()], axis=1)


def from_relative(rows, rows_own):
    count, width = rows.shape
    batch_total = lax.axis_size("batch")
    order = offset_order()
    part = width // batch_total
    columns = [
        rows[:, order.index(m) * part : (order.index(m) + 1) * part] for m in range(batch_total)
    ]
    blocks = [
        of_offset(columns, b).reshape(count, width // (batch_total * rows_own), rows_own)
        for b in range(batch_total)
    ]
    return jnp.stack(blocks, axis=2).reshape(count, width)


def gather_pieces(block):
    pieces = [block]
    for bit in reversed(batch_bits()):
        pieces = pieces + [swapped(piece, "batch", bit) for piece in pieces]
    return pieces


def gather_batch(block):
    return jnp.concatenate(gather_pieces(block), axis=0)


def partial_sum_batch(left, right):
    width = left.shape[1]
    held = None
    sends = []

    def product(first, last):
        part = contract_rows(left[:, first:last], right)
        return part if held is None else part + held[first:last]

    for bit in batch_bits():
        half = width // 2
        sends.append(product(half, width).astype(jnp.bfloat16))
        got = swapped(sends[-1], "batch", bit).astype(jnp.float32)
        held = got if held is None else held[:half] + got
        width = half
    return (product(0, width).astype(jnp.bfloat16), sends)


def scatter_sum_batch(blocks):
    held = blocks
    for bit in batch_bits():
        pairs = held.reshape((held.shape[0] // 2, 2) + held.shape[1:])
        got = swapped(pairs[:, 1], "batch", bit)
        held = (pairs[:, 0].astype(jnp.float32) + got.astype(jnp.float32)).astype(jnp.bfloat16)
    return held[0]


def seqs_in_block(columns, seq_total):
    return max(1, min(seq_total, 1024 // columns))


def rounded_by_owner(weight, groups):
    rows_own, width = weight.shape
    seq_total = lax.axis_size("seq")
    columns = width // (groups * seq_total)
    if columns % LANES:
        blocks = weight.astype(jnp.bfloat16).reshape(rows_own, groups, seq_total, columns)
        return jnp.transpose(blocks, (2, 0, 1, 3)).reshape(seq_total, rows_own, groups * columns)
    taken = seqs_in_block(columns, seq_total)
    steps = seq_total // taken

    def kernel(weight_ref, out_ref):
        for place in range(taken):
            out_ref[place] = weight_ref[:, place * columns : (place + 1) * columns].astype(
                jnp.bfloat16
            )

    return pl.pallas_call(
        kernel,
        grid=(groups, steps),
        in_specs=[pl.BlockSpec((rows_own, taken * columns), lambda g, j: (0, g * steps + j))],
        out_specs=pl.BlockSpec((taken, rows_own, columns), lambda g, j: (j, 0, g)),
        out_shape=jax.ShapeDtypeStruct(
            (seq_total, rows_own, groups * columns), jnp.bfloat16
        ),
        cost_estimate=pl.CostEstimate(flops=0, bytes_accessed=weight.size * 6, transcendentals=0),
    )(weight)


def to_column_owners(blocks):
    got = lax.all_to_all(blocks, "seq", 0, 0, tiled=True)
    return got.reshape(-1, blocks.shape[2])


def to_row_owners(grad):
    seq_total = lax.axis_size("seq")
    blocks = grad.reshape(seq_total, grad.shape[0] // seq_total, grad.shape[1])
    return lax.all_to_all(blocks, "seq", 0, 0, tiled=True)


def adam_by_owner(weight, first_moment, second, gradient, groups, step_rate, skipped=0):
    rows_own, width = weight.shape
    seq_total = lax.axis_size("seq")
    columns = width // (groups * seq_total)
    if columns % LANES:
        own = gradient[:, :, skipped * columns : (skipped + groups) * columns]
        natural = jnp.transpose(
            own.reshape(seq_total, rows_own, groups, columns), (1, 2, 0, 3)
        ).reshape(rows_own, width)
        return adam_update(weight, first_moment, second, natural.astype(jnp.float32), step_rate)
    taken = seqs_in_block(columns, seq_total)
    steps = seq_total // taken

    def kernel(weight_ref, first_ref, second_ref, gradient_ref, *out_refs):
        for place in range(taken):
            here = slice(place * columns, (place + 1) * columns)
            results = adam_update(
                weight_ref[:, here],
                first_ref[:, here],
                second_ref[:, here],
                gradient_ref[place].astype(jnp.float32),
                step_rate,
            )
            for out_ref, result in zip(out_refs, results):
                out_ref[:, here] = result

    whole = pl.BlockSpec((rows_own, taken * columns), lambda g, j: (0, g * steps + j))
    return pl.pallas_call(
        kernel,
        grid=(groups, steps),
        in_specs=[whole] * 3 + [
            pl.BlockSpec((taken, rows_own, columns), lambda g, j: (j, 0, g + skipped))
        ],
        out_specs=[whole] * 3,
        out_shape=[jax.ShapeDtypeStruct(weight.shape, jnp.float32)] * 3,
        cost_estimate=pl.CostEstimate(
            flops=weight.size * 15, bytes_accessed=weight.size * 26, transcendentals=weight.size
        ),
    )(weight, first_moment, second, gradient)


def swap_halves(values):
    lane = lax.broadcasted_iota(jnp.int32, values.shape, 1)
    return jnp.where(
        lane % HD < HD // 2,
        pltpu.roll(values, LANES - HD // 2, 1),
        pltpu.roll(values, HD // 2, 1),
    )


def of_head(values, head, axis=1):
    lane = lax.broadcasted_iota(jnp.int32, values.shape, axis)
    return jnp.where(lane // HD == head, values, jnp.zeros_like(values))


def allowed_here(starts_ref, first, rows):
    shape = (rows, QUERY_ROWS)
    key = lax.broadcasted_iota(jnp.int32, shape, 0)
    query = lax.broadcasted_iota(jnp.int32, shape, 1) + first
    return (key <= query) & (key >= starts_ref[:, first : first + QUERY_ROWS])


def mm_last(left, right):
    return lax.dot_general(
        left, right, (((1,), (1,)), ((), ())), preferred_element_type=jnp.float32
    )


def attend_kernel(
    query_in, key_in, value_in, cos_ref, sin_ref, starts_ref,
    out_ref, low_ref, query_ref, key_ref, value_ref, total_ref, key_own, value_turned,
):
    length = query_in.shape[0]
    cos, sin = cos_ref[...], sin_ref[...]
    raw_query, raw_key = query_in[...], key_in[...]
    query_ref[...] = (raw_query * cos + swap_halves(raw_query) * sin).astype(jnp.bfloat16) * HD**-0.5
    key_ref[...] = (raw_key * cos + swap_halves(raw_key) * sin).astype(jnp.bfloat16)
    value_ref[...] = value_in[...].astype(jnp.bfloat16)
    turned = value_in[...].T
    for head in range(2):
        key_own[head] = of_head(key_ref[...], head)
        value_turned[head] = of_head(turned, head, 0).astype(jnp.bfloat16)
    for first in range(0, length, QUERY_ROWS):
        last = first + QUERY_ROWS
        allowed = allowed_here(starts_ref, first, last)
        weighted = jnp.zeros((LANES, QUERY_ROWS), jnp.float32)
        for head in range(2):
            scores = mm_last(key_own[head, :last], query_ref[first:last])
            scores = jnp.where(allowed, scores, masked_score)
            top = jnp.max(scores, axis=0, keepdims=True)
            powers = jnp.exp(scores - top)
            total = jnp.sum(powers, axis=0, keepdims=True)
            probs = (powers * (1.0 / total)).astype(jnp.bfloat16)
            weighted += matmul(value_turned[head, :, :last], probs)
            total_ref[0, head : head + 1, first:last] = top + jnp.log(total)
        attended = weighted.T
        out_ref[first:last] = attended
        low_ref[first:last] = attended.astype(jnp.bfloat16)


def attend_back_kernel(
    query_ref, key_ref, value_ref, grad_ref, attended_ref, total_ref, cos_ref, sin_ref, starts_ref,
    out_ref, key_own, value_own, key_turned, key_grad, value_grad,
):
    length = query_ref.shape[0]
    pair = pl.program_id(0)
    width = out_ref.shape[1] // 3
    turned = key_ref[...].astype(jnp.float32).T
    for head in range(2):
        key_own[head] = of_head(key_ref[...], head)
        value_own[head] = of_head(value_ref[...], head)
        key_turned[head] = of_head(turned, head, 0).astype(jnp.bfloat16)
    key_grad[...] = jnp.zeros_like(key_grad)
    value_grad[...] = jnp.zeros_like(value_grad)

    def undone(values, rows):
        back = values * cos_ref[rows] - swap_halves(values) * sin_ref[rows]
        return back.astype(jnp.bfloat16)

    def lanes(group):
        return pl.ds(pl.multiple_of(group * width + pair * LANES, LANES), LANES)

    for first in range(0, length, QUERY_ROWS):
        last = first + QUERY_ROWS
        rows = slice(first, last)
        allowed = allowed_here(starts_ref, first, last)
        grad, query = grad_ref[rows], query_ref[rows]
        products = (grad.astype(jnp.float32) * attended_ref[rows]).T
        query_grad = jnp.zeros((LANES, QUERY_ROWS), jnp.float32)
        for head in range(2):
            scores = mm_last(key_own[head, :last], query)
            probs = jnp.where(allowed, jnp.exp(scores - total_ref[0, head : head + 1, rows]), 0.0)
            delta = jnp.sum(products[head * HD : (head + 1) * HD], axis=0, keepdims=True)
            grad_probs = mm_last(value_own[head, :last], grad)
            grad_scores = (probs * (grad_probs - delta)).astype(jnp.bfloat16)
            value_grad[:last] += matmul(probs.astype(jnp.bfloat16), of_head(grad, head))
            key_grad[:last] += matmul(grad_scores, of_head(query, head))
            query_grad += matmul(key_turned[head, :, :last], grad_scores)
        out_ref[rows, lanes(0)] = undone(query_grad.T * HD**-0.5, rows)
    everything = slice(0, length)
    out_ref[:, lanes(1)] = undone(key_grad[...], everything)
    out_ref[:, lanes(2)] = value_grad[...].astype(jnp.bfloat16)


def project_kernel(total, attended_ref, inputs_ref, gain_ref, *refs):
    weight_refs, (middle_ref, unit_ref) = refs[:total], refs[total:]
    width = inputs_ref.shape[1]
    part = width // total
    attended = attended_ref[...]
    squares = 0.0
    for place, weight_ref in enumerate(weight_refs):
        columns = slice(place * part, (place + 1) * part)
        block = inputs_ref[:, columns].astype(jnp.float32) + matmul(attended, weight_ref[...])
        middle_ref[:, columns] = block
        squares += jnp.sum(block * block, axis=1, keepdims=True)
    scale = lax.rsqrt(squares / width + norm_eps)
    unit_ref[...] = (middle_ref[...] * scale * gain_ref[...]).astype(jnp.bfloat16)


def project_rows(attended, inputs, gain, pieces):
    length, width = inputs.shape
    total = len(pieces)
    rows = pl.BlockSpec((QUERY_ROWS, width), lambda i: (i, 0))
    return pl.pallas_call(
        lambda *refs: project_kernel(total, *refs),
        grid=(length // QUERY_ROWS,),
        in_specs=[rows, rows, pl.BlockSpec((1, width), lambda i: (0, 0))]
        + [pl.BlockSpec((width, width // total), lambda i: (0, 0))] * total,
        out_specs=[rows, rows],
        out_shape=[
            jax.ShapeDtypeStruct((length, width), jnp.float32),
            jax.ShapeDtypeStruct((length, width), jnp.bfloat16),
        ],
        compiler_params=pltpu.CompilerParams(vmem_limit_bytes=48 << 20),
        cost_estimate=pl.CostEstimate(
            flops=2 * length * width * width,
            bytes_accessed=10 * length * width + 2 * width * width,
            transcendentals=length,
        ),
    )(attended, inputs, gain, *pieces)


def summed_product(left_ref, weight_refs):
    part = left_ref.shape[1] // len(weight_refs)
    return sum(
        matmul(left_ref[:, place * part : (place + 1) * part], weight_ref[...])
        for place, weight_ref in enumerate(weight_refs)
    )


def hidden_kernel(total, rows_ref, *refs):
    gate_ref, up_ref, low_ref = refs[2 * total :]
    gate = summed_product(rows_ref, refs[:total])
    up = summed_product(rows_ref, refs[total : 2 * total])
    gate_ref[...] = gate
    up_ref[...] = up
    low_ref[...] = (gate * jax.nn.sigmoid(gate) * up).astype(jnp.bfloat16)


def hidden_units(rows, gate_pieces):
    length, width = rows.shape
    total = len(gate_pieces)
    hidden = gate_pieces[0].shape[1] // 2
    tile = min(hidden, 2 * LANES)
    steps = hidden // tile
    own = pl.BlockSpec((length, tile), lambda j: (0, j))
    wide = jax.ShapeDtypeStruct((length, hidden), jnp.float32)
    return pl.pallas_call(
        lambda *refs: hidden_kernel(total, *refs),
        grid=(steps,),
        in_specs=[pl.BlockSpec((length, width), lambda j: (0, 0))]
        + [pl.BlockSpec((width // total, tile), lambda j: (0, j))] * total
        + [pl.BlockSpec((width // total, tile), lambda j: (0, steps + j))] * total,
        out_specs=[own] * 3,
        out_shape=[wide, wide, jax.ShapeDtypeStruct((length, hidden), jnp.bfloat16)],
        compiler_params=pltpu.CompilerParams(vmem_limit_bytes=48 << 20),
        cost_estimate=pl.CostEstimate(
            flops=4 * length * width * hidden,
            bytes_accessed=2 * length * width + 4 * width * hidden + 10 * length * hidden,
            transcendentals=length * hidden,
        ),
    )(rows, *gate_pieces, *gate_pieces)


def hidden_back_kernel(total, grads_ref, gate_ref, up_ref, *refs):
    grad_ref = refs[total]
    tile = gate_ref.shape[1]
    hidden = grad_ref.shape[1] // 2
    grad = summed_product(grads_ref, refs[:total])
    gate, up = gate_ref[...], up_ref[...]
    sigmoid = jax.nn.sigmoid(gate)
    first = pl.multiple_of(pl.program_id(0) * tile, tile)
    grad_gate = grad * up * (sigmoid * (1.0 + gate * (1.0 - sigmoid)))
    grad_ref[:, pl.ds(first, tile)] = grad_gate.astype(jnp.bfloat16)
    second = pl.multiple_of(hidden + pl.program_id(0) * tile, tile)
    grad_ref[:, pl.ds(second, tile)] = (grad * (gate * sigmoid)).astype(jnp.bfloat16)


def hidden_back(grads, gate, up, down_pieces):
    length, width = grads.shape
    total = len(down_pieces)
    hidden = gate.shape[1]
    tile = min(hidden, 2 * LANES)
    own = pl.BlockSpec((length, tile), lambda j: (0, j))
    return pl.pallas_call(
        lambda *refs: hidden_back_kernel(total, *refs),
        grid=(hidden // tile,),
        in_specs=[pl.BlockSpec((length, width), lambda j: (0, 0)), own, own]
        + [pl.BlockSpec((width // total, tile), lambda j: (0, j))] * total,
        out_specs=pl.BlockSpec((length, 2 * hidden), lambda j: (0, 0)),
        out_shape=jax.ShapeDtypeStruct((length, 2 * hidden), jnp.bfloat16),
        compiler_params=pltpu.CompilerParams(vmem_limit_bytes=48 << 20),
        cost_estimate=pl.CostEstimate(
            flops=2 * length * width * hidden,
            bytes_accessed=2 * length * width + 2 * width * hidden + 12 * length * hidden,
            transcendentals=length * hidden,
        ),
    )(grads, gate, up, *down_pieces)


def back_kernel(total, left_ref, *refs):
    each = pl.num_programs(0) // total
    for place in range(total):

        @pl.when(pl.program_id(0) // each == place)
        def _():
            refs[total][...] = mm_last(left_ref[...], refs[place][...]).astype(jnp.bfloat16)


def back_to_model(left, pieces):
    length, inner = left.shape
    total = len(pieces)
    part = pieces[0].shape[0]
    tile = min(part, 2 * LANES)
    each = part // tile

    def rows_of(place):
        return pl.BlockSpec((tile, inner), lambda i: (jnp.clip(i - place * each, 0, each - 1), 0))

    return pl.pallas_call(
        lambda *refs: back_kernel(total, *refs),
        grid=(total * each,),
        in_specs=[pl.BlockSpec((length, inner), lambda i: (0, 0))]
        + [rows_of(place) for place in range(total)],
        out_specs=pl.BlockSpec((length, tile), lambda i: (0, i)),
        out_shape=jax.ShapeDtypeStruct((length, part * total), jnp.bfloat16),
        compiler_params=pltpu.CompilerParams(vmem_limit_bytes=48 << 20),
        cost_estimate=pl.CostEstimate(
            flops=2 * length * part * total * inner,
            bytes_accessed=2 * inner * (length + part * total) + 2 * length * part * total,
            transcendentals=0,
        ),
    )(left, *pieces)


def attend_forward(qkv, cos_table, sin_table, starts):
    length, width = qkv.shape[0], qkv.shape[1] // 3
    pairs = width // LANES
    whole = pl.BlockSpec((length, LANES), lambda p: (0, 0))
    own = pl.BlockSpec((length, LANES), lambda p: (0, p))
    low = jax.ShapeDtypeStruct((length, width), jnp.bfloat16)
    work = pairs * length * length
    return pl.pallas_call(
        attend_kernel,
        grid=(pairs,),
        in_specs=[
            own,
            pl.BlockSpec((length, LANES), lambda p: (0, pairs + p)),
            pl.BlockSpec((length, LANES), lambda p: (0, 2 * pairs + p)),
            whole,
            whole,
            pl.BlockSpec((1, length), lambda p: (0, 0)),
        ],
        out_specs=[own] * 5 + [pl.BlockSpec((1, 2, length), lambda p: (p, 0, 0))],
        out_shape=[
            jax.ShapeDtypeStruct((length, width), jnp.float32),
            low,
            low,
            low,
            low,
            jax.ShapeDtypeStruct((pairs, 2, length), jnp.float32),
        ],
        scratch_shapes=[
            pltpu.VMEM((2, length, LANES), jnp.bfloat16),
            pltpu.VMEM((2, LANES, length), jnp.bfloat16),
        ],
        compiler_params=pltpu.CompilerParams(vmem_limit_bytes=48 << 20),
        cost_estimate=pl.CostEstimate(
            flops=8 * work * LANES, bytes_accessed=qkv.size * 8, transcendentals=2 * work
        ),
    )(qkv, qkv, qkv, cos_table, sin_table, starts)


def attend_backward(query, key, value, grad, attended, total, cos_table, sin_table, starts):
    length, width = query.shape
    pairs = width // LANES
    whole = pl.BlockSpec((length, LANES), lambda p: (0, 0))
    own = pl.BlockSpec((length, LANES), lambda p: (0, p))
    work = pairs * length * length
    return pl.pallas_call(
        attend_back_kernel,
        grid=(pairs,),
        in_specs=[own] * 5
        + [
            pl.BlockSpec((1, 2, length), lambda p: (p, 0, 0)),
            whole,
            whole,
            pl.BlockSpec((1, length), lambda p: (0, 0)),
        ],
        out_specs=pl.BlockSpec((length, 3 * width), lambda p: (0, 0)),
        out_shape=jax.ShapeDtypeStruct((length, 3 * width), jnp.bfloat16),
        scratch_shapes=[
            pltpu.VMEM((2, length, LANES), jnp.bfloat16),
            pltpu.VMEM((2, length, LANES), jnp.bfloat16),
            pltpu.VMEM((2, LANES, length), jnp.bfloat16),
            pltpu.VMEM((length, LANES), jnp.float32),
            pltpu.VMEM((length, LANES), jnp.float32),
        ],
        compiler_params=pltpu.CompilerParams(vmem_limit_bytes=48 << 20),
        cost_estimate=pl.CostEstimate(
            flops=work * LANES, bytes_accessed=query.size * 4, transcendentals=work // 16
        ),
    )(query, key, value, grad, attended, total, cos_table, sin_table, starts)


def on_device(
    tokens,
    out_grad,
    doc_lengths,
    qkv_weight,
    qkv_first,
    qkv_second,
    out_weight,
    out_first,
    out_second,
    gate_up_weight,
    gate_up_first,
    gate_up_second,
    down_weight,
    down_first,
    down_second,
    gains,
    gain_first,
    gain_second,
):
    local_rows = tokens.shape[1]
    model_width = tokens.shape[2]
    rows_own = qkv_weight.shape[0]
    seq_total = lax.axis_size("seq")
    batch_total = lax.axis_size("batch")
    head_width = model_width // seq_total
    heads = head_width // HD
    length = local_rows * seq_total
    hidden = down_weight.shape[1] // seq_total
    score_scale = HD ** (-0.5)
    positions = jnp.arange(length, dtype=jnp.int32)
    ends = jnp.cumsum(doc_lengths[0])
    starts = jnp.max(jnp.where(positions[:, None] >= ends[None, :], ends[None, :], 0), axis=1)
    cos_table, sin_table = rope_tables(positions)
    in_pairs = head_width % LANES == 0 and length % QUERY_ROWS == 0
    if in_pairs:
        sign = jnp.where(jnp.arange(HD) < HD // 2, -1.0, 1.0)
        cos_pair = jnp.tile(cos_table, (1, 2))
        sin_pair = jnp.tile(sin_table * sign, (1, 2))

    def split_heads(columns):
        return jnp.transpose(columns.reshape(length, heads, HD), (1, 0, 2))

    def join_heads(values):
        return jnp.transpose(values, (1, 0, 2)).reshape(length, head_width)

    def allowed_pairs():
        return (
            (positions[None, :] <= positions[:, None]) & (positions[None, :] >= starts[:, None])
        )[None]

    def attention(qkv):
        if in_pairs:
            attended, low, *kept = attend_forward(qkv, cos_pair, sin_pair, starts[None])
            return (low, (attended, kept))
        query = split_heads(qkv[:, :head_width])
        query = apply_rope(query, cos_table, sin_table).astype(jnp.bfloat16)
        key = split_heads(qkv[:, head_width : 2 * head_width])
        key = apply_rope(key, cos_table, sin_table).astype(jnp.bfloat16)
        value = split_heads(qkv[:, 2 * head_width :]).astype(jnp.bfloat16)
        scores = jnp.einsum("hqd,hkd->hqk", query, key, preferred_element_type=jnp.float32)
        scores = jnp.where(allowed_pairs(), scores * score_scale, masked_score)
        probs = jax.nn.softmax(scores, axis=-1)
        attended = jnp.einsum(
            "hqk,hkd->hqd", probs.astype(jnp.bfloat16), value, preferred_element_type=jnp.float32
        )
        return (join_heads(attended.astype(jnp.bfloat16)), (attended, (query, key, value, probs)))

    def attention_back(grad, kept):
        if in_pairs:
            attended, (query, key, value, total) = kept
            return attend_backward(
                query, key, value, grad, attended, total, cos_pair, sin_pair, starts[None]
            )
        attended, (query, key, value, probs) = kept
        grad = split_heads(grad)
        delta = jnp.sum(grad.astype(jnp.float32) * attended, axis=-1, keepdims=True)
        grad_probs = jnp.einsum("hqd,hkd->hqk", grad, value, preferred_element_type=jnp.float32)
        grad_scores = (probs * (grad_probs - delta)).astype(jnp.bfloat16)

        def over_queries(left, right):
            return jnp.einsum("hqk,hqd->hkd", left, right, preferred_element_type=jnp.float32)

        grad_value = over_queries(probs.astype(jnp.bfloat16), grad)
        grad_key = over_queries(grad_scores, query) * score_scale
        grad_query = (
            jnp.einsum("hqk,hkd->hqd", grad_scores, key, preferred_element_type=jnp.float32)
            * score_scale
        )
        return jnp.concatenate(
            [
                join_heads(undo_rope(grad_query, cos_table, sin_table)),
                join_heads(undo_rope(grad_key, cos_table, sin_table)),
                join_heads(grad_value),
            ],
            axis=1,
        ).astype(jnp.bfloat16)

    first_row = lax.axis_index("seq") * local_rows
    gains_here = to_relative(gains, rows_own)
    tokens_here = to_relative(tokens[0], rows_own)
    grads_here = to_relative(out_grad[0], rows_own)
    qkv_low = rounded_by_owner(qkv_weight, 3)
    out_columns = batch_columns(after(out_weight, qkv_low).astype(jnp.bfloat16), rows_own)
    out_here = [
        swapped(of_offset(out_columns, m), "batch", m) if m else of_offset(out_columns, m)
        for m in range(batch_total)
    ]
    out_here = [of_offset(out_here, b) for b in range(batch_total)]
    out_here = with_rows(jnp.concatenate(out_here, axis=0), local_rows)
    gate_low = rounded_by_owner(gate_up_weight, 2)
    down_low = rounded_by_owner(down_weight, 1)
    qkv_block = to_column_owners(qkv_low)
    tokens_all, out_all = ring_gather(
        [after(tokens_here, qkv_low), out_here], ((qkv_block,), (gate_low, down_low))
    )
    tokens_all = stacked_rows(tokens_all)
    out_all = stacked_rows(
        {offset: with_rows(block, head_width) for offset, block in out_all.items()}
    )
    qkv_full = gather_batch(qkv_block)
    gate_block = to_column_owners(after(gate_low, tokens_all))
    inputs = tokens_all.astype(jnp.float32)
    act_one = (unit_rows(inputs)[0] * gains_here[0]).astype(jnp.bfloat16)
    qkv = matmul(act_one, qkv_full)
    attn_own, attn_kept = attention(qkv)

    out_pieces = gather_pieces(out_all)
    out_full = jnp.concatenate(out_pieces, axis=1)

    gate_block = after(gate_block, attn_own)
    attn_own_late = after(attn_own, gate_block)
    attn_all = stacked_columns(ring_gather([attn_own_late])[0])
    down_block = to_column_owners(after(down_low, attn_all))
    gate_pieces, down_pieces = gather_pieces(gate_block), gather_pieces(down_block)
    grads_here_late = after(grads_here, down_block)
    if in_pairs and length * model_width <= 1 << 21:
        middle_all, act_two = project_rows(attn_all, tokens_all, gains_here[1:], out_pieces)
        gate_part, up_part, hidden_low = hidden_units(act_two, gate_pieces)
        late = {}

        def block_meanwhile(moved):
            *moved, low = lax.optimization_barrier((*moved, hidden_low))
            late["block"] = back_to_model(low, down_pieces)
            return moved

        grads_all = ring_gather(
            [grads_here_late],
            ((hidden_low,), block_meanwhile, lambda moved: after_all(moved, (late["block"],))),
        )
        grads_all, block_part = stacked_rows(grads_all[0]), late["block"]
        grad_gate_up = hidden_back(grads_all, gate_part, up_part, down_pieces)
        grad_two = back_to_model(grad_gate_up, gate_pieces)
    else:
        grads_all = stacked_rows(ring_gather([grads_here_late])[0])
        middle_all = inputs + matmul(attn_all, out_full)
        act_two = (unit_rows(middle_all)[0] * gains_here[1]).astype(jnp.bfloat16)
        gate_full, down_full = jnp.concatenate(gate_pieces), jnp.concatenate(down_pieces)
        gate_up = matmul(act_two, gate_full)
        gate_part, up_part = gate_up[:, :hidden], gate_up[:, hidden:]
        sigmoid_gate = jax.nn.sigmoid(gate_part)
        silu_gate = gate_part * sigmoid_gate
        hidden_low = (silu_gate * up_part).astype(jnp.bfloat16)
        grad_hidden = matmul(grads_all, down_full)
        grad_gate = (
            grad_hidden * up_part * (sigmoid_gate * (1.0 + gate_part * (1.0 - sigmoid_gate)))
        )
        grad_gate_up = jnp.concatenate([grad_gate, grad_hidden * silu_gate], axis=1)
        grad_gate_up = grad_gate_up.astype(jnp.bfloat16)
        grad_two = contract_cols(grad_gate_up, gate_full).astype(jnp.bfloat16)
        block_part = contract_cols(hidden_low, down_full).astype(jnp.bfloat16)

    sums = {}

    def weight_sums(moved):
        *moved, low, grad = lax.optimization_barrier((*moved, hidden_low, grad_gate_up))
        sums["down"] = partial_sum_batch(grads_all, low)
        sums["gate"] = partial_sum_batch(act_two, grad)
        return moved

    def sent(stage):
        return lambda moved: after_all(moved, (sums["down"][1][stage], sums["gate"][1][stage]))

    summed = ring_scatter_sum(
        ring_blocks([grad_two, block_part]), (weight_sums, sent(0), sent(-1))
    )
    grad_two, block_rest = summed[:, :model_width], summed[:, model_width:]
    down_own, gate_own = sums["down"][0], sums["gate"][0]

    def own_rows(whole):
        return lax.dynamic_slice_in_dim(whole, first_row, local_rows, 0)

    middle = own_rows(middle_all)
    unit_two, scale_two = unit_rows(middle)
    block_out = from_relative((middle + block_rest).astype(jnp.bfloat16), rows_own)
    grad_mid_norm, gain_two_grad = norm_back(grad_two, unit_two, scale_two, gains_here[1])
    grad_middle = grads_here.astype(jnp.float32) + grad_mid_norm
    grad_attn_low = grad_middle.astype(jnp.bfloat16)
    grad_heads = contract_cols(grad_attn_low, out_full).astype(jnp.bfloat16)
    by_owner = jnp.concatenate(
        [
            grad_heads.reshape(local_rows, seq_total, head_width),
            from_relative(grad_attn_low, rows_own).reshape(local_rows, seq_total, head_width),
        ],
        axis=2,
    )
    down_grad = to_row_owners(down_own)
    by_owner = after(jnp.transpose(by_owner, (1, 0, 2)), down_grad)
    got = lax.all_to_all(by_owner, "seq", 0, 0, tiled=True)
    got = got.reshape(length, 2 * head_width)
    grad_heads = got[:, :head_width]
    grad_attn_own = got[:, head_width:]
    gate_grad = to_row_owners(after(gate_own, got))

    grad_qkv = attention_back(grad_heads, attn_kept)
    qkv_own, qkv_sends = partial_sum_batch(act_one, grad_qkv)
    out_part = contract_rows(attn_all, grad_attn_own).astype(jnp.bfloat16)
    out_part = out_part.reshape(seq_total, batch_total, rows_own, head_width)
    out_part = [
        out_part[:, b].reshape(seq_total * rows_own, head_width) for b in range(batch_total)
    ]
    out_own = scatter_sum_batch(jnp.stack([of_offset(out_part, m) for m in range(batch_total)]))
    grad_qkv = after(grad_qkv, qkv_sends[0], out_own, gate_grad)
    grad_one_part = contract_cols(grad_qkv, qkv_full)
    gain_one_part = jnp.sum(grad_one_part * act_one.astype(jnp.float32), axis=0)
    gain_grad = jnp.stack([gain_one_part / gains_here[0], gain_two_grad])
    gain_grad = from_relative(gain_grad, rows_own)
    down_m, down_s, down_w = adam_by_owner(
        down_weight, down_first, down_second, after(down_grad, qkv_sends[-1]), 1, rate_down
    )
    steps = butterfly_steps()

    def next_gain_sum():
        if steps:
            axis, bit = steps.pop(0)
            sums["gain"] = sums["gain"] + swapped(sums["gain"], axis, bit)

    def tied(moved, *names):
        moved = lax.optimization_barrier((*moved, *(sums[name] for name in names)))
        for name, value in zip(names, moved[len(moved) - len(names) :]):
            sums[name] = value
        next_gain_sum()
        return moved[: len(moved) - len(names)]

    def gate_update(moved):
        moved = tied(moved, "gain", "gate_grad")
        sums["gate_new"] = adam_by_owner(
            gate_up_weight, gate_up_first, gate_up_second, sums["gate_grad"], 2, rate_gate
        )
        return moved

    def last_transfer(moved):
        moved = tied(after_all(moved, (sums["gate_new"][0],)), "gain")
        return moved

    def last_updates(moved):
        sums["qkv"] = adam_by_owner(
            qkv_weight, qkv_first, qkv_second, sums["rest"], 3, rate_qkv
        )
        sums["out"] = adam_by_owner(
            out_weight, out_first, out_second, sums["rest"], 1, rate_out, skipped=3
        )
        return tied(after_all(moved, (sums["qkv"][0], sums["out"][0])), "gain")

    sums["gain"], sums["gate_grad"] = gain_grad, gate_grad
    next_gain_sum()
    sums["rest"] = to_row_owners(jnp.concatenate([after(qkv_own, gate_grad), out_own], axis=1))
    grad_one = ring_scatter_sum(
        ring_blocks([after(grad_one_part.astype(jnp.bfloat16), qkv_own, down_m)]),
        (gate_update, last_transfer, lambda moved: tied(moved, "gain"), last_updates),
    )
    while steps:
        next_gain_sum()
    gain_grad = sums["gain"]
    (qkv_m, qkv_s, qkv_w), (out_m, out_s, out_w) = sums["qkv"], sums["out"]
    gate_m, gate_s, gate_w = sums["gate_new"]
    unit_one, scale_one = unit_rows(tokens_here.astype(jnp.float32))
    grad_in_norm = norm_back(grad_one, unit_one, scale_one, gains_here[0])[0]
    input_grad = from_relative(grad_middle + grad_in_norm, rows_own)
    gain_m, gain_s, gain_w = adam_update(gains, gain_first, gain_second, gain_grad, rate_gain)
    return (
        block_out[None],
        input_grad[None],
        qkv_m,
        qkv_s,
        qkv_w,
        out_m,
        out_s,
        out_w,
        gate_m,
        gate_s,
        gate_w,
        down_m,
        down_s,
        down_w,
        gain_m,
        gain_s,
        gain_w,
    )


def solution(mesh):
    rows = P(("seq", "batch"), None)
    blocks = P("batch", "seq", None)
    return jax.shard_map(
        on_device,
        mesh=mesh,
        in_specs=(blocks, blocks, P("batch", None)) + (rows,) * 12 + (P(),) * 3,
        out_specs=(blocks, blocks) + (rows,) * 12 + (P(),) * 3,
        check_vma=False,
    )
```

```python
import jax
import jax.numpy as jnp
from jax import lax
from jax.experimental import pallas as pl
from jax.experimental.pallas import tpu as pltpu
from jax.sharding import PartitionSpec as P

HD = 64
STEP = 10
LANES = 128
QUERY_ROWS = 256


norm_eps = 1e-05
rope_base = 130000.0
beta_one = 0.9
beta_two = 0.95
adam_eps = 1e-08
weight_decay = 0.1
masked_score = -1e30
rate_qkv = 0.05
rate_out = 0.5
rate_gate = 0.05
rate_down = 0.03
rate_gain = 0.3


def rotate_half(values):
    middle = values.shape[-1] // 2
    return jnp.concatenate([-values[..., middle:], values[..., :middle]], axis=-1)


def rope_tables(positions):
    inverse = rope_base ** (-jnp.arange(0, HD, 2, dtype=jnp.float32) / HD)
    angles = positions.astype(jnp.float32)[:, None] * inverse[None, :]
    angles = jnp.concatenate([angles, angles], axis=1)
    return (jnp.cos(angles), jnp.sin(angles))


def apply_rope(values, cos_table, sin_table):
    return values * cos_table + rotate_half(values) * sin_table


def undo_rope(values, cos_table, sin_table):
    return values * cos_table - rotate_half(values) * sin_table


def unit_rows(values):
    scale_rows = lax.rsqrt(jnp.mean(values * values, axis=-1, keepdims=True) + norm_eps)
    return (values * scale_rows, scale_rows)


def norm_back(grad_normed, unit_values, scale_rows, gain_row):
    grad_unit = grad_normed * gain_row
    gain_part = jnp.sum(grad_normed * unit_values, axis=0)
    grad_values = scale_rows * (
        grad_unit - unit_values * jnp.mean(grad_unit * unit_values, axis=-1, keepdims=True)
    )
    return (grad_values, gain_part)


def contract_rows(left_side, right_side):
    return lax.dot_general(
        left_side, right_side, (((0,), (0,)), ((), ())), preferred_element_type=jnp.float32
    )


def contract_cols(left_side, right_side):
    return lax.dot_general(
        left_side, right_side, (((1,), (1,)), ((), ())), preferred_element_type=jnp.float32
    )


def matmul(left_side, right_side):
    return jnp.dot(left_side, right_side, preferred_element_type=jnp.float32)


def adam_update(weight, first_moment, second, gradient, step_rate):
    first_new = beta_one * first_moment + (1.0 - beta_one) * gradient
    second_new = beta_two * second + (1.0 - beta_two) * gradient * gradient
    first_hat = first_new / (1.0 - beta_one**STEP)
    second_hat = second_new / (1.0 - beta_two**STEP)
    weight_new = weight - step_rate * (
        first_hat / (jnp.sqrt(second_hat) + adam_eps) + weight_decay * weight
    )
    return (first_new, second_new, weight_new)


def swapped(value, axis, bit):
    count = lax.axis_size(axis)
    return lax.ppermute(value, axis, [(source, source ^ bit) for source in range(count)])


def ring_order(count):
    return list(range(0, count, 2)) + list(range(count - 1, 0, -2))


def ring_shift(value, steps):
    count = lax.axis_size("seq")
    order = ring_order(count)
    pairs = [(order[i], order[(i + steps) % count]) for i in range(count)]
    return lax.ppermute(value, "seq", pairs)


def ring_place(offset):
    count = lax.axis_size("seq")
    own = lax.axis_index("seq")
    standing = jnp.where(own % 2 == 0, own // 2, count - 1 - own // 2)
    there = (standing + offset + count) % count
    return jnp.where(there < count // 2, 2 * there, 2 * (count - 1 - there) + 1)


def filled(arrays, filler):
    return filler(arrays) if callable(filler) else after_all(arrays, filler)


def ring_gather(parts, fillers=()):
    count = lax.axis_size("seq")
    far = count // 2
    packed = jnp.concatenate(parts, axis=1) if len(parts) > 1 else parts[0]
    middle = packed.shape[1] // 2
    blocks = {0: packed}
    ahead = behind = packed
    for step in range(1, far):
        if 0 <= step - 2 < len(fillers):
            ahead, behind = filled((ahead, behind), fillers[step - 2])
        ahead, behind = ring_shift(ahead, 1), ring_shift(behind, -1)
        blocks[-step], blocks[step] = ahead, behind
    if far - 2 < len(fillers):
        ahead, behind = filled((ahead, behind), fillers[far - 2])
    left, right = ring_shift(ahead[:, :middle], 1), ring_shift(behind[:, middle:], -1)
    blocks[far] = jnp.concatenate([left, right], axis=1)
    gathered = []
    first = 0
    for part in parts:
        last = first + part.shape[1]
        gathered.append({offset: block[:, first:last] for offset, block in blocks.items()})
        first = last
    return gathered


def with_rows(block, rows):
    if block.shape[0] >= rows:
        return jnp.concatenate(jnp.split(block, block.shape[0] // rows, axis=0), axis=1)
    return jnp.concatenate(jnp.split(block, rows // block.shape[0], axis=1), axis=0)


def stacked_rows(blocks):
    rows, width = blocks[0].shape
    whole = jnp.zeros((len(blocks) * rows, width), blocks[0].dtype)
    for offset, block in blocks.items():
        whole = lax.dynamic_update_slice(whole, block, (ring_place(offset) * rows, 0))
    return whole


def stacked_columns(blocks):
    rows, width = blocks[0].shape
    whole = jnp.zeros((rows, len(blocks) * width), blocks[0].dtype)
    for offset, block in blocks.items():
        whole = lax.dynamic_update_slice(whole, block, (0, ring_place(offset) * width))
    return whole


def ring_rows(whole, offsets):
    rows = whole.shape[0] // lax.axis_size("seq")
    return jnp.concatenate(
        [lax.dynamic_slice_in_dim(whole, ring_place(o) * rows, rows, 0) for o in offsets], axis=0
    )


def added(block, got):
    return (block.astype(jnp.float32) + got.astype(jnp.float32)).astype(block.dtype)


def ring_scatter_sum(blocks, fillers=()):
    far = lax.axis_size("seq") // 2
    middle = blocks[0].shape[1] // 2
    ahead = ring_shift(blocks[far][:, :middle], 1)
    behind = ring_shift(blocks[far][:, middle:], -1)
    for turn, step in enumerate(range(far - 1, 0, -1)):
        onward, backward = blocks[step], blocks[-step]
        if turn == 0:
            onward = jnp.concatenate([added(onward[:, :middle], ahead), onward[:, middle:]], axis=1)
            backward = jnp.concatenate(
                [backward[:, :middle], added(backward[:, middle:], behind)], axis=1
            )
        else:
            onward, backward = added(onward, ahead), added(backward, behind)
        if turn < len(fillers):
            onward, backward = filled([onward, backward], fillers[turn])
        ahead, behind = ring_shift(onward, 1), ring_shift(backward, -1)
    if far - 1 < len(fillers):
        ahead, behind = filled([ahead, behind], fillers[far - 1])
    return blocks[0].astype(jnp.float32) + ahead.astype(jnp.float32) + behind.astype(jnp.float32)


def ring_blocks(wholes):
    far = lax.axis_size("seq") // 2
    offsets = [far] + [sign * step for step in range(far - 1, 0, -1) for sign in (1, -1)] + [0]
    blocks = {far: jnp.concatenate([ring_rows(whole, [far]) for whole in wholes], axis=1)}
    wholes = after_all(wholes, (blocks[far],))
    for offset in offsets[1:]:
        blocks[offset] = jnp.concatenate([ring_rows(whole, [offset]) for whole in wholes], axis=1)
    return blocks


def butterfly_steps():
    steps = []
    for axis in ("batch", "seq"):
        bit = 1
        while bit < lax.axis_size(axis):
            steps.append((axis, bit))
            bit *= 2
    return steps


def after(value, *others):
    return lax.optimization_barrier((value,) + others)[0]


def after_all(values, others):
    return lax.optimization_barrier(tuple(values) + tuple(others))[: len(values)]


def batch_bits():
    count = lax.axis_size("batch")
    bits = []
    while (1 << len(bits)) < count:
        bits.append(1 << len(bits))
    return bits


def of_offset(choices, offset):
    index = lax.axis_index("batch")
    picked = choices[offset]
    for own in range(1, len(choices)):
        picked = jnp.where(index == own, choices[own ^ offset], picked)
    return picked


def offset_order():
    order = [0]
    for bit in reversed(batch_bits()):
        order = order + [offset ^ bit for offset in order]
    return order


def batch_columns(rows, rows_own):
    count, width = rows.shape
    batch_total = lax.axis_size("batch")
    blocks = rows.reshape(count, -1, batch_total, rows_own)
    return [blocks[:, :, b].reshape(count, width // batch_total) for b in range(batch_total)]


def to_relative(rows, rows_own):
    columns = batch_columns(rows, rows_own)
    return jnp.concatenate([of_offset(columns, m) for m in offset_order()], axis=1)


def from_relative(rows, rows_own):
    count, width = rows.shape
    batch_total = lax.axis_size("batch")
    order = offset_order()
    part = width // batch_total
    columns = [
        rows[:, order.index(m) * part : (order.index(m) + 1) * part] for m in range(batch_total)
    ]
    blocks = [
        of_offset(columns, b).reshape(count, width // (batch_total * rows_own), rows_own)
        for b in range(batch_total)
    ]
    return jnp.stack(blocks, axis=2).reshape(count, width)


def gather_pieces(block):
    pieces = [block]
    for bit in reversed(batch_bits()):
        pieces = pieces + [swapped(piece, "batch", bit) for piece in pieces]
    return pieces


def gather_batch(block):
    return jnp.concatenate(gather_pieces(block), axis=0)


def partial_sum_batch(left, right):
    width = left.shape[1]
    held = None
    sends = []

    def product(first, last):
        part = contract_rows(left[:, first:last], right)
        return part if held is None else part + held[first:last]

    for bit in batch_bits():
        half = width // 2
        sends.append(product(half, width).astype(jnp.bfloat16))
        got = swapped(sends[-1], "batch", bit).astype(jnp.float32)
        held = got if held is None else held[:half] + got
        width = half
    return (product(0, width).astype(jnp.bfloat16), sends)


def scatter_sum_batch(blocks):
    held = blocks
    for bit in batch_bits():
        pairs = held.reshape((held.shape[0] // 2, 2) + held.shape[1:])
        got = swapped(pairs[:, 1], "batch", bit)
        held = (pairs[:, 0].astype(jnp.float32) + got.astype(jnp.float32)).astype(jnp.bfloat16)
    return held[0]


def seqs_in_block(columns, seq_total):
    return max(1, min(seq_total, 1024 // columns))


def rounded_by_owner(weight, groups):
    rows_own, width = weight.shape
    seq_total = lax.axis_size("seq")
    columns = width // (groups * seq_total)
    if columns % LANES:
        blocks = weight.astype(jnp.bfloat16).reshape(rows_own, groups, seq_total, columns)
        return jnp.transpose(blocks, (2, 0, 1, 3)).reshape(seq_total, rows_own, groups * columns)
    taken = seqs_in_block(columns, seq_total)
    steps = seq_total // taken

    def kernel(weight_ref, out_ref):
        for place in range(taken):
            out_ref[place] = weight_ref[:, place * columns : (place + 1) * columns].astype(
                jnp.bfloat16
            )

    return pl.pallas_call(
        kernel,
        grid=(groups, steps),
        in_specs=[pl.BlockSpec((rows_own, taken * columns), lambda g, j: (0, g * steps + j))],
        out_specs=pl.BlockSpec((taken, rows_own, columns), lambda g, j: (j, 0, g)),
        out_shape=jax.ShapeDtypeStruct(
            (seq_total, rows_own, groups * columns), jnp.bfloat16
        ),
        cost_estimate=pl.CostEstimate(flops=0, bytes_accessed=weight.size * 6, transcendentals=0),
    )(weight)


def to_column_owners(blocks):
    got = lax.all_to_all(blocks, "seq", 0, 0, tiled=True)
    return got.reshape(-1, blocks.shape[2])


def to_row_owners(grad):
    seq_total = lax.axis_size("seq")
    blocks = grad.reshape(seq_total, grad.shape[0] // seq_total, grad.shape[1])
    return lax.all_to_all(blocks, "seq", 0, 0, tiled=True)


def adam_by_owner(weight, first_moment, second, gradient, groups, step_rate, skipped=0):
    rows_own, width = weight.shape
    seq_total = lax.axis_size("seq")
    columns = width // (groups * seq_total)
    if columns % LANES:
        own = gradient[:, :, skipped * columns : (skipped + groups) * columns]
        natural = jnp.transpose(
            own.reshape(seq_total, rows_own, groups, columns), (1, 2, 0, 3)
        ).reshape(rows_own, width)
        return adam_update(weight, first_moment, second, natural.astype(jnp.float32), step_rate)
    taken = seqs_in_block(columns, seq_total)
    steps = seq_total // taken

    def kernel(weight_ref, first_ref, second_ref, gradient_ref, *out_refs):
        for place in range(taken):
            here = slice(place * columns, (place + 1) * columns)
            results = adam_update(
                weight_ref[:, here],
                first_ref[:, here],
                second_ref[:, here],
                gradient_ref[place].astype(jnp.float32),
                step_rate,
            )
            for out_ref, result in zip(out_refs, results):
                out_ref[:, here] = result

    whole = pl.BlockSpec((rows_own, taken * columns), lambda g, j: (0, g * steps + j))
    return pl.pallas_call(
        kernel,
        grid=(groups, steps),
        in_specs=[whole] * 3 + [
            pl.BlockSpec((taken, rows_own, columns), lambda g, j: (j, 0, g + skipped))
        ],
        out_specs=[whole] * 3,
        out_shape=[jax.ShapeDtypeStruct(weight.shape, jnp.float32)] * 3,
        cost_estimate=pl.CostEstimate(
            flops=weight.size * 15, bytes_accessed=weight.size * 26, transcendentals=weight.size
        ),
    )(weight, first_moment, second, gradient)


def swap_halves(values):
    lane = lax.broadcasted_iota(jnp.int32, values.shape, 1)
    return jnp.where(
        lane % HD < HD // 2,
        pltpu.roll(values, LANES - HD // 2, 1),
        pltpu.roll(values, HD // 2, 1),
    )


def of_head(values, head, axis=1):
    lane = lax.broadcasted_iota(jnp.int32, values.shape, axis)
    return jnp.where(lane // HD == head, values, jnp.zeros_like(values))


def allowed_here(starts_ref, first, rows):
    shape = (rows, QUERY_ROWS)
    key = lax.broadcasted_iota(jnp.int32, shape, 0)
    query = lax.broadcasted_iota(jnp.int32, shape, 1) + first
    return (key <= query) & (key >= starts_ref[:, first : first + QUERY_ROWS])


def mm_last(left, right):
    return lax.dot_general(
        left, right, (((1,), (1,)), ((), ())), preferred_element_type=jnp.float32
    )


def attend_kernel(
    query_in, key_in, value_in, cos_ref, sin_ref, starts_ref,
    out_ref, low_ref, query_ref, key_ref, value_ref, total_ref, key_own, value_turned,
):
    length = query_in.shape[0]
    cos, sin = cos_ref[...], sin_ref[...]
    raw_query, raw_key = query_in[...], key_in[...]
    query_ref[...] = (raw_query * cos + swap_halves(raw_query) * sin).astype(jnp.bfloat16) * HD**-0.5
    key_ref[...] = (raw_key * cos + swap_halves(raw_key) * sin).astype(jnp.bfloat16)
    value_ref[...] = value_in[...].astype(jnp.bfloat16)
    turned = value_in[...].T
    for head in range(2):
        key_own[head] = of_head(key_ref[...], head)
        value_turned[head] = of_head(turned, head, 0).astype(jnp.bfloat16)
    for first in range(0, length, QUERY_ROWS):
        last = first + QUERY_ROWS
        allowed = allowed_here(starts_ref, first, last)
        weighted = jnp.zeros((LANES, QUERY_ROWS), jnp.float32)
        for head in range(2):
            scores = mm_last(key_own[head, :last], query_ref[first:last])
            scores = jnp.where(allowed, scores, masked_score)
            top = jnp.max(scores, axis=0, keepdims=True)
            powers = jnp.exp(scores - top)
            total = jnp.sum(powers, axis=0, keepdims=True)
            probs = (powers * (1.0 / total)).astype(jnp.bfloat16)
            weighted += matmul(value_turned[head, :, :last], probs)
            total_ref[0, head : head + 1, first:last] = top + jnp.log(total)
        attended = weighted.T
        out_ref[first:last] = attended
        low_ref[first:last] = attended.astype(jnp.bfloat16)


def attend_back_kernel(
    query_ref, key_ref, value_ref, grad_ref, attended_ref, total_ref, cos_ref, sin_ref, starts_ref,
    out_ref, key_own, value_own, key_turned, key_grad, value_grad,
):
    length = query_ref.shape[0]
    pair = pl.program_id(0)
    width = out_ref.shape[1] // 3
    turned = key_ref[...].astype(jnp.float32).T
    for head in range(2):
        key_own[head] = of_head(key_ref[...], head)
        value_own[head] = of_head(value_ref[...], head)
        key_turned[head] = of_head(turned, head, 0).astype(jnp.bfloat16)
    key_grad[...] = jnp.zeros_like(key_grad)
    value_grad[...] = jnp.zeros_like(value_grad)

    def undone(values, rows):
        back = values * cos_ref[rows] - swap_halves(values) * sin_ref[rows]
        return back.astype(jnp.bfloat16)

    def lanes(group):
        return pl.ds(pl.multiple_of(group * width + pair * LANES, LANES), LANES)

    for first in range(0, length, QUERY_ROWS):
        last = first + QUERY_ROWS
        rows = slice(first, last)
        allowed = allowed_here(starts_ref, first, last)
        grad, query = grad_ref[rows], query_ref[rows]
        products = (grad.astype(jnp.float32) * attended_ref[rows]).T
        query_grad = jnp.zeros((LANES, QUERY_ROWS), jnp.float32)
        for head in range(2):
            scores = mm_last(key_own[head, :last], query)
            probs = jnp.where(allowed, jnp.exp(scores - total_ref[0, head : head + 1, rows]), 0.0)
            delta = jnp.sum(products[head * HD : (head + 1) * HD], axis=0, keepdims=True)
            grad_probs = mm_last(value_own[head, :last], grad)
            grad_scores = (probs * (grad_probs - delta)).astype(jnp.bfloat16)
            value_grad[:last] += matmul(probs.astype(jnp.bfloat16), of_head(grad, head))
            key_grad[:last] += matmul(grad_scores, of_head(query, head))
            query_grad += matmul(key_turned[head, :, :last], grad_scores)
        out_ref[rows, lanes(0)] = undone(query_grad.T * HD**-0.5, rows)
    everything = slice(0, length)
    out_ref[:, lanes(1)] = undone(key_grad[...], everything)
    out_ref[:, lanes(2)] = value_grad[...].astype(jnp.bfloat16)


def project_kernel(total, attended_ref, inputs_ref, gain_ref, *refs):
    weight_refs, (middle_ref, unit_ref) = refs[:total], refs[total:]
    width = inputs_ref.shape[1]
    part = width // total
    attended = attended_ref[...]
    squares = 0.0
    for place, weight_ref in enumerate(weight_refs):
        columns = slice(place * part, (place + 1) * part)
        block = inputs_ref[:, columns].astype(jnp.float32) + matmul(attended, weight_ref[...])
        middle_ref[:, columns] = block
        squares += jnp.sum(block * block, axis=1, keepdims=True)
    scale = lax.rsqrt(squares / width + norm_eps)
    unit_ref[...] = (middle_ref[...] * scale * gain_ref[...]).astype(jnp.bfloat16)


def project_rows(attended, inputs, gain, pieces):
    length, width = inputs.shape
    total = len(pieces)
    rows = pl.BlockSpec((QUERY_ROWS, width), lambda i: (i, 0))
    return pl.pallas_call(
        lambda *refs: project_kernel(total, *refs),
        grid=(length // QUERY_ROWS,),
        in_specs=[rows, rows, pl.BlockSpec((1, width), lambda i: (0, 0))]
        + [pl.BlockSpec((width, width // total), lambda i: (0, 0))] * total,
        out_specs=[rows, rows],
        out_shape=[
            jax.ShapeDtypeStruct((length, width), jnp.float32),
            jax.ShapeDtypeStruct((length, width), jnp.bfloat16),
        ],
        compiler_params=pltpu.CompilerParams(vmem_limit_bytes=48 << 20),
        cost_estimate=pl.CostEstimate(
            flops=2 * length * width * width,
            bytes_accessed=10 * length * width + 2 * width * width,
            transcendentals=length,
        ),
    )(attended, inputs, gain, *pieces)


def summed_product(left_ref, weight_refs):
    part = left_ref.shape[1] // len(weight_refs)
    return sum(
        matmul(left_ref[:, place * part : (place + 1) * part], weight_ref[...])
        for place, weight_ref in enumerate(weight_refs)
    )


def hidden_kernel(total, rows_ref, *refs):
    gate_ref, up_ref, low_ref = refs[2 * total :]
    gate = summed_product(rows_ref, refs[:total])
    up = summed_product(rows_ref, refs[total : 2 * total])
    gate_ref[...] = gate
    up_ref[...] = up
    low_ref[...] = (gate * jax.nn.sigmoid(gate) * up).astype(jnp.bfloat16)


def hidden_units(rows, gate_pieces):
    length, width = rows.shape
    total = len(gate_pieces)
    hidden = gate_pieces[0].shape[1] // 2
    tile = min(hidden, 2 * LANES)
    steps = hidden // tile
    own = pl.BlockSpec((length, tile), lambda j: (0, j))
    wide = jax.ShapeDtypeStruct((length, hidden), jnp.float32)
    return pl.pallas_call(
        lambda *refs: hidden_kernel(total, *refs),
        grid=(steps,),
        in_specs=[pl.BlockSpec((length, width), lambda j: (0, 0))]
        + [pl.BlockSpec((width // total, tile), lambda j: (0, j))] * total
        + [pl.BlockSpec((width // total, tile), lambda j: (0, steps + j))] * total,
        out_specs=[own] * 3,
        out_shape=[wide, wide, jax.ShapeDtypeStruct((length, hidden), jnp.bfloat16)],
        compiler_params=pltpu.CompilerParams(vmem_limit_bytes=48 << 20),
        cost_estimate=pl.CostEstimate(
            flops=4 * length * width * hidden,
            bytes_accessed=2 * length * width + 4 * width * hidden + 10 * length * hidden,
            transcendentals=length * hidden,
        ),
    )(rows, *gate_pieces, *gate_pieces)


def hidden_back_kernel(total, grads_ref, gate_ref, up_ref, *refs):
    grad_ref = refs[total]
    tile = gate_ref.shape[1]
    hidden = grad_ref.shape[1] // 2
    grad = summed_product(grads_ref, refs[:total])
    gate, up = gate_ref[...], up_ref[...]
    sigmoid = jax.nn.sigmoid(gate)
    first = pl.multiple_of(pl.program_id(0) * tile, tile)
    grad_gate = grad * up * (sigmoid * (1.0 + gate * (1.0 - sigmoid)))
    grad_ref[:, pl.ds(first, tile)] = grad_gate.astype(jnp.bfloat16)
    second = pl.multiple_of(hidden + pl.program_id(0) * tile, tile)
    grad_ref[:, pl.ds(second, tile)] = (grad * (gate * sigmoid)).astype(jnp.bfloat16)


def hidden_back(grads, gate, up, down_pieces):
    length, width = grads.shape
    total = len(down_pieces)
    hidden = gate.shape[1]
    tile = min(hidden, 2 * LANES)
    own = pl.BlockSpec((length, tile), lambda j: (0, j))
    return pl.pallas_call(
        lambda *refs: hidden_back_kernel(total, *refs),
        grid=(hidden // tile,),
        in_specs=[pl.BlockSpec((length, width), lambda j: (0, 0)), own, own]
        + [pl.BlockSpec((width // total, tile), lambda j: (0, j))] * total,
        out_specs=pl.BlockSpec((length, 2 * hidden), lambda j: (0, 0)),
        out_shape=jax.ShapeDtypeStruct((length, 2 * hidden), jnp.bfloat16),
        compiler_params=pltpu.CompilerParams(vmem_limit_bytes=48 << 20),
        cost_estimate=pl.CostEstimate(
            flops=2 * length * width * hidden,
            bytes_accessed=2 * length * width + 2 * width * hidden + 12 * length * hidden,
            transcendentals=length * hidden,
        ),
    )(grads, gate, up, *down_pieces)


def back_kernel(total, left_ref, *refs):
    each = pl.num_programs(0) // total
    for place in range(total):

        @pl.when(pl.program_id(0) // each == place)
        def _():
            refs[total][...] = mm_last(left_ref[...], refs[place][...]).astype(jnp.bfloat16)


def back_to_model(left, pieces):
    length, inner = left.shape
    total = len(pieces)
    part = pieces[0].shape[0]
    tile = min(part, 2 * LANES)
    each = part // tile

    def rows_of(place):
        return pl.BlockSpec((tile, inner), lambda i: (jnp.clip(i - place * each, 0, each - 1), 0))

    return pl.pallas_call(
        lambda *refs: back_kernel(total, *refs),
        grid=(total * each,),
        in_specs=[pl.BlockSpec((length, inner), lambda i: (0, 0))]
        + [rows_of(place) for place in range(total)],
        out_specs=pl.BlockSpec((length, tile), lambda i: (0, i)),
        out_shape=jax.ShapeDtypeStruct((length, part * total), jnp.bfloat16),
        compiler_params=pltpu.CompilerParams(vmem_limit_bytes=48 << 20),
        cost_estimate=pl.CostEstimate(
            flops=2 * length * part * total * inner,
            bytes_accessed=2 * inner * (length + part * total) + 2 * length * part * total,
            transcendentals=0,
        ),
    )(left, *pieces)


def attend_forward(qkv, cos_table, sin_table, starts):
    length, width = qkv.shape[0], qkv.shape[1] // 3
    pairs = width // LANES
    whole = pl.BlockSpec((length, LANES), lambda p: (0, 0))
    own = pl.BlockSpec((length, LANES), lambda p: (0, p))
    low = jax.ShapeDtypeStruct((length, width), jnp.bfloat16)
    work = pairs * length * length
    return pl.pallas_call(
        attend_kernel,
        grid=(pairs,),
        in_specs=[
            own,
            pl.BlockSpec((length, LANES), lambda p: (0, pairs + p)),
            pl.BlockSpec((length, LANES), lambda p: (0, 2 * pairs + p)),
            whole,
            whole,
            pl.BlockSpec((1, length), lambda p: (0, 0)),
        ],
        out_specs=[own] * 5 + [pl.BlockSpec((1, 2, length), lambda p: (p, 0, 0))],
        out_shape=[
            jax.ShapeDtypeStruct((length, width), jnp.float32),
            low,
            low,
            low,
            low,
            jax.ShapeDtypeStruct((pairs, 2, length), jnp.float32),
        ],
        scratch_shapes=[
            pltpu.VMEM((2, length, LANES), jnp.bfloat16),
            pltpu.VMEM((2, LANES, length), jnp.bfloat16),
        ],
        compiler_params=pltpu.CompilerParams(vmem_limit_bytes=48 << 20),
        cost_estimate=pl.CostEstimate(
            flops=8 * work * LANES, bytes_accessed=qkv.size * 8, transcendentals=2 * work
        ),
    )(qkv, qkv, qkv, cos_table, sin_table, starts)


def attend_backward(query, key, value, grad, attended, total, cos_table, sin_table, starts):
    length, width = query.shape
    pairs = width // LANES
    whole = pl.BlockSpec((length, LANES), lambda p: (0, 0))
    own = pl.BlockSpec((length, LANES), lambda p: (0, p))
    work = pairs * length * length
    return pl.pallas_call(
        attend_back_kernel,
        grid=(pairs,),
        in_specs=[own] * 5
        + [
            pl.BlockSpec((1, 2, length), lambda p: (p, 0, 0)),
            whole,
            whole,
            pl.BlockSpec((1, length), lambda p: (0, 0)),
        ],
        out_specs=pl.BlockSpec((length, 3 * width), lambda p: (0, 0)),
        out_shape=jax.ShapeDtypeStruct((length, 3 * width), jnp.bfloat16),
        scratch_shapes=[
            pltpu.VMEM((2, length, LANES), jnp.bfloat16),
            pltpu.VMEM((2, length, LANES), jnp.bfloat16),
            pltpu.VMEM((2, LANES, length), jnp.bfloat16),
            pltpu.VMEM((length, LANES), jnp.float32),
            pltpu.VMEM((length, LANES), jnp.float32),
        ],
        compiler_params=pltpu.CompilerParams(vmem_limit_bytes=48 << 20),
        cost_estimate=pl.CostEstimate(
            flops=work * LANES, bytes_accessed=query.size * 4, transcendentals=work // 16
        ),
    )(query, key, value, grad, attended, total, cos_table, sin_table, starts)


def on_device(
    tokens,
    out_grad,
    doc_lengths,
    qkv_weight,
    qkv_first,
    qkv_second,
    out_weight,
    out_first,
    out_second,
    gate_up_weight,
    gate_up_first,
    gate_up_second,
    down_weight,
    down_first,
    down_second,
    gains,
    gain_first,
    gain_second,
):
    local_rows = tokens.shape[1]
    model_width = tokens.shape[2]
    rows_own = qkv_weight.shape[0]
    seq_total = lax.axis_size("seq")
    batch_total = lax.axis_size("batch")
    head_width = model_width // seq_total
    heads = head_width // HD
    length = local_rows * seq_total
    hidden = down_weight.shape[1] // seq_total
    score_scale = HD ** (-0.5)
    positions = jnp.arange(length, dtype=jnp.int32)
    ends = jnp.cumsum(doc_lengths[0])
    starts = jnp.max(jnp.where(positions[:, None] >= ends[None, :], ends[None, :], 0), axis=1)
    cos_table, sin_table = rope_tables(positions)
    in_pairs = head_width % LANES == 0 and length % QUERY_ROWS == 0
    if in_pairs:
        sign = jnp.where(jnp.arange(HD) < HD // 2, -1.0, 1.0)
        cos_pair = jnp.tile(cos_table, (1, 2))
        sin_pair = jnp.tile(sin_table * sign, (1, 2))

    def split_heads(columns):
        return jnp.transpose(columns.reshape(length, heads, HD), (1, 0, 2))

    def join_heads(values):
        return jnp.transpose(values, (1, 0, 2)).reshape(length, head_width)

    def allowed_pairs():
        return (
            (positions[None, :] <= positions[:, None]) & (positions[None, :] >= starts[:, None])
        )[None]

    def attention(qkv):
        if in_pairs:
            attended, low, *kept = attend_forward(qkv, cos_pair, sin_pair, starts[None])
            return (low, (attended, kept))
        query = split_heads(qkv[:, :head_width])
        query = apply_rope(query, cos_table, sin_table).astype(jnp.bfloat16)
        key = split_heads(qkv[:, head_width : 2 * head_width])
        key = apply_rope(key, cos_table, sin_table).astype(jnp.bfloat16)
        value = split_heads(qkv[:, 2 * head_width :]).astype(jnp.bfloat16)
        scores = jnp.einsum("hqd,hkd->hqk", query, key, preferred_element_type=jnp.float32)
        scores = jnp.where(allowed_pairs(), scores * score_scale, masked_score)
        probs = jax.nn.softmax(scores, axis=-1)
        attended = jnp.einsum(
            "hqk,hkd->hqd", probs.astype(jnp.bfloat16), value, preferred_element_type=jnp.float32
        )
        return (join_heads(attended.astype(jnp.bfloat16)), (attended, (query, key, value, probs)))

    def attention_back(grad, kept):
        if in_pairs:
            attended, (query, key, value, total) = kept
            return attend_backward(
                query, key, value, grad, attended, total, cos_pair, sin_pair, starts[None]
            )
        attended, (query, key, value, probs) = kept
        grad = split_heads(grad)
        delta = jnp.sum(grad.astype(jnp.float32) * attended, axis=-1, keepdims=True)
        grad_probs = jnp.einsum("hqd,hkd->hqk", grad, value, preferred_element_type=jnp.float32)
        grad_scores = (probs * (grad_probs - delta)).astype(jnp.bfloat16)

        def over_queries(left, right):
            return jnp.einsum("hqk,hqd->hkd", left, right, preferred_element_type=jnp.float32)

        grad_value = over_queries(probs.astype(jnp.bfloat16), grad)
        grad_key = over_queries(grad_scores, query) * score_scale
        grad_query = (
            jnp.einsum("hqk,hkd->hqd", grad_scores, key, preferred_element_type=jnp.float32)
            * score_scale
        )
        return jnp.concatenate(
            [
                join_heads(undo_rope(grad_query, cos_table, sin_table)),
                join_heads(undo_rope(grad_key, cos_table, sin_table)),
                join_heads(grad_value),
            ],
            axis=1,
        ).astype(jnp.bfloat16)

    first_row = lax.axis_index("seq") * local_rows
    gains_here = to_relative(gains, rows_own)
    tokens_here = to_relative(tokens[0], rows_own)
    grads_here = to_relative(out_grad[0], rows_own)
    qkv_low = rounded_by_owner(qkv_weight, 3)
    out_columns = batch_columns(after(out_weight, qkv_low).astype(jnp.bfloat16), rows_own)
    out_here = [
        swapped(of_offset(out_columns, m), "batch", m) if m else of_offset(out_columns, m)
        for m in range(batch_total)
    ]
    out_here = [of_offset(out_here, b) for b in range(batch_total)]
    out_here = with_rows(jnp.concatenate(out_here, axis=0), local_rows)
    gate_low = rounded_by_owner(gate_up_weight, 2)
    down_low = rounded_by_owner(down_weight, 1)
    qkv_block = to_column_owners(qkv_low)
    tokens_all, out_all = ring_gather(
        [after(tokens_here, qkv_low), out_here], ((qkv_block,), (gate_low, down_low))
    )
    tokens_all = stacked_rows(tokens_all)
    out_all = stacked_rows(
        {offset: with_rows(block, head_width) for offset, block in out_all.items()}
    )
    qkv_full = gather_batch(qkv_block)
    gate_block = to_column_owners(after(gate_low, tokens_all))
    inputs = tokens_all.astype(jnp.float32)
    act_one = (unit_rows(inputs)[0] * gains_here[0]).astype(jnp.bfloat16)
    qkv = matmul(act_one, qkv_full)
    attn_own, attn_kept = attention(qkv)

    out_pieces = gather_pieces(out_all)
    out_full = jnp.concatenate(out_pieces, axis=1)

    gate_block = after(gate_block, attn_own)
    attn_own_late = after(attn_own, gate_block)
    attn_all = stacked_columns(ring_gather([attn_own_late])[0])
    down_block = to_column_owners(after(down_low, attn_all))
    gate_pieces, down_pieces = gather_pieces(gate_block), gather_pieces(down_block)
    grads_here_late = after(grads_here, down_block)
    if in_pairs and length * model_width <= 1 << 21:
        middle_all, act_two = project_rows(attn_all, tokens_all, gains_here[1:], out_pieces)
        gate_part, up_part, hidden_low = hidden_units(act_two, gate_pieces)
        late = {}

        def block_meanwhile(moved):
            *moved, low = lax.optimization_barrier((*moved, hidden_low))
            late["block"] = back_to_model(low, down_pieces)
            return moved

        grads_all = ring_gather(
            [grads_here_late],
            ((hidden_low,), block_meanwhile, lambda moved: after_all(moved, (late["block"],))),
        )
        grads_all, block_part = stacked_rows(grads_all[0]), late["block"]
        grad_gate_up = hidden_back(grads_all, gate_part, up_part, down_pieces)
        grad_two = back_to_model(grad_gate_up, gate_pieces)
    else:
        grads_all = stacked_rows(ring_gather([grads_here_late])[0])
        middle_all = inputs + matmul(attn_all, out_full)
        act_two = (unit_rows(middle_all)[0] * gains_here[1]).astype(jnp.bfloat16)
        gate_full, down_full = jnp.concatenate(gate_pieces), jnp.concatenate(down_pieces)
        gate_up = matmul(act_two, gate_full)
        gate_part, up_part = gate_up[:, :hidden], gate_up[:, hidden:]
        sigmoid_gate = jax.nn.sigmoid(gate_part)
        silu_gate = gate_part * sigmoid_gate
        hidden_low = (silu_gate * up_part).astype(jnp.bfloat16)
        grad_hidden = matmul(grads_all, down_full)
        grad_gate = (
            grad_hidden * up_part * (sigmoid_gate * (1.0 + gate_part * (1.0 - sigmoid_gate)))
        )
        grad_gate_up = jnp.concatenate([grad_gate, grad_hidden * silu_gate], axis=1)
        grad_gate_up = grad_gate_up.astype(jnp.bfloat16)
        grad_two = contract_cols(grad_gate_up, gate_full).astype(jnp.bfloat16)
        block_part = contract_cols(hidden_low, down_full).astype(jnp.bfloat16)

    sums = {}

    def weight_sums(moved):
        *moved, low, grad = lax.optimization_barrier((*moved, hidden_low, grad_gate_up))
        sums["down"] = partial_sum_batch(grads_all, low)
        sums["gate"] = partial_sum_batch(act_two, grad)
        return moved

    def sent(stage):
        return lambda moved: after_all(moved, (sums["down"][1][stage], sums["gate"][1][stage]))

    summed = ring_scatter_sum(
        ring_blocks([grad_two, block_part]), (weight_sums, sent(0), sent(-1))
    )
    grad_two, block_rest = summed[:, :model_width], summed[:, model_width:]
    down_own, gate_own = sums["down"][0], sums["gate"][0]

    def own_rows(whole):
        return lax.dynamic_slice_in_dim(whole, first_row, local_rows, 0)

    middle = own_rows(middle_all)
    unit_two, scale_two = unit_rows(middle)
    block_out = from_relative((middle + block_rest).astype(jnp.bfloat16), rows_own)
    grad_mid_norm, gain_two_grad = norm_back(grad_two, unit_two, scale_two, gains_here[1])
    grad_middle = grads_here.astype(jnp.float32) + grad_mid_norm
    grad_attn_low = grad_middle.astype(jnp.bfloat16)
    grad_heads = contract_cols(grad_attn_low, out_full).astype(jnp.bfloat16)
    by_owner = jnp.concatenate(
        [
            grad_heads.reshape(local_rows, seq_total, head_width),
            from_relative(grad_attn_low, rows_own).reshape(local_rows, seq_total, head_width),
        ],
        axis=2,
    )
    by_owner = jnp.transpose(by_owner, (1, 0, 2))
    got = lax.all_to_all(by_owner, "seq", 0, 0, tiled=True)
    got = got.reshape(length, 2 * head_width)
    grad_heads = got[:, :head_width]
    grad_attn_own = got[:, head_width:]
    gate_grad = to_row_owners(after(gate_own, got))
    down_grad = to_row_owners(after(down_own, gate_grad))

    grad_qkv = attention_back(grad_heads, attn_kept)
    qkv_own, qkv_sends = partial_sum_batch(act_one, grad_qkv)
    out_part = contract_rows(attn_all, grad_attn_own).astype(jnp.bfloat16)
    out_part = out_part.reshape(seq_total, batch_total, rows_own, head_width)
    out_part = [
        out_part[:, b].reshape(seq_total * rows_own, head_width) for b in range(batch_total)
    ]
    out_own = scatter_sum_batch(jnp.stack([of_offset(out_part, m) for m in range(batch_total)]))
    grad_qkv = after(grad_qkv, qkv_sends[0], out_own, gate_grad)
    grad_one_part = contract_cols(grad_qkv, qkv_full)
    gain_one_part = jnp.sum(grad_one_part * act_one.astype(jnp.float32), axis=0)
    gain_grad = jnp.stack([gain_one_part / gains_here[0], gain_two_grad])
    gain_grad = from_relative(gain_grad, rows_own)
    down_m, down_s, down_w = adam_by_owner(
        down_weight, down_first, down_second, after(down_grad, qkv_sends[-1]), 1, rate_down
    )
    steps = butterfly_steps()

    def next_gain_sum():
        if steps:
            axis, bit = steps.pop(0)
            sums["gain"] = sums["gain"] + swapped(sums["gain"], axis, bit)

    def tied(moved, *names):
        moved = lax.optimization_barrier((*moved, *(sums[name] for name in names)))
        for name, value in zip(names, moved[len(moved) - len(names) :]):
            sums[name] = value
        next_gain_sum()
        return moved[: len(moved) - len(names)]

    def gate_update(moved):
        moved = tied(moved, "gain", "gate_grad")
        sums["gate_new"] = adam_by_owner(
            gate_up_weight, gate_up_first, gate_up_second, sums["gate_grad"], 2, rate_gate
        )
        return moved

    def last_transfer(moved):
        moved = tied(after_all(moved, (sums["gate_new"][0],)), "gain")
        return moved

    def last_updates(moved):
        sums["qkv"] = adam_by_owner(
            qkv_weight, qkv_first, qkv_second, sums["rest"], 3, rate_qkv
        )
        sums["out"] = adam_by_owner(
            out_weight, out_first, out_second, sums["rest"], 1, rate_out, skipped=3
        )
        return tied(after_all(moved, (sums["qkv"][0], sums["out"][0])), "gain")

    sums["gain"], sums["gate_grad"] = gain_grad, gate_grad
    next_gain_sum()
    sums["rest"] = to_row_owners(jnp.concatenate([after(qkv_own, down_grad), out_own], axis=1))
    grad_one = ring_scatter_sum(
        ring_blocks([after(grad_one_part.astype(jnp.bfloat16), qkv_sends[-1])]),
        (gate_update, last_transfer, lambda moved: tied(after_all(moved, (down_m,)), "gain"), last_updates),
    )
    while steps:
        next_gain_sum()
    gain_grad = sums["gain"]
    (qkv_m, qkv_s, qkv_w), (out_m, out_s, out_w) = sums["qkv"], sums["out"]
    gate_m, gate_s, gate_w = sums["gate_new"]
    unit_one, scale_one = unit_rows(tokens_here.astype(jnp.float32))
    grad_in_norm = norm_back(grad_one, unit_one, scale_one, gains_here[0])[0]
    input_grad = from_relative(grad_middle + grad_in_norm, rows_own)
    gain_m, gain_s, gain_w = adam_update(gains, gain_first, gain_second, gain_grad, rate_gain)
    return (
        block_out[None],
        input_grad[None],
        qkv_m,
        qkv_s,
        qkv_w,
        out_m,
        out_s,
        out_w,
        gate_m,
        gate_s,
        gate_w,
        down_m,
        down_s,
        down_w,
        gain_m,
        gain_s,
        gain_w,
    )


def solution(mesh):
    rows = P(("seq", "batch"), None)
    blocks = P("batch", "seq", None)
    return jax.shard_map(
        on_device,
        mesh=mesh,
        in_specs=(blocks, blocks, P("batch", None)) + (rows,) * 12 + (P(),) * 3,
        out_specs=(blocks, blocks) + (rows,) * 12 + (P(),) * 3,
        check_vma=False,
    )
```

```python
import jax
import jax.numpy as jnp
from jax import lax
from jax.experimental import pallas as pl
from jax.experimental.pallas import tpu as pltpu
from jax.sharding import PartitionSpec as P

HD = 64
STEP = 10
LANES = 128
QUERY_ROWS = 256


norm_eps = 1e-05
rope_base = 130000.0
beta_one = 0.9
beta_two = 0.95
adam_eps = 1e-08
weight_decay = 0.1
masked_score = -1e30
rate_qkv = 0.05
rate_out = 0.5
rate_gate = 0.05
rate_down = 0.03
rate_gain = 0.3


def rotate_half(values):
    middle = values.shape[-1] // 2
    return jnp.concatenate([-values[..., middle:], values[..., :middle]], axis=-1)


def rope_tables(positions):
    inverse = rope_base ** (-jnp.arange(0, HD, 2, dtype=jnp.float32) / HD)
    angles = positions.astype(jnp.float32)[:, None] * inverse[None, :]
    angles = jnp.concatenate([angles, angles], axis=1)
    return (jnp.cos(angles), jnp.sin(angles))


def apply_rope(values, cos_table, sin_table):
    return values * cos_table + rotate_half(values) * sin_table


def undo_rope(values, cos_table, sin_table):
    return values * cos_table - rotate_half(values) * sin_table


def unit_rows(values):
    scale_rows = lax.rsqrt(jnp.mean(values * values, axis=-1, keepdims=True) + norm_eps)
    return (values * scale_rows, scale_rows)


def norm_back(grad_normed, unit_values, scale_rows, gain_row):
    grad_unit = grad_normed * gain_row
    gain_part = jnp.sum(grad_normed * unit_values, axis=0)
    grad_values = scale_rows * (
        grad_unit - unit_values * jnp.mean(grad_unit * unit_values, axis=-1, keepdims=True)
    )
    return (grad_values, gain_part)


def contract_rows(left_side, right_side):
    return lax.dot_general(
        left_side, right_side, (((0,), (0,)), ((), ())), preferred_element_type=jnp.float32
    )


def contract_cols(left_side, right_side):
    return lax.dot_general(
        left_side, right_side, (((1,), (1,)), ((), ())), preferred_element_type=jnp.float32
    )


def matmul(left_side, right_side):
    return jnp.dot(left_side, right_side, preferred_element_type=jnp.float32)


def adam_update(weight, first_moment, second, gradient, step_rate):
    first_new = beta_one * first_moment + (1.0 - beta_one) * gradient
    second_new = beta_two * second + (1.0 - beta_two) * gradient * gradient
    first_hat = first_new / (1.0 - beta_one**STEP)
    second_hat = second_new / (1.0 - beta_two**STEP)
    weight_new = weight - step_rate * (
        first_hat / (jnp.sqrt(second_hat) + adam_eps) + weight_decay * weight
    )
    return (first_new, second_new, weight_new)


def swapped(value, axis, bit):
    count = lax.axis_size(axis)
    return lax.ppermute(value, axis, [(source, source ^ bit) for source in range(count)])


def ring_order(count):
    return list(range(0, count, 2)) + list(range(count - 1, 0, -2))


def ring_shift(value, steps):
    count = lax.axis_size("seq")
    order = ring_order(count)
    pairs = [(order[i], order[(i + steps) % count]) for i in range(count)]
    return lax.ppermute(value, "seq", pairs)


def ring_place(offset):
    count = lax.axis_size("seq")
    own = lax.axis_index("seq")
    standing = jnp.where(own % 2 == 0, own // 2, count - 1 - own // 2)
    there = (standing + offset + count) % count
    return jnp.where(there < count // 2, 2 * there, 2 * (count - 1 - there) + 1)


def filled(arrays, filler):
    return filler(arrays) if callable(filler) else after_all(arrays, filler)


def ring_gather(parts, fillers=()):
    count = lax.axis_size("seq")
    far = count // 2
    packed = jnp.concatenate(parts, axis=1) if len(parts) > 1 else parts[0]
    middle = packed.shape[1] // 2
    blocks = {0: packed}
    ahead = behind = packed
    for step in range(1, far):
        if 0 <= step - 2 < len(fillers):
            ahead, behind = filled((ahead, behind), fillers[step - 2])
        ahead, behind = ring_shift(ahead, 1), ring_shift(behind, -1)
        blocks[-step], blocks[step] = ahead, behind
    if far - 2 < len(fillers):
        ahead, behind = filled((ahead, behind), fillers[far - 2])
    left, right = ring_shift(ahead[:, :middle], 1), ring_shift(behind[:, middle:], -1)
    blocks[far] = jnp.concatenate([left, right], axis=1)
    gathered = []
    first = 0
    for part in parts:
        last = first + part.shape[1]
        gathered.append({offset: block[:, first:last] for offset, block in blocks.items()})
        first = last
    return gathered


def with_rows(block, rows):
    if block.shape[0] >= rows:
        return jnp.concatenate(jnp.split(block, block.shape[0] // rows, axis=0), axis=1)
    return jnp.concatenate(jnp.split(block, rows // block.shape[0], axis=1), axis=0)


def stacked_rows(blocks):
    rows, width = blocks[0].shape
    whole = jnp.zeros((len(blocks) * rows, width), blocks[0].dtype)
    for offset, block in blocks.items():
        whole = lax.dynamic_update_slice(whole, block, (ring_place(offset) * rows, 0))
    return whole


def stacked_columns(blocks):
    rows, width = blocks[0].shape
    whole = jnp.zeros((rows, len(blocks) * width), blocks[0].dtype)
    for offset, block in blocks.items():
        whole = lax.dynamic_update_slice(whole, block, (0, ring_place(offset) * width))
    return whole


def ring_rows(whole, offsets):
    rows = whole.shape[0] // lax.axis_size("seq")
    return jnp.concatenate(
        [lax.dynamic_slice_in_dim(whole, ring_place(o) * rows, rows, 0) for o in offsets], axis=0
    )


def added(block, got):
    return (block.astype(jnp.float32) + got.astype(jnp.float32)).astype(block.dtype)


def ring_scatter_sum(blocks, fillers=()):
    far = lax.axis_size("seq") // 2
    middle = blocks[0].shape[1] // 2
    ahead = ring_shift(blocks[far][:, :middle], 1)
    behind = ring_shift(blocks[far][:, middle:], -1)
    for turn, step in enumerate(range(far - 1, 0, -1)):
        onward, backward = blocks[step], blocks[-step]
        if turn == 0:
            onward = jnp.concatenate([added(onward[:, :middle], ahead), onward[:, middle:]], axis=1)
            backward = jnp.concatenate(
                [backward[:, :middle], added(backward[:, middle:], behind)], axis=1
            )
        else:
            onward, backward = added(onward, ahead), added(backward, behind)
        if turn < len(fillers):
            onward, backward = filled([onward, backward], fillers[turn])
        ahead, behind = ring_shift(onward, 1), ring_shift(backward, -1)
    if far - 1 < len(fillers):
        ahead, behind = filled([ahead, behind], fillers[far - 1])
    return blocks[0].astype(jnp.float32) + ahead.astype(jnp.float32) + behind.astype(jnp.float32)


def ring_blocks(wholes):
    far = lax.axis_size("seq") // 2
    offsets = [far] + [sign * step for step in range(far - 1, 0, -1) for sign in (1, -1)] + [0]
    blocks = {far: jnp.concatenate([ring_rows(whole, [far]) for whole in wholes], axis=1)}
    wholes = after_all(wholes, (blocks[far],))
    for offset in offsets[1:]:
        blocks[offset] = jnp.concatenate([ring_rows(whole, [offset]) for whole in wholes], axis=1)
    return blocks


def butterfly_steps():
    steps = []
    for axis in ("batch", "seq"):
        bit = 1
        while bit < lax.axis_size(axis):
            steps.append((axis, bit))
            bit *= 2
    return steps


def after(value, *others):
    return lax.optimization_barrier((value,) + others)[0]


def after_all(values, others):
    return lax.optimization_barrier(tuple(values) + tuple(others))[: len(values)]


def batch_bits():
    count = lax.axis_size("batch")
    bits = []
    while (1 << len(bits)) < count:
        bits.append(1 << len(bits))
    return bits


def of_offset(choices, offset):
    index = lax.axis_index("batch")
    picked = choices[offset]
    for own in range(1, len(choices)):
        picked = jnp.where(index == own, choices[own ^ offset], picked)
    return picked


def offset_order():
    order = [0]
    for bit in reversed(batch_bits()):
        order = order + [offset ^ bit for offset in order]
    return order


def batch_columns(rows, rows_own):
    count, width = rows.shape
    batch_total = lax.axis_size("batch")
    blocks = rows.reshape(count, -1, batch_total, rows_own)
    return [blocks[:, :, b].reshape(count, width // batch_total) for b in range(batch_total)]


def to_relative(rows, rows_own):
    columns = batch_columns(rows, rows_own)
    return jnp.concatenate([of_offset(columns, m) for m in offset_order()], axis=1)


def from_relative(rows, rows_own):
    count, width = rows.shape
    batch_total = lax.axis_size("batch")
    order = offset_order()
    part = width // batch_total
    columns = [
        rows[:, order.index(m) * part : (order.index(m) + 1) * part] for m in range(batch_total)
    ]
    blocks = [
        of_offset(columns, b).reshape(count, width // (batch_total * rows_own), rows_own)
        for b in range(batch_total)
    ]
    return jnp.stack(blocks, axis=2).reshape(count, width)


def gather_pieces(block):
    pieces = [block]
    for bit in reversed(batch_bits()):
        pieces = pieces + [swapped(piece, "batch", bit) for piece in pieces]
    return pieces


def gather_batch(block):
    return jnp.concatenate(gather_pieces(block), axis=0)


def partial_sum_batch(left, right):
    width = left.shape[1]
    held = None
    sends = []

    def product(first, last):
        part = contract_rows(left[:, first:last], right)
        return part if held is None else part + held[first:last]

    for bit in batch_bits():
        half = width // 2
        sends.append(product(half, width).astype(jnp.bfloat16))
        got = swapped(sends[-1], "batch", bit).astype(jnp.float32)
        held = got if held is None else held[:half] + got
        width = half
    return (product(0, width).astype(jnp.bfloat16), sends)


def scatter_sum_batch(blocks):
    held = blocks
    for bit in batch_bits():
        pairs = held.reshape((held.shape[0] // 2, 2) + held.shape[1:])
        got = swapped(pairs[:, 1], "batch", bit)
        held = (pairs[:, 0].astype(jnp.float32) + got.astype(jnp.float32)).astype(jnp.bfloat16)
    return held[0]


def seqs_in_block(columns, seq_total):
    return max(1, min(seq_total, 1024 // columns))


def rounded_by_owner(weight, groups):
    rows_own, width = weight.shape
    seq_total = lax.axis_size("seq")
    columns = width // (groups * seq_total)
    if columns % LANES:
        blocks = weight.astype(jnp.bfloat16).reshape(rows_own, groups, seq_total, columns)
        return jnp.transpose(blocks, (2, 0, 1, 3)).reshape(seq_total, rows_own, groups * columns)
    taken = seqs_in_block(columns, seq_total)
    steps = seq_total // taken

    def kernel(weight_ref, out_ref):
        for place in range(taken):
            out_ref[place] = weight_ref[:, place * columns : (place + 1) * columns].astype(
                jnp.bfloat16
            )

    return pl.pallas_call(
        kernel,
        grid=(groups, steps),
        in_specs=[pl.BlockSpec((rows_own, taken * columns), lambda g, j: (0, g * steps + j))],
        out_specs=pl.BlockSpec((taken, rows_own, columns), lambda g, j: (j, 0, g)),
        out_shape=jax.ShapeDtypeStruct(
            (seq_total, rows_own, groups * columns), jnp.bfloat16
        ),
        cost_estimate=pl.CostEstimate(flops=0, bytes_accessed=weight.size * 6, transcendentals=0),
    )(weight)


def to_column_owners(blocks):
    got = lax.all_to_all(blocks, "seq", 0, 0, tiled=True)
    return got.reshape(-1, blocks.shape[2])


def to_row_owners(grad):
    seq_total = lax.axis_size("seq")
    blocks = grad.reshape(seq_total, grad.shape[0] // seq_total, grad.shape[1])
    return lax.all_to_all(blocks, "seq", 0, 0, tiled=True)


def adam_by_owner(weight, first_moment, second, gradient, groups, step_rate, skipped=0):
    rows_own, width = weight.shape
    seq_total = lax.axis_size("seq")
    columns = width // (groups * seq_total)
    if columns % LANES:
        own = gradient[:, :, skipped * columns : (skipped + groups) * columns]
        natural = jnp.transpose(
            own.reshape(seq_total, rows_own, groups, columns), (1, 2, 0, 3)
        ).reshape(rows_own, width)
        return adam_update(weight, first_moment, second, natural.astype(jnp.float32), step_rate)
    taken = seqs_in_block(columns, seq_total)
    steps = seq_total // taken

    def kernel(weight_ref, first_ref, second_ref, gradient_ref, *out_refs):
        for place in range(taken):
            here = slice(place * columns, (place + 1) * columns)
            results = adam_update(
                weight_ref[:, here],
                first_ref[:, here],
                second_ref[:, here],
                gradient_ref[place].astype(jnp.float32),
                step_rate,
            )
            for out_ref, result in zip(out_refs, results):
                out_ref[:, here] = result

    whole = pl.BlockSpec((rows_own, taken * columns), lambda g, j: (0, g * steps + j))
    return pl.pallas_call(
        kernel,
        grid=(groups, steps),
        in_specs=[whole] * 3 + [
            pl.BlockSpec((taken, rows_own, columns), lambda g, j: (j, 0, g + skipped))
        ],
        out_specs=[whole] * 3,
        out_shape=[jax.ShapeDtypeStruct(weight.shape, jnp.float32)] * 3,
        cost_estimate=pl.CostEstimate(
            flops=weight.size * 15, bytes_accessed=weight.size * 26, transcendentals=weight.size
        ),
    )(weight, first_moment, second, gradient)


def swap_halves(values):
    lane = lax.broadcasted_iota(jnp.int32, values.shape, 1)
    return jnp.where(
        lane % HD < HD // 2,
        pltpu.roll(values, LANES - HD // 2, 1),
        pltpu.roll(values, HD // 2, 1),
    )


def of_head(values, head, axis=1):
    lane = lax.broadcasted_iota(jnp.int32, values.shape, axis)
    return jnp.where(lane // HD == head, values, jnp.zeros_like(values))


def allowed_here(starts_ref, first, rows):
    shape = (rows, QUERY_ROWS)
    key = lax.broadcasted_iota(jnp.int32, shape, 0)
    query = lax.broadcasted_iota(jnp.int32, shape, 1) + first
    return (key <= query) & (key >= starts_ref[:, first : first + QUERY_ROWS])


def mm_last(left, right):
    return lax.dot_general(
        left, right, (((1,), (1,)), ((), ())), preferred_element_type=jnp.float32
    )


def attend_kernel(
    query_in, key_in, value_in, cos_ref, sin_ref, starts_ref,
    out_ref, low_ref, query_ref, key_ref, value_ref, total_ref, key_own, value_turned,
):
    length = query_in.shape[0]
    cos, sin = cos_ref[...], sin_ref[...]
    raw_query, raw_key = query_in[...], key_in[...]
    query_ref[...] = (raw_query * cos + swap_halves(raw_query) * sin).astype(jnp.bfloat16) * HD**-0.5
    key_ref[...] = (raw_key * cos + swap_halves(raw_key) * sin).astype(jnp.bfloat16)
    value_ref[...] = value_in[...].astype(jnp.bfloat16)
    turned = value_in[...].T
    for head in range(2):
        key_own[head] = of_head(key_ref[...], head)
        value_turned[head] = of_head(turned, head, 0).astype(jnp.bfloat16)
    for first in range(0, length, QUERY_ROWS):
        last = first + QUERY_ROWS
        allowed = allowed_here(starts_ref, first, last)
        weighted = jnp.zeros((LANES, QUERY_ROWS), jnp.float32)
        for head in range(2):
            scores = mm_last(key_own[head, :last], query_ref[first:last])
            scores = jnp.where(allowed, scores, masked_score)
            top = jnp.max(scores, axis=0, keepdims=True)
            powers = jnp.exp(scores - top)
            total = jnp.sum(powers, axis=0, keepdims=True)
            probs = (powers * (1.0 / total)).astype(jnp.bfloat16)
            weighted += matmul(value_turned[head, :, :last], probs)
            total_ref[0, head : head + 1, first:last] = top + jnp.log(total)
        attended = weighted.T
        out_ref[first:last] = attended
        low_ref[first:last] = attended.astype(jnp.bfloat16)


def attend_back_kernel(
    query_ref, key_ref, value_ref, grad_ref, attended_ref, total_ref, cos_ref, sin_ref, starts_ref,
    out_ref, key_own, value_own, key_turned, key_grad, value_grad,
):
    length = query_ref.shape[0]
    pair = pl.program_id(0)
    width = out_ref.shape[1] // 3
    turned = key_ref[...].astype(jnp.float32).T
    for head in range(2):
        key_own[head] = of_head(key_ref[...], head)
        value_own[head] = of_head(value_ref[...], head)
        key_turned[head] = of_head(turned, head, 0).astype(jnp.bfloat16)
    key_grad[...] = jnp.zeros_like(key_grad)
    value_grad[...] = jnp.zeros_like(value_grad)

    def undone(values, rows):
        back = values * cos_ref[rows] - swap_halves(values) * sin_ref[rows]
        return back.astype(jnp.bfloat16)

    def lanes(group):
        return pl.ds(pl.multiple_of(group * width + pair * LANES, LANES), LANES)

    for first in range(0, length, QUERY_ROWS):
        last = first + QUERY_ROWS
        rows = slice(first, last)
        allowed = allowed_here(starts_ref, first, last)
        grad, query = grad_ref[rows], query_ref[rows]
        products = (grad.astype(jnp.float32) * attended_ref[rows]).T
        query_grad = jnp.zeros((LANES, QUERY_ROWS), jnp.float32)
        for head in range(2):
            scores = mm_last(key_own[head, :last], query)
            probs = jnp.where(allowed, jnp.exp(scores - total_ref[0, head : head + 1, rows]), 0.0)
            delta = jnp.sum(products[head * HD : (head + 1) * HD], axis=0, keepdims=True)
            grad_probs = mm_last(value_own[head, :last], grad)
            grad_scores = (probs * (grad_probs - delta)).astype(jnp.bfloat16)
            value_grad[:last] += matmul(probs.astype(jnp.bfloat16), of_head(grad, head))
            key_grad[:last] += matmul(grad_scores, of_head(query, head))
            query_grad += matmul(key_turned[head, :, :last], grad_scores)
        out_ref[rows, lanes(0)] = undone(query_grad.T * HD**-0.5, rows)
    everything = slice(0, length)
    out_ref[:, lanes(1)] = undone(key_grad[...], everything)
    out_ref[:, lanes(2)] = value_grad[...].astype(jnp.bfloat16)


def project_kernel(total, attended_ref, inputs_ref, gain_ref, *refs):
    weight_refs, (middle_ref, unit_ref) = refs[:total], refs[total:]
    width = inputs_ref.shape[1]
    part = width // total
    attended = attended_ref[...]
    squares = 0.0
    for place, weight_ref in enumerate(weight_refs):
        columns = slice(place * part, (place + 1) * part)
        block = inputs_ref[:, columns].astype(jnp.float32) + matmul(attended, weight_ref[...])
        middle_ref[:, columns] = block
        squares += jnp.sum(block * block, axis=1, keepdims=True)
    scale = lax.rsqrt(squares / width + norm_eps)
    unit_ref[...] = (middle_ref[...] * scale * gain_ref[...]).astype(jnp.bfloat16)


def project_rows(attended, inputs, gain, pieces):
    length, width = inputs.shape
    total = len(pieces)
    rows = pl.BlockSpec((QUERY_ROWS, width), lambda i: (i, 0))
    return pl.pallas_call(
        lambda *refs: project_kernel(total, *refs),
        grid=(length // QUERY_ROWS,),
        in_specs=[rows, rows, pl.BlockSpec((1, width), lambda i: (0, 0))]
        + [pl.BlockSpec((width, width // total), lambda i: (0, 0))] * total,
        out_specs=[rows, rows],
        out_shape=[
            jax.ShapeDtypeStruct((length, width), jnp.float32),
            jax.ShapeDtypeStruct((length, width), jnp.bfloat16),
        ],
        compiler_params=pltpu.CompilerParams(vmem_limit_bytes=48 << 20),
        cost_estimate=pl.CostEstimate(
            flops=2 * length * width * width,
            bytes_accessed=10 * length * width + 2 * width * width,
            transcendentals=length,
        ),
    )(attended, inputs, gain, *pieces)


def summed_product(left_ref, weight_refs):
    part = left_ref.shape[1] // len(weight_refs)
    return sum(
        matmul(left_ref[:, place * part : (place + 1) * part], weight_ref[...])
        for place, weight_ref in enumerate(weight_refs)
    )


def hidden_kernel(total, rows_ref, *refs):
    gate_ref, up_ref, low_ref = refs[2 * total :]
    gate = summed_product(rows_ref, refs[:total])
    up = summed_product(rows_ref, refs[total : 2 * total])
    gate_ref[...] = gate
    up_ref[...] = up
    low_ref[...] = (gate * jax.nn.sigmoid(gate) * up).astype(jnp.bfloat16)


def hidden_units(rows, gate_pieces):
    length, width = rows.shape
    total = len(gate_pieces)
    hidden = gate_pieces[0].shape[1] // 2
    tile = min(hidden, 2 * LANES)
    steps = hidden // tile
    own = pl.BlockSpec((length, tile), lambda j: (0, j))
    wide = jax.ShapeDtypeStruct((length, hidden), jnp.float32)
    return pl.pallas_call(
        lambda *refs: hidden_kernel(total, *refs),
        grid=(steps,),
        in_specs=[pl.BlockSpec((length, width), lambda j: (0, 0))]
        + [pl.BlockSpec((width // total, tile), lambda j: (0, j))] * total
        + [pl.BlockSpec((width // total, tile), lambda j: (0, steps + j))] * total,
        out_specs=[own] * 3,
        out_shape=[wide, wide, jax.ShapeDtypeStruct((length, hidden), jnp.bfloat16)],
        compiler_params=pltpu.CompilerParams(vmem_limit_bytes=48 << 20),
        cost_estimate=pl.CostEstimate(
            flops=4 * length * width * hidden,
            bytes_accessed=2 * length * width + 4 * width * hidden + 10 * length * hidden,
            transcendentals=length * hidden,
        ),
    )(rows, *gate_pieces, *gate_pieces)


def hidden_back_kernel(total, grads_ref, gate_ref, up_ref, *refs):
    grad_ref = refs[total]
    tile = gate_ref.shape[1]
    hidden = grad_ref.shape[1] // 2
    grad = summed_product(grads_ref, refs[:total])
    gate, up = gate_ref[...], up_ref[...]
    sigmoid = jax.nn.sigmoid(gate)
    first = pl.multiple_of(pl.program_id(0) * tile, tile)
    grad_gate = grad * up * (sigmoid * (1.0 + gate * (1.0 - sigmoid)))
    grad_ref[:, pl.ds(first, tile)] = grad_gate.astype(jnp.bfloat16)
    second = pl.multiple_of(hidden + pl.program_id(0) * tile, tile)
    grad_ref[:, pl.ds(second, tile)] = (grad * (gate * sigmoid)).astype(jnp.bfloat16)


def hidden_back(grads, gate, up, down_pieces):
    length, width = grads.shape
    total = len(down_pieces)
    hidden = gate.shape[1]
    tile = min(hidden, 2 * LANES)
    own = pl.BlockSpec((length, tile), lambda j: (0, j))
    return pl.pallas_call(
        lambda *refs: hidden_back_kernel(total, *refs),
        grid=(hidden // tile,),
        in_specs=[pl.BlockSpec((length, width), lambda j: (0, 0)), own, own]
        + [pl.BlockSpec((width // total, tile), lambda j: (0, j))] * total,
        out_specs=pl.BlockSpec((length, 2 * hidden), lambda j: (0, 0)),
        out_shape=jax.ShapeDtypeStruct((length, 2 * hidden), jnp.bfloat16),
        compiler_params=pltpu.CompilerParams(vmem_limit_bytes=48 << 20),
        cost_estimate=pl.CostEstimate(
            flops=2 * length * width * hidden,
            bytes_accessed=2 * length * width + 2 * width * hidden + 12 * length * hidden,
            transcendentals=length * hidden,
        ),
    )(grads, gate, up, *down_pieces)


def back_kernel(total, left_ref, *refs):
    each = pl.num_programs(0) // total
    for place in range(total):

        @pl.when(pl.program_id(0) // each == place)
        def _():
            refs[total][...] = mm_last(left_ref[...], refs[place][...]).astype(jnp.bfloat16)


def back_to_model(left, pieces):
    length, inner = left.shape
    total = len(pieces)
    part = pieces[0].shape[0]
    tile = min(part, 2 * LANES)
    each = part // tile

    def rows_of(place):
        return pl.BlockSpec((tile, inner), lambda i: (jnp.clip(i - place * each, 0, each - 1), 0))

    return pl.pallas_call(
        lambda *refs: back_kernel(total, *refs),
        grid=(total * each,),
        in_specs=[pl.BlockSpec((length, inner), lambda i: (0, 0))]
        + [rows_of(place) for place in range(total)],
        out_specs=pl.BlockSpec((length, tile), lambda i: (0, i)),
        out_shape=jax.ShapeDtypeStruct((length, part * total), jnp.bfloat16),
        compiler_params=pltpu.CompilerParams(vmem_limit_bytes=48 << 20),
        cost_estimate=pl.CostEstimate(
            flops=2 * length * part * total * inner,
            bytes_accessed=2 * inner * (length + part * total) + 2 * length * part * total,
            transcendentals=0,
        ),
    )(left, *pieces)


def attend_forward(qkv, cos_table, sin_table, starts):
    length, width = qkv.shape[0], qkv.shape[1] // 3
    pairs = width // LANES
    whole = pl.BlockSpec((length, LANES), lambda p: (0, 0))
    own = pl.BlockSpec((length, LANES), lambda p: (0, p))
    low = jax.ShapeDtypeStruct((length, width), jnp.bfloat16)
    work = pairs * length * length
    return pl.pallas_call(
        attend_kernel,
        grid=(pairs,),
        in_specs=[
            own,
            pl.BlockSpec((length, LANES), lambda p: (0, pairs + p)),
            pl.BlockSpec((length, LANES), lambda p: (0, 2 * pairs + p)),
            whole,
            whole,
            pl.BlockSpec((1, length), lambda p: (0, 0)),
        ],
        out_specs=[own] * 5 + [pl.BlockSpec((1, 2, length), lambda p: (p, 0, 0))],
        out_shape=[
            jax.ShapeDtypeStruct((length, width), jnp.float32),
            low,
            low,
            low,
            low,
            jax.ShapeDtypeStruct((pairs, 2, length), jnp.float32),
        ],
        scratch_shapes=[
            pltpu.VMEM((2, length, LANES), jnp.bfloat16),
            pltpu.VMEM((2, LANES, length), jnp.bfloat16),
        ],
        compiler_params=pltpu.CompilerParams(vmem_limit_bytes=48 << 20),
        cost_estimate=pl.CostEstimate(
            flops=8 * work * LANES, bytes_accessed=qkv.size * 8, transcendentals=2 * work
        ),
    )(qkv, qkv, qkv, cos_table, sin_table, starts)


def attend_backward(query, key, value, grad, attended, total, cos_table, sin_table, starts):
    length, width = query.shape
    pairs = width // LANES
    whole = pl.BlockSpec((length, LANES), lambda p: (0, 0))
    own = pl.BlockSpec((length, LANES), lambda p: (0, p))
    work = pairs * length * length
    return pl.pallas_call(
        attend_back_kernel,
        grid=(pairs,),
        in_specs=[own] * 5
        + [
            pl.BlockSpec((1, 2, length), lambda p: (p, 0, 0)),
            whole,
            whole,
            pl.BlockSpec((1, length), lambda p: (0, 0)),
        ],
        out_specs=pl.BlockSpec((length, 3 * width), lambda p: (0, 0)),
        out_shape=jax.ShapeDtypeStruct((length, 3 * width), jnp.bfloat16),
        scratch_shapes=[
            pltpu.VMEM((2, length, LANES), jnp.bfloat16),
            pltpu.VMEM((2, length, LANES), jnp.bfloat16),
            pltpu.VMEM((2, LANES, length), jnp.bfloat16),
            pltpu.VMEM((length, LANES), jnp.float32),
            pltpu.VMEM((length, LANES), jnp.float32),
        ],
        compiler_params=pltpu.CompilerParams(vmem_limit_bytes=48 << 20),
        cost_estimate=pl.CostEstimate(
            flops=work * LANES, bytes_accessed=query.size * 4, transcendentals=work // 16
        ),
    )(query, key, value, grad, attended, total, cos_table, sin_table, starts)


def on_device(
    tokens,
    out_grad,
    doc_lengths,
    qkv_weight,
    qkv_first,
    qkv_second,
    out_weight,
    out_first,
    out_second,
    gate_up_weight,
    gate_up_first,
    gate_up_second,
    down_weight,
    down_first,
    down_second,
    gains,
    gain_first,
    gain_second,
):
    local_rows = tokens.shape[1]
    model_width = tokens.shape[2]
    rows_own = qkv_weight.shape[0]
    seq_total = lax.axis_size("seq")
    batch_total = lax.axis_size("batch")
    head_width = model_width // seq_total
    heads = head_width // HD
    length = local_rows * seq_total
    hidden = down_weight.shape[1] // seq_total
    score_scale = HD ** (-0.5)
    positions = jnp.arange(length, dtype=jnp.int32)
    ends = jnp.cumsum(doc_lengths[0])
    starts = jnp.max(jnp.where(positions[:, None] >= ends[None, :], ends[None, :], 0), axis=1)
    cos_table, sin_table = rope_tables(positions)
    in_pairs = head_width % LANES == 0 and length % QUERY_ROWS == 0
    if in_pairs:
        sign = jnp.where(jnp.arange(HD) < HD // 2, -1.0, 1.0)
        cos_pair = jnp.tile(cos_table, (1, 2))
        sin_pair = jnp.tile(sin_table * sign, (1, 2))

    def split_heads(columns):
        return jnp.transpose(columns.reshape(length, heads, HD), (1, 0, 2))

    def join_heads(values):
        return jnp.transpose(values, (1, 0, 2)).reshape(length, head_width)

    def allowed_pairs():
        return (
            (positions[None, :] <= positions[:, None]) & (positions[None, :] >= starts[:, None])
        )[None]

    def attention(qkv):
        if in_pairs:
            attended, low, *kept = attend_forward(qkv, cos_pair, sin_pair, starts[None])
            return (low, (attended, kept))
        query = split_heads(qkv[:, :head_width])
        query = apply_rope(query, cos_table, sin_table).astype(jnp.bfloat16)
        key = split_heads(qkv[:, head_width : 2 * head_width])
        key = apply_rope(key, cos_table, sin_table).astype(jnp.bfloat16)
        value = split_heads(qkv[:, 2 * head_width :]).astype(jnp.bfloat16)
        scores = jnp.einsum("hqd,hkd->hqk", query, key, preferred_element_type=jnp.float32)
        scores = jnp.where(allowed_pairs(), scores * score_scale, masked_score)
        probs = jax.nn.softmax(scores, axis=-1)
        attended = jnp.einsum(
            "hqk,hkd->hqd", probs.astype(jnp.bfloat16), value, preferred_element_type=jnp.float32
        )
        return (join_heads(attended.astype(jnp.bfloat16)), (attended, (query, key, value, probs)))

    def attention_back(grad, kept):
        if in_pairs:
            attended, (query, key, value, total) = kept
            return attend_backward(
                query, key, value, grad, attended, total, cos_pair, sin_pair, starts[None]
            )
        attended, (query, key, value, probs) = kept
        grad = split_heads(grad)
        delta = jnp.sum(grad.astype(jnp.float32) * attended, axis=-1, keepdims=True)
        grad_probs = jnp.einsum("hqd,hkd->hqk", grad, value, preferred_element_type=jnp.float32)
        grad_scores = (probs * (grad_probs - delta)).astype(jnp.bfloat16)

        def over_queries(left, right):
            return jnp.einsum("hqk,hqd->hkd", left, right, preferred_element_type=jnp.float32)

        grad_value = over_queries(probs.astype(jnp.bfloat16), grad)
        grad_key = over_queries(grad_scores, query) * score_scale
        grad_query = (
            jnp.einsum("hqk,hkd->hqd", grad_scores, key, preferred_element_type=jnp.float32)
            * score_scale
        )
        return jnp.concatenate(
            [
                join_heads(undo_rope(grad_query, cos_table, sin_table)),
                join_heads(undo_rope(grad_key, cos_table, sin_table)),
                join_heads(grad_value),
            ],
            axis=1,
        ).astype(jnp.bfloat16)

    first_row = lax.axis_index("seq") * local_rows
    gains_here = to_relative(gains, rows_own)
    tokens_here = to_relative(tokens[0], rows_own)
    grads_here = to_relative(out_grad[0], rows_own)
    qkv_low = rounded_by_owner(qkv_weight, 3)
    out_columns = batch_columns(after(out_weight, qkv_low).astype(jnp.bfloat16), rows_own)
    out_here = [
        swapped(of_offset(out_columns, m), "batch", m) if m else of_offset(out_columns, m)
        for m in range(batch_total)
    ]
    out_here = [of_offset(out_here, b) for b in range(batch_total)]
    out_here = with_rows(jnp.concatenate(out_here, axis=0), local_rows)
    gate_low = rounded_by_owner(gate_up_weight, 2)
    down_low = rounded_by_owner(down_weight, 1)
    qkv_block = to_column_owners(qkv_low)
    tokens_all, out_all = ring_gather(
        [after(tokens_here, qkv_low), out_here], ((qkv_block,), (gate_low, down_low))
    )
    tokens_all = stacked_rows(tokens_all)
    out_all = stacked_rows(
        {offset: with_rows(block, head_width) for offset, block in out_all.items()}
    )
    qkv_full = gather_batch(qkv_block)
    gate_block = to_column_owners(after(gate_low, tokens_all))
    inputs = tokens_all.astype(jnp.float32)
    act_one = (unit_rows(inputs)[0] * gains_here[0]).astype(jnp.bfloat16)
    qkv = matmul(act_one, qkv_full)
    attn_own, attn_kept = attention(qkv)

    out_pieces = gather_pieces(out_all)
    out_full = jnp.concatenate(out_pieces, axis=1)

    gate_block = after(gate_block, attn_own)
    attn_own_late = after(attn_own, gate_block)
    attn_all = stacked_columns(ring_gather([attn_own_late])[0])
    down_block = to_column_owners(after(down_low, attn_all))
    gate_pieces, down_pieces = gather_pieces(gate_block), gather_pieces(down_block)
    grads_here_late = after(grads_here, down_block)
    if in_pairs and length * model_width <= 1 << 21:
        middle_all, act_two = project_rows(attn_all, tokens_all, gains_here[1:], out_pieces)
        gate_part, up_part, hidden_low = hidden_units(act_two, gate_pieces)
        late = {}

        def block_meanwhile(moved):
            *moved, low = lax.optimization_barrier((*moved, hidden_low))
            late["block"] = back_to_model(low, down_pieces)
            return moved

        grads_all = ring_gather(
            [grads_here_late],
            ((hidden_low,), block_meanwhile, lambda moved: after_all(moved, (late["block"],))),
        )
        grads_all, block_part = stacked_rows(grads_all[0]), late["block"]
        grad_gate_up = hidden_back(grads_all, gate_part, up_part, down_pieces)
        grad_two = back_to_model(grad_gate_up, gate_pieces)
    else:
        grads_all = stacked_rows(ring_gather([grads_here_late])[0])
        middle_all = inputs + matmul(attn_all, out_full)
        act_two = (unit_rows(middle_all)[0] * gains_here[1]).astype(jnp.bfloat16)
        gate_full, down_full = jnp.concatenate(gate_pieces), jnp.concatenate(down_pieces)
        gate_up = matmul(act_two, gate_full)
        gate_part, up_part = gate_up[:, :hidden], gate_up[:, hidden:]
        sigmoid_gate = jax.nn.sigmoid(gate_part)
        silu_gate = gate_part * sigmoid_gate
        hidden_low = (silu_gate * up_part).astype(jnp.bfloat16)
        grad_hidden = matmul(grads_all, down_full)
        grad_gate = (
            grad_hidden * up_part * (sigmoid_gate * (1.0 + gate_part * (1.0 - sigmoid_gate)))
        )
        grad_gate_up = jnp.concatenate([grad_gate, grad_hidden * silu_gate], axis=1)
        grad_gate_up = grad_gate_up.astype(jnp.bfloat16)
        grad_two = contract_cols(grad_gate_up, gate_full).astype(jnp.bfloat16)
        block_part = contract_cols(hidden_low, down_full).astype(jnp.bfloat16)

    sums = {}

    def weight_sums(moved):
        *moved, low, grad = lax.optimization_barrier((*moved, hidden_low, grad_gate_up))
        sums["down"] = partial_sum_batch(grads_all, low)
        sums["gate"] = partial_sum_batch(act_two, grad)
        return moved

    def sent(stage):
        return lambda moved: after_all(moved, (sums["down"][1][stage], sums["gate"][1][stage]))

    summed = ring_scatter_sum(
        ring_blocks([grad_two, block_part]), (weight_sums, sent(0), sent(-1))
    )
    grad_two, block_rest = summed[:, :model_width], summed[:, model_width:]
    down_own, gate_own = sums["down"][0], sums["gate"][0]

    def own_rows(whole):
        return lax.dynamic_slice_in_dim(whole, first_row, local_rows, 0)

    middle = own_rows(middle_all)
    unit_two, scale_two = unit_rows(middle)
    block_out = from_relative((middle + block_rest).astype(jnp.bfloat16), rows_own)
    grad_mid_norm, gain_two_grad = norm_back(grad_two, unit_two, scale_two, gains_here[1])
    grad_middle = grads_here.astype(jnp.float32) + grad_mid_norm
    grad_attn_low = grad_middle.astype(jnp.bfloat16)
    grad_heads = contract_cols(grad_attn_low, out_full).astype(jnp.bfloat16)
    by_owner = jnp.concatenate(
        [
            grad_heads.reshape(local_rows, seq_total, head_width),
            from_relative(grad_attn_low, rows_own).reshape(local_rows, seq_total, head_width),
        ],
        axis=2,
    )
    by_owner = jnp.transpose(by_owner, (1, 0, 2))
    got = lax.all_to_all(by_owner, "seq", 0, 0, tiled=True)
    got = got.reshape(length, 2 * head_width)
    grad_heads = got[:, :head_width]
    grad_attn_own = got[:, head_width:]
    gate_grad = to_row_owners(after(gate_own, got))
    down_grad = to_row_owners(after(down_own, gate_grad))

    grad_qkv = attention_back(grad_heads, attn_kept)
    qkv_own, qkv_sends = partial_sum_batch(act_one, grad_qkv)
    out_part = contract_rows(attn_all, grad_attn_own).astype(jnp.bfloat16)
    out_part = out_part.reshape(seq_total, batch_total, rows_own, head_width)
    out_part = [
        out_part[:, b].reshape(seq_total * rows_own, head_width) for b in range(batch_total)
    ]
    out_own = scatter_sum_batch(jnp.stack([of_offset(out_part, m) for m in range(batch_total)]))
    grad_qkv = after(grad_qkv, qkv_sends[0], out_own, gate_grad)
    grad_one_part = contract_cols(grad_qkv, qkv_full)
    gain_one_part = jnp.sum(grad_one_part * act_one.astype(jnp.float32), axis=0)
    gain_grad = jnp.stack([gain_one_part / gains_here[0], gain_two_grad])
    gain_grad = from_relative(gain_grad, rows_own)
    down_m, down_s, down_w = adam_by_owner(
        down_weight, down_first, down_second, after(down_grad, qkv_sends[-1]), 1, rate_down
    )
    steps = butterfly_steps()

    def next_gain_sum():
        if steps:
            axis, bit = steps.pop(0)
            sums["gain"] = sums["gain"] + swapped(sums["gain"], axis, bit)

    def tied(moved, *names):
        moved = lax.optimization_barrier((*moved, *(sums[name] for name in names)))
        for name, value in zip(names, moved[len(moved) - len(names) :]):
            sums[name] = value
        next_gain_sum()
        return moved[: len(moved) - len(names)]

    def gate_update(moved):
        moved = tied(moved, "gain", "gate_grad")
        sums["gate_new"] = adam_by_owner(
            gate_up_weight, gate_up_first, gate_up_second, sums["gate_grad"], 2, rate_gate
        )
        return moved

    def last_transfer(moved):
        moved = tied(after_all(moved, (sums["gate_new"][0],)), "gain")
        return moved

    def last_updates(moved):
        sums["qkv"] = adam_by_owner(
            qkv_weight, qkv_first, qkv_second, sums["rest"], 3, rate_qkv
        )
        sums["out"] = adam_by_owner(
            out_weight, out_first, out_second, sums["rest"], 1, rate_out, skipped=3
        )
        return tied(after_all(moved, (sums["qkv"][0], sums["out"][0], down_m)), "gain")

    sums["gain"], sums["gate_grad"] = gain_grad, gate_grad
    next_gain_sum()
    sums["rest"] = to_row_owners(jnp.concatenate([after(qkv_own, down_grad), out_own], axis=1))
    grad_one = ring_scatter_sum(
        ring_blocks([after(grad_one_part.astype(jnp.bfloat16), qkv_sends[-1])]),
        (gate_update, last_transfer, lambda moved: tied(moved, "gain"), last_updates),
    )
    while steps:
        next_gain_sum()
    gain_grad = sums["gain"]
    (qkv_m, qkv_s, qkv_w), (out_m, out_s, out_w) = sums["qkv"], sums["out"]
    gate_m, gate_s, gate_w = sums["gate_new"]
    unit_one, scale_one = unit_rows(tokens_here.astype(jnp.float32))
    grad_in_norm = norm_back(grad_one, unit_one, scale_one, gains_here[0])[0]
    input_grad = from_relative(grad_middle + grad_in_norm, rows_own)
    gain_m, gain_s, gain_w = adam_update(gains, gain_first, gain_second, gain_grad, rate_gain)
    return (
        block_out[None],
        input_grad[None],
        qkv_m,
        qkv_s,
        qkv_w,
        out_m,
        out_s,
        out_w,
        gate_m,
        gate_s,
        gate_w,
        down_m,
        down_s,
        down_w,
        gain_m,
        gain_s,
        gain_w,
    )


def solution(mesh):
    rows = P(("seq", "batch"), None)
    blocks = P("batch", "seq", None)
    return jax.shard_map(
        on_device,
        mesh=mesh,
        in_specs=(blocks, blocks, P("batch", None)) + (rows,) * 12 + (P(),) * 3,
        out_specs=(blocks, blocks) + (rows,) * 12 + (P(),) * 3,
        check_vma=False,
    )
```
